32 devices in a mesh: groups: 2 (over x), section: 2 (over core), tensor: 8 (over z, y).
Axes of the slice: x: 2, y: 2, z: 4, core: 2. Of those that a mesh axis runs over, the one named last changes fastest.
Arguments:
- hidden: bfloat16 [16, 8192], P(('groups', 'section'), 'tensor'), parts along dimension 0, may hold values from -6 to 6
- w_query: bfloat16 [8192, 8192], P(None, 'tensor'), may hold values from -0.0625 to 0.0625
- w_output: bfloat16 [8192, 8192], P('tensor'), may hold values from -0.75 to 0.75
- cache: bfloat16 [16, 1024, 2048], P(('groups', 'section'), 'tensor'), parts along dimension 0
- fresh: bfloat16 [16, 512, 2048], P(('groups', 'section'), 'tensor'), parts along dimension 0, may hold values from -6 to 6
- cache_lengths: int32 [16], P(('groups', 'section')), parts along dimension 0, may hold values from 1 to 1024, 4097 in all
- new_lengths: int32 [16], P(('groups', 'section')), parts along dimension 0, may hold values from 1 to 512, 2049 in all
Outputs:
- attended: bfloat16 [16, 8192], P(('groups', 'section'), 'tensor'), parts along dimension 0
The draws below stay inside these ranges and needn't reach their ends.
There are 2 independent parts, one for each index of `groups`. The reference program is written for one: setup_inputs(seed, part) draws one part's arguments, and reference() takes and returns one part's arrays. A program takes and returns all parts, laid end to end along the dimension named above; an argument that names none is the same for every part. Nothing has to cross between parts.
All inputs are finite; a program needn't handle non-finite values. No bound on the sum of `cache_lengths` or of `new_lengths` on one device may be relied on, other than what follows from the above.
Results may differ from the reference program's by a relative error of at most 0.035.
Values may be sent and summed in bfloat16 or wider, within the bound.
No kernel may reach another device: no remote copies, remote signals or barrier semaphores. Data moves between devices by JAX's collectives and lax.ppermute only.
A program may use at most 128 MiB of HBM per device.

```python
import math
import jax
import jax.numpy as jnp
import numpy as np
from jax import lax

D = 8192
HEADS = 64
KVH = 8
HD = 128
R = 8
CTX = 1024
NEW = 512


def draw_cache(key, part):
    key = jax.random.fold_in(key, 11)
    first = jax.random.fold_in(key, 0)
    shape = (R, CTX, 2 * KVH * HD)
    base = jax.random.normal(first, shape, jnp.float32)
    return base.astype(jnp.bfloat16)


def block_scale(own_key, extent, cuts, low, high):
    gain = 1.0
    for dim, blocks in cuts:
        draws = jax.random.uniform(jax.random.fold_in(jax.random.fold_in(own_key, 6), dim), (blocks,), jnp.float32, low / len(cuts), high / len(cuts))
        gain = gain * jnp.repeat(jnp.exp(draws), extent[dim] // blocks).reshape((-1,) + (1,) * (len(extent) - 1 - dim))
    return gain


def profile(number_of, total, most, slope):
    loads = [(1 << 20) // math.isqrt(grade ** slope) + 1 for grade in range(2, number_of + 1)]
    spare, given = total - most - (number_of - 1), [1] * (number_of - 1)
    while spare > 0:
        movable = [i for i in range(number_of - 1) if given[i] < most]
        mass, remaining = sum([loads[i] for i in movable]), spare
        for i in movable:
            extra = min(most - given[i], max(1, remaining * loads[i] // mass), spare)
            given[i] = given[i] + extra
            spare = spare - extra
    return np.array([most] + given)


def ragged(rng, amount, total, most, slope):
    if amount == 2:
        one = jax.random.randint(rng, (), max(1, total - most), min(most, total - 1) + 1)
        return jnp.stack([one, total - one])
    tallies = jnp.asarray(profile(amount, total, most, slope), jnp.int32)
    twos = (amount - 1) // 2
    donor, sink = tallies[1:1 + 2 * twos:2], tallies[2:2 + 2 * twos:2]
    margin = jnp.minimum(donor - 1, most - sink)
    shifted = jax.random.randint(jax.random.fold_in(rng, 1), (twos,), 0, 1 << 20) % (margin + 1)
    tallies = tallies.at[1:1 + 2 * twos:2].set(donor - shifted).at[2:2 + 2 * twos:2].set(sink + shifted)
    return tallies[jax.random.permutation(jax.random.fold_in(rng, 2), amount)]


def noise(own_key, dims, spread, reach, shards=(), kind=jnp.bfloat16):
    entries = spread * jax.random.normal(own_key, dims, jnp.float32)
    if shards:
        entries = entries * block_scale(own_key, dims, shards, -0.22, 0.18)
    return jnp.clip(entries, -reach, reach).astype(kind)


def setup_inputs(seed: int = 0, part: int = 0) -> dict:
    key_of = jax.random.split(jax.random.key(seed), 8)
    part_keys = jax.random.split(jax.random.fold_in(key_of[7], part), 8)
    hidden = noise(part_keys[0], (R, D), 1.0, 6.0, ((0, 2), (1, 8)))
    w_query = noise(key_of[1], (D, HEADS * HD), D ** -0.5, 0.0625, ((1, 8),))
    w_output = noise(key_of[2], (HEADS * HD, D), (HD // 2) ** -0.5, 0.75, ((0, 8),))
    cache = draw_cache(jax.random.fold_in(jax.random.fold_in(key_of[7], part), 71), part)
    fresh = noise(part_keys[4], (R, NEW, 2 * KVH * HD), 1.0, 6.0, ((0, 2), (1, 8)))
    cache_lengths = ragged(part_keys[5], R, R * CTX // 2 + 1, CTX, 2).astype(jnp.int32)
    new_lengths = ragged(part_keys[6], R, R * NEW // 2 + 1, NEW, 2).astype(jnp.int32)
    return {"hidden": hidden, "w_query": w_query, "w_output": w_output, "cache": cache, "fresh": fresh, "cache_lengths": cache_lengths, "new_lengths": new_lengths}


def attend_one(packed):
    query, cache_row, fresh_row, cache_len, new_len = packed
    group = HEADS // KVH
    width = KVH * HD
    keys = jnp.concatenate([cache_row[:, :width], fresh_row[:, :width]], axis=0).astype(jnp.float32)
    values = jnp.concatenate([cache_row[:, width:], fresh_row[:, width:]], axis=0).astype(jnp.float32)
    total_keys = keys.shape[0]
    keys = keys.reshape(total_keys, KVH, HD)
    values = values.reshape(total_keys, KVH, HD)
    heads = query.astype(jnp.float32).reshape(KVH, group, HD)
    scores = jnp.einsum("kgd,tkd->kgt", heads, keys) * (HD ** -0.5)
    position = jnp.arange(total_keys, dtype=jnp.int32)
    counting = jnp.where(position < CTX, position < cache_len, (position - CTX) < new_len)
    masked = jnp.where(counting[None, None, :], scores, -1e30)
    top = jnp.max(masked, axis=2, keepdims=True)
    weights = jnp.where(counting[None, None, :], jnp.exp(masked - top), 0.0)
    total = jnp.sum(weights, axis=2)
    rounded = weights.astype(jnp.bfloat16).astype(jnp.float32)
    numerator = jnp.einsum("kgt,tkd->kgd", rounded, values)
    context = numerator / total[:, :, None]
    return context.reshape(HEADS * HD).astype(jnp.bfloat16)


def reference(hidden, w_query, w_output, cache, fresh, cache_lengths, new_lengths):
    queries = jnp.dot(hidden, w_query, preferred_element_type=jnp.float32).astype(jnp.bfloat16)
    context = lax.map(attend_one, (queries, cache, fresh, cache_lengths, new_lengths))
    return jnp.dot(context, w_output, preferred_element_type=jnp.float32).astype(jnp.bfloat16)
```

```python
import jax
import jax.numpy as jnp
from jax import lax
from jax.sharding import PartitionSpec as P

KVH = 8
HD = 128


def exchange(x, axis):
    return lax.all_to_all(x, axis, 0, 0, tiled=True)


def pieces(x, count):
    out = []
    for _ in range(count):
        part = x.astype(jnp.bfloat16)
        out.append(part)
        x = x - part.astype(jnp.float32)
    return out


def body(hidden, w_query, w_output, cache, fresh, cache_lengths, new_lengths):
    rows, feat = hidden.shape
    n = lax.axis_size("tensor")
    width = KVH * HD
    index = lax.axis_index("tensor")
    whole = exchange(jnp.broadcast_to(hidden[None], (n, rows, feat)), "tensor")
    whole = whole.transpose(1, 0, 2).reshape(rows, n * feat)
    own = jnp.dot(whole, w_query, preferred_element_type=jnp.float32).astype(jnp.bfloat16)
    cols = own.shape[1]
    q = exchange(jnp.broadcast_to(own[None], (n, rows, cols)), "tensor")
    q = q.transpose(1, 0, 2).reshape(rows, KVH, n * cols // width, HD)
    heads = KVH * q.shape[2]
    both = jnp.concatenate([cache, fresh], axis=1)
    cc, fc = cache.shape[1], fresh.shape[1]
    pos = jnp.concatenate([index * cc + jnp.arange(cc), index * fc + jnp.arange(fc)])
    limit = jnp.where(
        jnp.arange(cc + fc)[None, :] < cc, cache_lengths[:, None], new_lengths[:, None]
    )
    valid = (pos[None, :] < limit)[:, None, None, :]
    keys = both[:, :, :width].reshape(rows, cc + fc, KVH, HD)
    vals = both[:, :, width:].reshape(rows, cc + fc, KVH, HD)
    s = jnp.einsum("rkgd,rtkd->rkgt", q, keys, preferred_element_type=jnp.float32)
    s = jnp.where(valid, s * HD**-0.5, -1e30)
    top = jnp.max(s, axis=3, keepdims=True)
    w = jnp.where(valid, jnp.exp(s - top), 0.0)
    total = jnp.sum(w, axis=3, keepdims=True)
    num = jnp.einsum(
        "rkgt,rtkd->rkgd", w.astype(jnp.bfloat16), vals, preferred_element_type=jnp.float32
    )
    num = num.astype(jnp.bfloat16).reshape(rows, heads, HD)
    stats = jnp.concatenate(pieces(top, 3) + pieces(total, 2), axis=3).reshape(rows, heads, 5)
    stats = jnp.pad(stats, ((0, 0), (0, 0), (0, HD - 5)))
    pay = jnp.concatenate([num, stats], axis=2).reshape(rows, n, heads // n, 2 * HD)
    got = exchange(pay.transpose(1, 0, 2, 3), "tensor").astype(jnp.float32)
    tops = got[..., HD] + got[..., HD + 1] + got[..., HD + 2]
    sums = got[..., HD + 3] + got[..., HD + 4]
    scale = jnp.exp(tops - jnp.max(tops, axis=0))
    num = jnp.sum(got[..., :HD] * scale[..., None], axis=0)
    den = jnp.sum(sums * scale, axis=0)
    context = (num / den[..., None]).astype(jnp.bfloat16).reshape(rows, heads // n * HD)
    terms = jnp.dot(context, w_output, preferred_element_type=jnp.float32)
    terms = terms.astype(jnp.bfloat16).reshape(rows, n, -1).transpose(1, 0, 2)
    return jnp.sum(exchange(terms, "tensor").astype(jnp.float32), axis=0).astype(jnp.bfloat16)


def solution(mesh):
    return jax.shard_map(
        body,
        mesh=mesh,
        in_specs=(
            P(("groups", "section"), "tensor"),
            P(None, "tensor"),
            P("tensor", None),
            P(("groups", "section"), "tensor", None),
            P(("groups", "section"), "tensor", None),
            P(("groups", "section")),
            P(("groups", "section")),
        ),
        out_specs=P(("groups", "section"), "tensor"),
        check_vma=False,
    )
```

```python
import functools

import jax
import jax.numpy as jnp
from jax import lax
from jax.experimental import pallas as pl
from jax.experimental.pallas import tpu as pltpu
from jax.sharding import PartitionSpec as P

KVH = 8
HD = 128
GROUP = 8
F32 = jnp.float32
BF16 = jnp.bfloat16
VMEM = pl.BlockSpec(memory_space=pltpu.VMEM)
SMEM = pl.BlockSpec(memory_space=pltpu.SMEM)


def exchange(x):
    return lax.all_to_all(x, "tensor", 0, 0, tiled=True)


def dot(a, b):
    return jnp.dot(a, b, preferred_element_type=F32)


def call(kernel, shape, dtype, *args, specs=None, scratch=(), limit=8, cost=pl.CostEstimate(flops=10**12, bytes_accessed=64 << 20, transcendentals=10**9)):
    return pl.pallas_call(
        kernel,
        in_specs=specs or [VMEM] * len(args),
        out_specs=VMEM,
        out_shape=jax.ShapeDtypeStruct(shape, dtype),
        scratch_shapes=scratch,
        cost_estimate=cost,
        compiler_params=pltpu.CompilerParams(vmem_limit_bytes=limit << 20),
    )(*args)


def spread_kernel(x_ref, o_ref):
    o_ref[...] = jnp.broadcast_to(x_ref[...][None], o_ref.shape)


def query_kernel(all_ref, w_ref, o_ref, heads_ref):
    n, rows, feat = all_ref.shape
    own = w_ref.shape[1] // HD
    acc = jnp.zeros((rows, own * HD), F32)
    for t in range(n):
        acc += dot(all_ref[t], w_ref[t * feat : (t + 1) * feat, :])
    for h in range(own):
        heads_ref[pl.ds(h, rows, stride=own), :] = acc[:, h * HD : (h + 1) * HD]
    o_ref[...] = jnp.broadcast_to(heads_ref[...].astype(BF16)[None], o_ref.shape)


def attend_kernel(place_ref, clen_ref, nlen_ref, q_ref, cache_ref, fresh_ref, o_ref):
    rows, cc, width = cache_ref.shape
    width = width // 2
    fc = fresh_ref.shape[1]
    place = place_ref[0]
    lane = lax.broadcasted_iota(jnp.int32, (2 * GROUP, HD), 1)
    zero = jnp.zeros((GROUP, HD), F32)

    def logits(q, ref, r, cols, start, length):
        keys = ref[r, :, cols]
        s = lax.dot_general(q, keys, (((1,), (1,)), ((), ())), preferred_element_type=F32)
        pos = start + lax.broadcasted_iota(jnp.int32, s.shape, 1)
        valid = pos < length
        return jnp.where(valid, s * HD**-0.5, -1e30), valid

    def attend(r, pair, q):
        cols = slice(2 * pair * HD, 2 * (pair + 1) * HD)
        vals = slice(width + 2 * pair * HD, width + 2 * (pair + 1) * HD)
        sc, okc = logits(q, cache_ref, r, cols, place * cc, clen_ref[r])
        sf, okf = logits(q, fresh_ref, r, cols, place * fc, nlen_ref[r])
        top = jnp.maximum(
            jnp.max(sc, axis=1, keepdims=True), jnp.max(sf, axis=1, keepdims=True)
        )
        wc = jnp.where(okc, jnp.exp(sc - top), 0.0)
        wf = jnp.where(okf, jnp.exp(sf - top), 0.0)
        total = jnp.sum(wc, axis=1, keepdims=True) + jnp.sum(wf, axis=1, keepdims=True)
        num = dot(wc.astype(BF16), cache_ref[r, :, vals])
        num += dot(wf.astype(BF16), fresh_ref[r, :, vals])
        stats = jnp.zeros((2 * GROUP, HD), F32)
        rest = top
        for i in range(3):
            piece = rest.astype(BF16).astype(F32)
            stats = jnp.where(lane == i, piece, stats)
            rest = rest - piece
        rest = total
        for i in range(3, 6):
            piece = rest.astype(BF16).astype(F32)
            stats = jnp.where(lane == i, piece, stats)
            rest = rest - piece
        return num, stats

    for pair in range(KVH // 2):
        for two in range(rows // 2):
            at = slice(two * 2 * GROUP, (two + 1) * 2 * GROUP)
            qa = q_ref[2 * pair, at, :].astype(F32)
            qb = q_ref[2 * pair + 1, at, :].astype(F32)
            out = []
            for i in range(2):
                half = slice(i * GROUP, (i + 1) * GROUP)
                q = jnp.concatenate(
                    [
                        jnp.concatenate([qa[half], zero], axis=1),
                        jnp.concatenate([zero, qb[half]], axis=1),
                    ],
                    axis=0,
                ).astype(BF16)
                out.append(attend(2 * two + i, pair, q))
            for j in range(2):
                half = slice(j * GROUP, (j + 1) * GROUP)
                cols = slice(j * HD, (j + 1) * HD)
                num = jnp.concatenate([o[0][half, cols] for o in out], axis=0)
                stats = jnp.concatenate([o[1][half] for o in out], axis=0)
                o_ref[2 * pair + j, at, 0:HD] = num.astype(BF16)
                o_ref[2 * pair + j, at, HD : 2 * HD] = stats.astype(BF16)


def project_kernel(own, got_ref, w_ref, o_ref, heads_ref):
    n, both, _ = got_ref.shape
    rows = both // own
    line = lax.broadcasted_iota(jnp.int32, (HD, 2 * HD), 0)
    column = lax.broadcasted_iota(jnp.int32, (HD, 2 * HD), 1)
    first = jnp.where(column < HD, 0, 3)
    pick = ((line >= first) & (line < first + 3)).astype(F32).astype(BF16)
    stats = [dot(got_ref[t, :, HD : 2 * HD], pick) for t in range(n)]
    top = functools.reduce(jnp.maximum, [s[:, :HD] for s in stats])
    num = jnp.zeros((both, HD), F32)
    den = jnp.zeros((both, HD), F32)
    for t in range(n):
        scale = jnp.exp(stats[t][:, :HD] - top)
        num += got_ref[t, :, 0:HD].astype(F32) * scale
        den += stats[t][:, HD:] * scale
    heads_ref[...] = num / den
    context = jnp.concatenate(
        [heads_ref[pl.ds(h, rows, stride=own), :] for h in range(own)], axis=1
    ).astype(BF16)
    wide = o_ref.shape[2]
    for t in range(n):
        o_ref[t] = dot(context, w_ref[:, t * wide : (t + 1) * wide]).astype(BF16)


def sum_kernel(x_ref, o_ref):
    o_ref[...] = jnp.sum(x_ref[...].astype(F32), axis=0).astype(BF16)


def body(hidden, w_query, w_output, cache, fresh, cache_lengths, new_lengths):
    rows, feat = hidden.shape
    n = lax.axis_size("tensor")
    own = w_query.shape[1] // HD
    place = lax.axis_index("tensor").astype(jnp.int32).reshape(1)
    wide = w_output.shape[1] // n
    w_query = pltpu.with_memory_space_constraint(w_query, pltpu.VMEM)
    w_output = pltpu.with_memory_space_constraint(w_output, pltpu.VMEM)
    cache = pltpu.with_memory_space_constraint(cache, pltpu.VMEM)
    fresh = pltpu.with_memory_space_constraint(fresh, pltpu.VMEM)

    long = pl.CostEstimate(flops=0, bytes_accessed=64 << 20, transcendentals=0)
    x = call(spread_kernel, (n, rows, feat), BF16, hidden)
    x = exchange(x)
    q = call(
        query_kernel,
        (n, rows * own, HD),
        BF16,
        x,
        w_query,
        scratch=[pltpu.VMEM((rows * own, HD), F32)],
    )
    q = exchange(q)
    if own != GROUP:
        q = q.reshape(KVH, GROUP, rows, HD).transpose(0, 2, 1, 3).reshape(KVH, rows * GROUP, HD)
    part = call(
        attend_kernel,
        (KVH, rows * GROUP, 2 * HD),
        BF16,
        place,
        cache_lengths,
        new_lengths,
        q,
        cache,
        fresh,
        specs=[SMEM] * 3 + [VMEM] * 3,
    )
    if own != GROUP:
        part = part.reshape(KVH, rows, GROUP, 2 * HD).transpose(0, 2, 1, 3)
        part = part.reshape(n, rows * own, 2 * HD)
    part = exchange(part)
    terms = call(
        functools.partial(project_kernel, own),
        (n, rows, wide),
        BF16,
        part,
        w_output,
        scratch=[pltpu.VMEM((rows * own, HD), F32)],
    )
    terms = exchange(terms)
    return call(sum_kernel, (rows, wide), BF16, terms)


def solution(mesh):
    return jax.shard_map(
        body,
        mesh=mesh,
        in_specs=(
            P(("groups", "section"), "tensor"),
            P(None, "tensor"),
            P("tensor", None),
            P(("groups", "section"), "tensor", None),
            P(("groups", "section"), "tensor", None),
            P(("groups", "section")),
            P(("groups", "section")),
        ),
        out_specs=P(("groups", "section"), "tensor"),
        check_vma=False,
    )
```

```python
import functools

import jax
import jax.numpy as jnp
from jax import lax
from jax.experimental import pallas as pl
from jax.experimental.pallas import tpu as pltpu
from jax.sharding import PartitionSpec as P

KVH = 8
HD = 128
GROUP = 8
F32 = jnp.float32
BF16 = jnp.bfloat16
VMEM = pl.BlockSpec(memory_space=pltpu.VMEM)
SMEM = pl.BlockSpec(memory_space=pltpu.SMEM)


def exchange(x):
    return lax.all_to_all(x, "tensor", 0, 0, tiled=True)


def dot(a, b):
    return jnp.dot(a, b, preferred_element_type=F32)


def call(kernel, shape, dtype, *args, specs=None, scratch=(), limit=8, cost=pl.CostEstimate(flops=10**12, bytes_accessed=64 << 20, transcendentals=10**9)):
    return pl.pallas_call(
        kernel,
        in_specs=specs or [VMEM] * len(args),
        out_specs=VMEM,
        out_shape=jax.ShapeDtypeStruct(shape, dtype),
        scratch_shapes=scratch,
        cost_estimate=cost,
        compiler_params=pltpu.CompilerParams(vmem_limit_bytes=limit << 20),
    )(*args)


def spread_kernel(x_ref, o_ref):
    o_ref[...] = jnp.broadcast_to(x_ref[...][None], o_ref.shape)


def query_kernel(all_ref, w_ref, o_ref, heads_ref):
    n, rows, feat = all_ref.shape
    own = w_ref.shape[1] // HD
    acc = jnp.zeros((rows, own * HD), F32)
    for t in range(n):
        acc += dot(all_ref[t], w_ref[t * feat : (t + 1) * feat, :])
    for h in range(own):
        heads_ref[pl.ds(h, rows, stride=own), :] = acc[:, h * HD : (h + 1) * HD]
    o_ref[...] = jnp.broadcast_to(heads_ref[...].astype(BF16)[None], o_ref.shape)


def attend_kernel(clen_ref, nlen_ref, q_ref, cache_ref, fresh_ref, o_ref):
    rows, cc, width = cache_ref.shape
    width = width // 2
    fc = fresh_ref.shape[1]
    heads = KVH * GROUP
    place = lax.axis_index("tensor")
    head_of = lax.broadcasted_iota(jnp.int32, (heads, width), 0) // GROUP
    diagonal = head_of == lax.broadcasted_iota(jnp.int32, (heads, width), 1) // HD

    def logits(ref, r, wide, start, length):
        s = lax.dot_general(
            ref[r, :, 0:width], wide, (((1,), (1,)), ((), ())), preferred_element_type=F32
        )
        valid = start + lax.broadcasted_iota(jnp.int32, s.shape, 0) < length
        return jnp.where(valid, s * HD**-0.5, -1e30), valid

    def attend(r, q):
        wide = jnp.where(diagonal, jnp.concatenate([q] * KVH, axis=1), 0.0).astype(BF16)
        sc, okc = logits(cache_ref, r, wide, place * cc, clen_ref[r])
        sf, okf = logits(fresh_ref, r, wide, place * fc, nlen_ref[r])
        top = jnp.maximum(
            jnp.max(sc, axis=0, keepdims=True), jnp.max(sf, axis=0, keepdims=True)
        )
        wc = jnp.where(okc, jnp.exp(sc - top), 0.0)
        wf = jnp.where(okf, jnp.exp(sf - top), 0.0)
        total = jnp.sum(wc, axis=0, keepdims=True) + jnp.sum(wf, axis=0, keepdims=True)
        stats = []
        for rest in (top, total):
            for _ in range(3):
                piece = rest.astype(BF16).astype(F32)
                stats.append(piece)
                rest = rest - piece
        stats = jnp.concatenate(stats + [jnp.zeros((HD - 6, heads), F32)], axis=0)
        pc = wc.T.astype(BF16)
        pf = wf.T.astype(BF16)
        nums = []
        for pair in range(KVH // 2):
            at = slice(2 * pair * GROUP, 2 * (pair + 1) * GROUP)
            vals = slice(width + 2 * pair * HD, width + 2 * (pair + 1) * HD)
            num = dot(pc[at], cache_ref[r, :, vals]) + dot(pf[at], fresh_ref[r, :, vals])
            nums += [num[:GROUP, :HD], num[GROUP:, HD:]]
        return nums, stats.T

    for two in range(rows // 2):
        at = slice(two * 2 * GROUP, (two + 1) * 2 * GROUP)
        both = [q_ref[g, at, :].astype(F32) for g in range(KVH)]
        out = []
        for i in range(2):
            half = slice(i * GROUP, (i + 1) * GROUP)
            out.append(attend(2 * two + i, jnp.concatenate([q[half] for q in both], axis=0)))
        for g in range(KVH):
            half = slice(g * GROUP, (g + 1) * GROUP)
            num = jnp.concatenate([o[0][g] for o in out], axis=0)
            stats = jnp.concatenate([o[1][half] for o in out], axis=0)
            o_ref[g, at, 0:HD] = num.astype(BF16)
            o_ref[g, at, HD : 2 * HD] = stats.astype(BF16)


def project_kernel(own, got_ref, w_ref, o_ref, heads_ref):
    n, both, _ = got_ref.shape
    rows = both // own
    line = lax.broadcasted_iota(jnp.int32, (HD, 2 * HD), 0)
    column = lax.broadcasted_iota(jnp.int32, (HD, 2 * HD), 1)
    first = jnp.where(column < HD, 0, 3)
    pick = ((line >= first) & (line < first + 3)).astype(F32).astype(BF16)
    stats = [dot(got_ref[t, :, HD : 2 * HD], pick) for t in range(n)]
    top = functools.reduce(jnp.maximum, [s[:, :HD] for s in stats])
    num = jnp.zeros((both, HD), F32)
    den = jnp.zeros((both, HD), F32)
    for t in range(n):
        scale = jnp.exp(stats[t][:, :HD] - top)
        num += got_ref[t, :, 0:HD].astype(F32) * scale
        den += stats[t][:, HD:] * scale
    heads_ref[...] = num / den
    context = jnp.concatenate(
        [heads_ref[pl.ds(h, rows, stride=own), :] for h in range(own)], axis=1
    ).astype(BF16)
    wide = o_ref.shape[2]
    for t in range(n):
        o_ref[t] = dot(context, w_ref[:, t * wide : (t + 1) * wide]).astype(BF16)


def sum_kernel(x_ref, o_ref):
    o_ref[...] = jnp.sum(x_ref[...].astype(F32), axis=0).astype(BF16)


def body(hidden, w_query, w_output, cache, fresh, cache_lengths, new_lengths):
    rows, feat = hidden.shape
    n = lax.axis_size("tensor")
    own = w_query.shape[1] // HD
    wide = w_output.shape[1] // n
    w_query = pltpu.with_memory_space_constraint(w_query, pltpu.VMEM)
    w_output = pltpu.with_memory_space_constraint(w_output, pltpu.VMEM)
    cache = pltpu.with_memory_space_constraint(cache, pltpu.VMEM)
    fresh = pltpu.with_memory_space_constraint(fresh, pltpu.VMEM)

    long = pl.CostEstimate(flops=0, bytes_accessed=64 << 20, transcendentals=0)
    x = call(spread_kernel, (n, rows, feat), BF16, hidden)
    x = exchange(x)
    q = call(
        query_kernel,
        (n, rows * own, HD),
        BF16,
        x,
        w_query,
        scratch=[pltpu.VMEM((rows * own, HD), F32)],
    )
    q = exchange(q)
    if own != GROUP:
        q = q.reshape(KVH, GROUP, rows, HD).transpose(0, 2, 1, 3).reshape(KVH, rows * GROUP, HD)
    part = call(
        attend_kernel,
        (KVH, rows * GROUP, 2 * HD),
        BF16,
        cache_lengths,
        new_lengths,
        q,
        cache,
        fresh,
        specs=[SMEM] * 2 + [VMEM] * 3,
    )
    if own != GROUP:
        part = part.reshape(KVH, rows, GROUP, 2 * HD).transpose(0, 2, 1, 3)
        part = part.reshape(n, rows * own, 2 * HD)
    part = exchange(part)
    terms = call(
        functools.partial(project_kernel, own),
        (n, rows, wide),
        BF16,
        part,
        w_output,
        scratch=[pltpu.VMEM((rows * own, HD), F32)],
    )
    terms = exchange(terms)
    return call(sum_kernel, (rows, wide), BF16, terms)


def solution(mesh):
    return jax.shard_map(
        body,
        mesh=mesh,
        in_specs=(
            P(("groups", "section"), "tensor"),
            P(None, "tensor"),
            P("tensor", None),
            P(("groups", "section"), "tensor", None),
            P(("groups", "section"), "tensor", None),
            P(("groups", "section")),
            P(("groups", "section")),
        ),
        out_specs=P(("groups", "section"), "tensor"),
        check_vma=False,
    )
```

```python
import functools

import jax
import jax.numpy as jnp
from jax import lax
from jax.experimental import pallas as pl
from jax.experimental.pallas import tpu as pltpu
from jax.sharding import PartitionSpec as P

KVH = 8
HD = 128
GROUP = 8
HEADS = KVH * GROUP
STATS = 8
F32 = jnp.float32
BF16 = jnp.bfloat16
VMEM = pl.BlockSpec(memory_space=pltpu.VMEM)
SMEM = pl.BlockSpec(memory_space=pltpu.SMEM)
BOTH = ("section", "tensor")
SPLIT_OUTPUT = False
ORDER = (4, 6, 2)
LONG = 10**12
FIRST = 0
ATTEND = 10**12


def exchange(x, shared):
    return lax.all_to_all(x, BOTH if shared > 1 else "tensor", 0, 0, tiled=True)


def dot(a, b):
    return jnp.dot(a, b, preferred_element_type=F32)


def swap(x, apart):
    n = lax.axis_size("tensor")
    return lax.ppermute(x, "tensor", [(i, i ^ apart) for i in range(n)])


def call(kernel, shape, dtype, *args, specs=None, scratch=(), flops=0):
    return pl.pallas_call(
        kernel,
        in_specs=specs or [VMEM] * len(args),
        out_specs=VMEM,
        out_shape=jax.ShapeDtypeStruct(shape, dtype),
        scratch_shapes=scratch,
        cost_estimate=pl.CostEstimate(flops=flops, bytes_accessed=0, transcendentals=0),
        compiler_params=pltpu.CompilerParams(vmem_limit_bytes=8 << 20),
    )(*args)


def spread_kernel(x_ref, o_ref):
    o_ref[...] = jnp.broadcast_to(x_ref[...][None], o_ref.shape)


def copy_kernel(x_ref, o_ref):
    o_ref[...] = x_ref[...]


def stack_kernel(x_ref, y_ref, o_ref):
    o_ref[0] = x_ref[...]
    o_ref[1] = y_ref[...]


def write_queries(acc, o_ref, heads_ref):
    rows = acc.shape[0]
    own = acc.shape[1] // HD
    for h in range(own):
        heads_ref[pl.ds(h, rows, stride=own), :] = acc[:, h * HD : (h + 1) * HD]
    o_ref[...] = jnp.broadcast_to(heads_ref[...].astype(BF16)[None], o_ref.shape)


def query_kernel(all_ref, w_ref, o_ref, heads_ref):
    n, rows, feat = all_ref.shape
    acc = jnp.zeros((rows, w_ref.shape[1]), F32)
    for t in range(n):
        acc += dot(all_ref[t], w_ref[t * feat : (t + 1) * feat, :])
    write_queries(acc, o_ref, heads_ref)


def pair_product(apart, x_ref, w_ref):
    feat = x_ref.shape[2]
    me = lax.axis_index("tensor")
    acc = jnp.zeros((x_ref.shape[1], w_ref.shape[1]), F32)
    for i in range(2):
        at = pl.multiple_of((me ^ (apart + i)) * feat, feat)
        acc += dot(x_ref[i], w_ref[pl.ds(at, feat), :])
    return acc


def first_kernel(x_ref, w_ref, acc_ref):
    acc_ref[...] = pair_product(0, x_ref, w_ref)


def next_kernel(apart, x_ref, w_ref, old_ref, acc_ref):
    acc_ref[...] = old_ref[...] + pair_product(apart, x_ref, w_ref)


def last_kernel(apart, x_ref, w_ref, old_ref, o_ref, heads_ref):
    write_queries(old_ref[...] + pair_product(apart, x_ref, w_ref), o_ref, heads_ref)


def attend_kernel(clen_ref, nlen_ref, q_ref, cache_ref, fresh_ref, o_ref):
    rows, cc, width = cache_ref.shape
    width = width // 2
    fc = fresh_ref.shape[1]
    shares = q_ref.shape[0] // KVH
    part = GROUP // shares
    place = lax.axis_index("tensor")
    head_of = lax.broadcasted_iota(jnp.int32, (HEADS, width), 0) // GROUP
    diagonal = head_of == lax.broadcasted_iota(jnp.int32, (HEADS, width), 1) // HD

    def logits(ref, r, wide, start, length):
        s = lax.dot_general(
            ref[r, :, 0:width], wide, (((1,), (1,)), ((), ())), preferred_element_type=F32
        )
        valid = start + lax.broadcasted_iota(jnp.int32, s.shape, 0) < length
        return jnp.where(valid, s * HD**-0.5, -1e30), valid

    def attend(r, q):
        wide = jnp.where(diagonal, jnp.concatenate([q] * KVH, axis=1), 0.0).astype(BF16)
        sc, okc = logits(cache_ref, r, wide, place * cc, clen_ref[r])
        sf, okf = logits(fresh_ref, r, wide, place * fc, nlen_ref[r])
        top = jnp.maximum(
            jnp.max(sc, axis=0, keepdims=True), jnp.max(sf, axis=0, keepdims=True)
        )
        wc = jnp.where(okc, jnp.exp(sc - top), 0.0)
        wf = jnp.where(okf, jnp.exp(sf - top), 0.0)
        total = jnp.sum(wc, axis=0, keepdims=True) + jnp.sum(wf, axis=0, keepdims=True)
        some = total > 0.0
        total = jnp.where(some, total, 1.0)
        inverse = 1.0 / total
        pc = (wc * inverse).T.astype(BF16)
        pf = (wf * inverse).T.astype(BF16)
        nums = []
        for pair in range(KVH // 2):
            at = slice(2 * pair * GROUP, 2 * (pair + 1) * GROUP)
            vals = slice(width + 2 * pair * HD, width + 2 * (pair + 1) * HD)
            num = dot(pc[at], cache_ref[r, :, vals]) + dot(pf[at], fresh_ref[r, :, vals])
            nums += [num[:GROUP, :HD], num[GROUP:, HD:]]
        return nums, jnp.where(some, top + jnp.log(total), -1e30)

    stats = []
    for two in range(rows // 2):
        out = []
        for r in (2 * two, 2 * two + 1):
            at = slice(r * part, (r + 1) * part)
            at16 = slice(2 * two * part, 2 * (two + 1) * part)
            half = slice((r % 2) * part, (r % 2 + 1) * part)
            q = [
                q_ref[s * KVH + g, at16, :].astype(F32)[half]
                for g in range(KVH)
                for s in range(shares)
            ]
            out.append(attend(r, jnp.concatenate(q, axis=0)))
        at = slice(two * 2 * GROUP, (two + 1) * 2 * GROUP)
        for d in range(o_ref.shape[0]):
            g = d % KVH
            o_ref[d, at, :] = jnp.concatenate([o[0][g] for o in out], axis=0).astype(BF16)
        rest = jnp.concatenate([o[1] for o in out], axis=1)
        for _ in range(3):
            piece = rest.astype(BF16).astype(F32)
            stats.append(piece)
            rest = rest - piece
        stats.append(jnp.zeros_like(rest))
    stats = jnp.concatenate(stats, axis=0).astype(BF16)
    for d in range(o_ref.shape[0]):
        o_ref[d, rows * GROUP :, :] = stats


def project_kernel(shared, own, got_ref, w_ref, o_ref, heads_ref):
    total, both, _ = got_ref.shape
    both -= STATS
    n = total // shared
    rows = both // own
    wide = o_ref.shape[2]
    me = lax.axis_index("tensor")
    line = lax.broadcasted_iota(jnp.int32, (both, HD), 0)
    column = lax.broadcasted_iota(jnp.int32, (both, HD), 1)
    mine = column == (line // own % 2) * HEADS + me * own + line % own
    mine = mine.astype(F32).astype(BF16)
    line = lax.broadcasted_iota(jnp.int32, (both, n * STATS), 0)
    column = lax.broadcasted_iota(jnp.int32, (both, n * STATS), 1)
    pair = (column % STATS) // (STATS // 2) == line // own // 2
    context = []
    for s in range(shared):
        stats = [got_ref[s * n + t, both:, :].astype(F32) for t in range(n)]
        stats = jnp.concatenate(stats, axis=0).astype(BF16)
        pieces = lax.dot_general(
            mine, stats, (((1,), (1,)), ((), ())), preferred_element_type=F32
        )
        pieces = jnp.where(pair, pieces, 0.0)
        logs = [
            jnp.sum(jnp.where(column // STATS == t, pieces, 0.0), axis=1, keepdims=True)
            for t in range(n)
        ]
        top = functools.reduce(jnp.maximum, logs)
        scales = [jnp.exp(x - top) for x in logs]
        inverse = 1.0 / functools.reduce(jnp.add, scales)
        heads_ref[...] = functools.reduce(
            jnp.add,
            [
                got_ref[s * n + t, 0:both, :].astype(F32) * (scales[t] * inverse)
                for t in range(n)
            ],
        )
        context.append(
            jnp.concatenate(
                [heads_ref[pl.ds(h, rows, stride=own), :] for h in range(own)], axis=1
            )
        )
    context = jnp.concatenate(context, axis=0).astype(BF16)
    offset = 0
    if shared > 1:
        offset = lax.axis_index("section") * wide
    for t in range(n):
        at = t * shared * wide + offset
        if shared > 1:
            at = pl.multiple_of(at, HD)
        terms = dot(context, w_ref[:, pl.ds(at, wide)])
        for s in range(shared):
            o_ref[s * n + t] = terms[s * rows : (s + 1) * rows].astype(BF16)


def sum_kernel(x_ref, o_ref):
    total, _, wide = x_ref.shape
    shared = o_ref.shape[1] // wide
    n = total // shared
    for s in range(shared):
        x = x_ref[s * n : (s + 1) * n].astype(F32)
        o_ref[:, s * wide : (s + 1) * wide] = jnp.sum(x, axis=0).astype(BF16)


def body(hidden, w_query, w_output, cache, fresh, cache_lengths, new_lengths):
    rows, feat = hidden.shape
    n = lax.axis_size("tensor")
    cores = lax.axis_size("section")
    own = w_query.shape[1] // HD
    wide = w_output.shape[1] // n
    usual = own == GROUP
    o_shared = cores if usual and SPLIT_OUTPUT else 1
    w_query = pltpu.with_memory_space_constraint(w_query, pltpu.VMEM)
    w_output = pltpu.with_memory_space_constraint(w_output, pltpu.VMEM)
    cache = pltpu.with_memory_space_constraint(cache, pltpu.VMEM)
    fresh = pltpu.with_memory_space_constraint(fresh, pltpu.VMEM)

    scratch = [pltpu.VMEM((rows * own, HD), F32)]
    if n == 8:
        mine = call(copy_kernel, (rows, feat), BF16, hidden, flops=LONG)
        near = swap(mine, 1)
        pair = call(stack_kernel, (2, rows, feat), BF16, mine, near)
        acc = call(first_kernel, (rows, own * HD), F32, pair, w_query, flops=FIRST)
        got = [swap(pair, apart) for apart in ORDER]
        for apart, x in zip(ORDER[:2], got):
            step = functools.partial(next_kernel, apart)
            acc = call(step, (rows, own * HD), F32, x, w_query, acc)
        step = functools.partial(last_kernel, ORDER[2])
        q = call(step, (n, rows * own, HD), BF16, got[2], w_query, acc, scratch=scratch)
    else:
        x = call(spread_kernel, (n, rows, feat), BF16, hidden, flops=LONG)
        x = exchange(x, 1)
        q = call(query_kernel, (n, rows * own, HD), BF16, x, w_query, scratch=scratch)
    q = exchange(q, 1)
    if not usual:
        q = q.reshape(KVH, GROUP, rows, HD).transpose(0, 2, 1, 3).reshape(KVH, rows * GROUP, HD)
    part = call(
        attend_kernel,
        (o_shared * KVH, rows * GROUP + STATS, HD),
        BF16,
        cache_lengths,
        new_lengths,
        q,
        cache,
        fresh,
        flops=ATTEND,
        specs=[SMEM] * 2 + [VMEM] * 3,
    )
    if not usual:
        stats = jnp.broadcast_to(part[:1, rows * GROUP :], (n, STATS, HD))
        part = part[:, : rows * GROUP].reshape(KVH, rows, GROUP, HD).transpose(0, 2, 1, 3)
        part = jnp.concatenate([part.reshape(n, rows * own, HD), stats], axis=1)
    part = exchange(part, o_shared)
    terms = call(
        functools.partial(project_kernel, o_shared, own),
        (o_shared * n, rows, wide // o_shared),
        BF16,
        part,
        w_output,
        scratch=[pltpu.VMEM((rows * own, HD), F32)],
    )
    terms = exchange(terms, o_shared)
    return call(sum_kernel, (rows, wide), BF16, terms)


def solution(mesh):
    return jax.shard_map(
        body,
        mesh=mesh,
        in_specs=(
            P(("groups", "section"), "tensor"),
            P(None, "tensor"),
            P("tensor", None),
            P(("groups", "section"), "tensor", None),
            P(("groups", "section"), "tensor", None),
            P(("groups", "section")),
            P(("groups", "section")),
        ),
        out_specs=P(("groups", "section"), "tensor"),
        check_vma=False,
    )
```

```python
import functools

import jax
import jax.numpy as jnp
from jax import lax
from jax.experimental import pallas as pl
from jax.experimental.pallas import tpu as pltpu
from jax.sharding import PartitionSpec as P

KVH = 8
HD = 128
GROUP = 8
HEADS = KVH * GROUP
STATS = 8
F32 = jnp.float32
BF16 = jnp.bfloat16
VMEM = pl.BlockSpec(memory_space=pltpu.VMEM)
SMEM = pl.BlockSpec(memory_space=pltpu.SMEM)
BOTH = ("section", "tensor")
SPLIT_OUTPUT = False
ORDER = (4, 6, 2)
LONG = 10**12
FIRST = 0
ATTEND = 10**12


def exchange(x, shared):
    return lax.all_to_all(x, BOTH if shared > 1 else "tensor", 0, 0, tiled=True)


def dot(a, b):
    return jnp.dot(a, b, preferred_element_type=F32)


def swap(x, apart):
    n = lax.axis_size("tensor")
    return lax.ppermute(x, "tensor", [(i, i ^ apart) for i in range(n)])


def call(kernel, shape, dtype, *args, specs=None, scratch=(), flops=0):
    return pl.pallas_call(
        kernel,
        in_specs=specs or [VMEM] * len(args),
        out_specs=VMEM,
        out_shape=jax.ShapeDtypeStruct(shape, dtype),
        scratch_shapes=scratch,
        cost_estimate=pl.CostEstimate(flops=flops, bytes_accessed=0, transcendentals=0),
        compiler_params=pltpu.CompilerParams(vmem_limit_bytes=8 << 20),
    )(*args)


def spread_kernel(x_ref, o_ref):
    o_ref[...] = jnp.broadcast_to(x_ref[...][None], o_ref.shape)


def copy_kernel(x_ref, o_ref):
    o_ref[...] = x_ref[...]


def stack_kernel(x_ref, y_ref, o_ref):
    o_ref[0] = x_ref[...]
    o_ref[1] = y_ref[...]


def write_queries(acc, o_ref, heads_ref):
    rows = acc.shape[0]
    own = acc.shape[1] // HD
    for h in range(own):
        heads_ref[pl.ds(h, rows, stride=own), :] = acc[:, h * HD : (h + 1) * HD]
    o_ref[...] = jnp.broadcast_to(heads_ref[...].astype(BF16)[None], o_ref.shape)


def query_kernel(all_ref, w_ref, o_ref, heads_ref):
    n, rows, feat = all_ref.shape
    acc = jnp.zeros((rows, w_ref.shape[1]), F32)
    for t in range(n):
        acc += dot(all_ref[t], w_ref[t * feat : (t + 1) * feat, :])
    write_queries(acc, o_ref, heads_ref)


def pair_product(apart, x_ref, w_ref):
    feat = x_ref.shape[2]
    me = lax.axis_index("tensor")
    acc = jnp.zeros((x_ref.shape[1], w_ref.shape[1]), F32)
    for i in range(2):
        at = pl.multiple_of((me ^ (apart + i)) * feat, feat)
        acc += dot(x_ref[i], w_ref[pl.ds(at, feat), :])
    return acc


def first_kernel(x_ref, w_ref, acc_ref):
    acc_ref[...] = pair_product(0, x_ref, w_ref)


def next_kernel(apart, x_ref, w_ref, old_ref, acc_ref):
    acc_ref[...] = old_ref[...] + pair_product(apart, x_ref, w_ref)


def last_kernel(apart, x_ref, w_ref, old_ref, o_ref, heads_ref):
    write_queries(old_ref[...] + pair_product(apart, x_ref, w_ref), o_ref, heads_ref)


def attend_kernel(clen_ref, nlen_ref, q_ref, cache_ref, fresh_ref, o_ref):
    rows, cc, width = cache_ref.shape
    width = width // 2
    fc = fresh_ref.shape[1]
    shares = q_ref.shape[0] // KVH
    part = GROUP // shares
    place = lax.axis_index("tensor")
    head_of = lax.broadcasted_iota(jnp.int32, (HEADS, width), 0) // GROUP
    diagonal = head_of == lax.broadcasted_iota(jnp.int32, (HEADS, width), 1) // HD
    none = jnp.zeros((HEADS, width), BF16)

    def logits(ref, r, wide, start, length_ref):
        s = [
            lax.dot_general(
                ref[r + i, :, 0:width],
                wide[i],
                (((1,), (1,)), ((), ())),
                preferred_element_type=F32,
            )
            for i in range(2)
        ]
        s = s[0] + s[1]
        second = lax.broadcasted_iota(jnp.int32, s.shape, 1) >= HEADS
        length = jnp.where(second, length_ref[r + 1], length_ref[r])
        valid = start + lax.broadcasted_iota(jnp.int32, s.shape, 0) < length
        return jnp.where(valid, s * HD**-0.5, -1e30), valid

    scores = []
    for r in range(0, rows, 2):
        at = slice(r * part, (r + 2) * part)
        both = [
            q_ref[s * KVH + g, at, :].astype(F32) for g in range(KVH) for s in range(shares)
        ]
        wide = []
        for i in range(2):
            q = jnp.concatenate([x[i * part : (i + 1) * part] for x in both], axis=0)
            q = jnp.where(diagonal, jnp.concatenate([q] * KVH, axis=1), 0.0).astype(BF16)
            wide.append(jnp.concatenate([q, none] if i == 0 else [none, q], axis=0))
        scores.append(
            (
                logits(cache_ref, r, wide, place * cc, clen_ref),
                logits(fresh_ref, r, wide, place * fc, nlen_ref),
            )
        )
    stats, weights = [], []
    for (sc, okc), (sf, okf) in scores:
        top = jnp.maximum(
            jnp.max(sc, axis=0, keepdims=True), jnp.max(sf, axis=0, keepdims=True)
        )
        wc = jnp.where(okc, jnp.exp(sc - top), 0.0)
        wf = jnp.where(okf, jnp.exp(sf - top), 0.0)
        total = jnp.sum(wc, axis=0, keepdims=True) + jnp.sum(wf, axis=0, keepdims=True)
        some = total > 0.0
        total = jnp.where(some, total, 1.0)
        inverse = 1.0 / total
        weights.append(((wc * inverse).T.astype(BF16), (wf * inverse).T.astype(BF16)))
        rest = jnp.where(some, top + jnp.log(total), -1e30)
        for _ in range(3):
            piece = rest.astype(BF16).astype(F32)
            stats.append(piece)
            rest = rest - piece
        stats.append(jnp.zeros_like(rest))
    for two, (pc, pf) in enumerate(weights):
        for pair in range(KVH // 2):
            vals = slice(width + 2 * pair * HD, width + 2 * (pair + 1) * HD)
            nums = []
            for i in range(2):
                at = slice(i * HEADS + 2 * pair * GROUP, i * HEADS + 2 * (pair + 1) * GROUP)
                nums.append(
                    dot(pc[at], cache_ref[2 * two + i, :, vals])
                    + dot(pf[at], fresh_ref[2 * two + i, :, vals])
                )
            at = slice(two * 2 * GROUP, (two + 1) * 2 * GROUP)
            for j in range(2):
                num = [x[j * GROUP : (j + 1) * GROUP, j * HD : (j + 1) * HD] for x in nums]
                num = jnp.concatenate(num, axis=0).astype(BF16)
                for d in range(2 * pair + j, o_ref.shape[0], KVH):
                    o_ref[d, at, :] = num
    stats = jnp.concatenate(stats, axis=0).astype(BF16)
    for d in range(o_ref.shape[0]):
        o_ref[d, rows * GROUP :, :] = stats


def project_kernel(shared, own, got_ref, w_ref, o_ref, heads_ref):
    total, both, _ = got_ref.shape
    both -= STATS
    n = total // shared
    rows = both // own
    wide = o_ref.shape[2]
    me = lax.axis_index("tensor")
    line = lax.broadcasted_iota(jnp.int32, (both, HD), 0)
    column = lax.broadcasted_iota(jnp.int32, (both, HD), 1)
    mine = column == (line // own % 2) * HEADS + me * own + line % own
    mine = mine.astype(F32).astype(BF16)
    line = lax.broadcasted_iota(jnp.int32, (both, n * STATS), 0)
    column = lax.broadcasted_iota(jnp.int32, (both, n * STATS), 1)
    pair = (column % STATS) // (STATS // 2) == line // own // 2
    context = []
    for s in range(shared):
        stats = [got_ref[s * n + t, both:, :].astype(F32) for t in range(n)]
        stats = jnp.concatenate(stats, axis=0).astype(BF16)
        pieces = lax.dot_general(
            mine, stats, (((1,), (1,)), ((), ())), preferred_element_type=F32
        )
        pieces = jnp.where(pair, pieces, 0.0)
        logs = [
            jnp.sum(jnp.where(column // STATS == t, pieces, 0.0), axis=1, keepdims=True)
            for t in range(n)
        ]
        top = functools.reduce(jnp.maximum, logs)
        scales = [jnp.exp(x - top) for x in logs]
        inverse = 1.0 / functools.reduce(jnp.add, scales)
        heads_ref[...] = functools.reduce(
            jnp.add,
            [
                got_ref[s * n + t, 0:both, :].astype(F32) * (scales[t] * inverse)
                for t in range(n)
            ],
        )
        context.append(
            jnp.concatenate(
                [heads_ref[pl.ds(h, rows, stride=own), :] for h in range(own)], axis=1
            )
        )
    context = jnp.concatenate(context, axis=0).astype(BF16)
    offset = 0
    if shared > 1:
        offset = lax.axis_index("section") * wide
    for t in range(n):
        at = t * shared * wide + offset
        if shared > 1:
            at = pl.multiple_of(at, HD)
        terms = dot(context, w_ref[:, pl.ds(at, wide)])
        for s in range(shared):
            o_ref[s * n + t] = terms[s * rows : (s + 1) * rows].astype(BF16)


def sum_kernel(x_ref, o_ref):
    total, _, wide = x_ref.shape
    shared = o_ref.shape[1] // wide
    n = total // shared
    for s in range(shared):
        x = x_ref[s * n : (s + 1) * n].astype(F32)
        o_ref[:, s * wide : (s + 1) * wide] = jnp.sum(x, axis=0).astype(BF16)


def body(hidden, w_query, w_output, cache, fresh, cache_lengths, new_lengths):
    rows, feat = hidden.shape
    n = lax.axis_size("tensor")
    cores = lax.axis_size("section")
    own = w_query.shape[1] // HD
    wide = w_output.shape[1] // n
    usual = own == GROUP
    o_shared = cores if usual and SPLIT_OUTPUT else 1
    w_query = pltpu.with_memory_space_constraint(w_query, pltpu.VMEM)
    w_output = pltpu.with_memory_space_constraint(w_output, pltpu.VMEM)
    cache = pltpu.with_memory_space_constraint(cache, pltpu.VMEM)
    fresh = pltpu.with_memory_space_constraint(fresh, pltpu.VMEM)

    scratch = [pltpu.VMEM((rows * own, HD), F32)]
    if n == 8:
        mine = call(copy_kernel, (rows, feat), BF16, hidden, flops=LONG)
        near = swap(mine, 1)
        pair = call(stack_kernel, (2, rows, feat), BF16, mine, near)
        acc = call(first_kernel, (rows, own * HD), F32, pair, w_query, flops=FIRST)
        got = [swap(pair, apart) for apart in ORDER]
        for apart, x in zip(ORDER[:2], got):
            step = functools.partial(next_kernel, apart)
            acc = call(step, (rows, own * HD), F32, x, w_query, acc)
        step = functools.partial(last_kernel, ORDER[2])
        q = call(step, (n, rows * own, HD), BF16, got[2], w_query, acc, scratch=scratch)
    else:
        x = call(spread_kernel, (n, rows, feat), BF16, hidden, flops=LONG)
        x = exchange(x, 1)
        q = call(query_kernel, (n, rows * own, HD), BF16, x, w_query, scratch=scratch)
    q = exchange(q, 1)
    if not usual:
        q = q.reshape(KVH, GROUP, rows, HD).transpose(0, 2, 1, 3).reshape(KVH, rows * GROUP, HD)
    part = call(
        attend_kernel,
        (o_shared * KVH, rows * GROUP + STATS, HD),
        BF16,
        cache_lengths,
        new_lengths,
        q,
        cache,
        fresh,
        flops=ATTEND,
        specs=[SMEM] * 2 + [VMEM] * 3,
    )
    if not usual:
        stats = jnp.broadcast_to(part[:1, rows * GROUP :], (n, STATS, HD))
        part = part[:, : rows * GROUP].reshape(KVH, rows, GROUP, HD).transpose(0, 2, 1, 3)
        part = jnp.concatenate([part.reshape(n, rows * own, HD), stats], axis=1)
    part = exchange(part, o_shared)
    terms = call(
        functools.partial(project_kernel, o_shared, own),
        (o_shared * n, rows, wide // o_shared),
        BF16,
        part,
        w_output,
        scratch=[pltpu.VMEM((rows * own, HD), F32)],
    )
    terms = exchange(terms, o_shared)
    return call(sum_kernel, (rows, wide), BF16, terms)


def solution(mesh):
    return jax.shard_map(
        body,
        mesh=mesh,
        in_specs=(
            P(("groups", "section"), "tensor"),
            P(None, "tensor"),
            P("tensor", None),
            P(("groups", "section"), "tensor", None),
            P(("groups", "section"), "tensor", None),
            P(("groups", "section")),
            P(("groups", "section")),
        ),
        out_specs=P(("groups", "section"), "tensor"),
        check_vma=False,
    )
```

```python
import functools

import jax
import jax.numpy as jnp
from jax import lax
from jax.experimental import pallas as pl
from jax.experimental.pallas import tpu as pltpu
from jax.sharding import PartitionSpec as P

KVH = 8
HD = 128
GROUP = 8
HEADS = KVH * GROUP
STATS = 8
F32 = jnp.float32
BF16 = jnp.bfloat16
VMEM = pl.BlockSpec(memory_space=pltpu.VMEM)
SMEM = pl.BlockSpec(memory_space=pltpu.SMEM)
BOTH = ("section", "tensor")
SPLIT_OUTPUT = False
ORDER = (4, 6, 2)
LONG = 10**12
FIRST = 0
ATTEND = 0


def exchange(x, shared):
    return lax.all_to_all(x, BOTH if shared > 1 else "tensor", 0, 0, tiled=True)


def dot(a, b):
    return jnp.dot(a, b, preferred_element_type=F32)


def swap(x, apart):
    n = lax.axis_size("tensor")
    return lax.ppermute(x, "tensor", [(i, i ^ apart) for i in range(n)])


def call(kernel, shape, dtype, *args, specs=None, scratch=(), flops=0):
    return pl.pallas_call(
        kernel,
        in_specs=specs or [VMEM] * len(args),
        out_specs=VMEM,
        out_shape=jax.ShapeDtypeStruct(shape, dtype),
        scratch_shapes=scratch,
        cost_estimate=pl.CostEstimate(flops=flops, bytes_accessed=0, transcendentals=0),
        compiler_params=pltpu.CompilerParams(vmem_limit_bytes=8 << 20),
    )(*args)


def spread_kernel(x_ref, o_ref):
    o_ref[...] = jnp.broadcast_to(x_ref[...][None], o_ref.shape)


def copy_kernel(x_ref, o_ref):
    o_ref[...] = x_ref[...]


def stack_kernel(x_ref, y_ref, o_ref):
    o_ref[0] = x_ref[...]
    o_ref[1] = y_ref[...]


def write_queries(acc, o_ref, heads_ref):
    rows = acc.shape[0]
    own = acc.shape[1] // HD
    for h in range(own):
        heads_ref[pl.ds(h, rows, stride=own), :] = acc[:, h * HD : (h + 1) * HD]
    o_ref[...] = jnp.broadcast_to(heads_ref[...].astype(BF16)[None], o_ref.shape)


def query_kernel(all_ref, w_ref, o_ref, heads_ref):
    n, rows, feat = all_ref.shape
    acc = jnp.zeros((rows, w_ref.shape[1]), F32)
    for t in range(n):
        acc += dot(all_ref[t], w_ref[t * feat : (t + 1) * feat, :])
    write_queries(acc, o_ref, heads_ref)


def pair_product(apart, x_ref, w_ref):
    feat = x_ref.shape[2]
    me = lax.axis_index("tensor")
    acc = jnp.zeros((x_ref.shape[1], w_ref.shape[1]), F32)
    for i in range(2):
        at = pl.multiple_of((me ^ (apart + i)) * feat, feat)
        acc += dot(x_ref[i], w_ref[pl.ds(at, feat), :])
    return acc


def first_kernel(x_ref, w_ref, acc_ref):
    acc_ref[...] = pair_product(0, x_ref, w_ref)


def next_kernel(apart, x_ref, w_ref, old_ref, acc_ref):
    acc_ref[...] = old_ref[...] + pair_product(apart, x_ref, w_ref)


def last_kernel(apart, x_ref, w_ref, old_ref, o_ref, heads_ref):
    write_queries(old_ref[...] + pair_product(apart, x_ref, w_ref), o_ref, heads_ref)


def attend_kernel(clen_ref, nlen_ref, q_ref, cache_ref, fresh_ref, o_ref):
    rows, cc, width = cache_ref.shape
    width = width // 2
    fc = fresh_ref.shape[1]
    shares = q_ref.shape[0] // KVH
    part = GROUP // shares
    place = lax.axis_index("tensor")
    lane = lax.broadcasted_iota(jnp.int32, (HD, 2 * HEADS), 1)

    def logits(ref, r, wide, start, length_ref):
        s = [
            dot(ref[r + i, :, 0:width], wide[i])
            for i in range(2)
        ]
        s = s[0] + s[1]
        second = lax.broadcasted_iota(jnp.int32, s.shape, 1) >= HEADS
        length = jnp.where(second, length_ref[r + 1], length_ref[r])
        valid = start + lax.broadcasted_iota(jnp.int32, s.shape, 0) < length
        return jnp.where(valid, s * HD**-0.5, -1e30), valid

    scores = []
    for r in range(0, rows, 2):
        at = slice(r * part, (r + 2) * part)
        both = [
            q_ref[s * KVH + g, at, :].astype(F32) for g in range(KVH) for s in range(shares)
        ]
        q = [x[i * part : (i + 1) * part] for i in range(2) for x in both]
        q = jnp.concatenate(q, axis=0).T
        wide = []
        for i in range(2):
            blocks = []
            for g in range(KVH):
                first = i * HEADS + g * GROUP
                blocks.append(jnp.where((lane >= first) & (lane < first + GROUP), q, 0.0))
            wide.append(jnp.concatenate(blocks, axis=0).astype(BF16))
        scores.append(
            (
                logits(cache_ref, r, wide, place * cc, clen_ref),
                logits(fresh_ref, r, wide, place * fc, nlen_ref),
            )
        )
    stats, weights = [], []
    for (sc, okc), (sf, okf) in scores:
        top = jnp.maximum(
            jnp.max(sc, axis=0, keepdims=True), jnp.max(sf, axis=0, keepdims=True)
        )
        wc = jnp.where(okc, jnp.exp(sc - top), 0.0)
        wf = jnp.where(okf, jnp.exp(sf - top), 0.0)
        total = jnp.sum(wc, axis=0, keepdims=True) + jnp.sum(wf, axis=0, keepdims=True)
        some = total > 0.0
        total = jnp.where(some, total, 1.0)
        inverse = 1.0 / total
        weights.append(((wc * inverse).T.astype(BF16), (wf * inverse).T.astype(BF16)))
        rest = jnp.where(some, top + jnp.log(total), -1e30)
        for _ in range(3):
            piece = rest.astype(BF16).astype(F32)
            stats.append(piece)
            rest = rest - piece
        stats.append(jnp.zeros_like(rest))
    for two, (pc, pf) in enumerate(weights):
        for pair in range(KVH // 2):
            vals = slice(width + 2 * pair * HD, width + 2 * (pair + 1) * HD)
            nums = []
            for i in range(2):
                at = slice(i * HEADS + 2 * pair * GROUP, i * HEADS + 2 * (pair + 1) * GROUP)
                nums.append(
                    dot(pc[at], cache_ref[2 * two + i, :, vals])
                    + dot(pf[at], fresh_ref[2 * two + i, :, vals])
                )
            at = slice(two * 2 * GROUP, (two + 1) * 2 * GROUP)
            for j in range(2):
                num = [x[j * GROUP : (j + 1) * GROUP, j * HD : (j + 1) * HD] for x in nums]
                num = jnp.concatenate(num, axis=0).astype(BF16)
                for d in range(2 * pair + j, o_ref.shape[0], KVH):
                    o_ref[d, at, :] = num
    stats = jnp.concatenate(stats, axis=0).astype(BF16)
    for d in range(o_ref.shape[0]):
        o_ref[d, rows * GROUP :, :] = stats


def project_kernel(shared, own, got_ref, w_ref, o_ref, heads_ref):
    total, both, _ = got_ref.shape
    both -= STATS
    n = total // shared
    rows = both // own
    wide = o_ref.shape[2]
    me = lax.axis_index("tensor")
    line = lax.broadcasted_iota(jnp.int32, (both, HD), 0)
    column = lax.broadcasted_iota(jnp.int32, (both, HD), 1)
    mine = column == (line // own % 2) * HEADS + me * own + line % own
    mine = mine.astype(F32).astype(BF16)
    line = lax.broadcasted_iota(jnp.int32, (both, n * STATS), 0)
    column = lax.broadcasted_iota(jnp.int32, (both, n * STATS), 1)
    pair = (column % STATS) // (STATS // 2) == line // own // 2
    context = []
    for s in range(shared):
        stats = [got_ref[s * n + t, both:, :].astype(F32) for t in range(n)]
        stats = jnp.concatenate(stats, axis=0).astype(BF16)
        pieces = lax.dot_general(
            mine, stats, (((1,), (1,)), ((), ())), preferred_element_type=F32
        )
        pieces = jnp.where(pair, pieces, 0.0)
        logs = [
            jnp.sum(jnp.where(column // STATS == t, pieces, 0.0), axis=1, keepdims=True)
            for t in range(n)
        ]
        top = functools.reduce(jnp.maximum, logs)
        scales = [jnp.exp(x - top) for x in logs]
        inverse = 1.0 / functools.reduce(jnp.add, scales)
        heads_ref[...] = functools.reduce(
            jnp.add,
            [
                got_ref[s * n + t, 0:both, :].astype(F32) * (scales[t] * inverse)
                for t in range(n)
            ],
        )
        context.append(
            jnp.concatenate(
                [heads_ref[pl.ds(h, rows, stride=own), :] for h in range(own)], axis=1
            )
        )
    context = jnp.concatenate(context, axis=0).astype(BF16)
    offset = 0
    if shared > 1:
        offset = lax.axis_index("section") * wide
    for t in range(n):
        at = t * shared * wide + offset
        if shared > 1:
            at = pl.multiple_of(at, HD)
        terms = dot(context, w_ref[:, pl.ds(at, wide)])
        for s in range(shared):
            o_ref[s * n + t] = terms[s * rows : (s + 1) * rows].astype(BF16)


def sum_kernel(x_ref, o_ref):
    total, _, wide = x_ref.shape
    shared = o_ref.shape[1] // wide
    n = total // shared
    for s in range(shared):
        x = x_ref[s * n : (s + 1) * n].astype(F32)
        o_ref[:, s * wide : (s + 1) * wide] = jnp.sum(x, axis=0).astype(BF16)


def body(hidden, w_query, w_output, cache, fresh, cache_lengths, new_lengths):
    rows, feat = hidden.shape
    n = lax.axis_size("tensor")
    cores = lax.axis_size("section")
    own = w_query.shape[1] // HD
    wide = w_output.shape[1] // n
    usual = own == GROUP
    o_shared = cores if usual and SPLIT_OUTPUT else 1
    w_query = pltpu.with_memory_space_constraint(w_query, pltpu.VMEM)
    w_output = pltpu.with_memory_space_constraint(w_output, pltpu.VMEM)
    cache = pltpu.with_memory_space_constraint(cache, pltpu.VMEM)
    fresh = pltpu.with_memory_space_constraint(fresh, pltpu.VMEM)

    scratch = [pltpu.VMEM((rows * own, HD), F32)]
    if n == 8:
        mine = call(copy_kernel, (rows, feat), BF16, hidden, flops=LONG)
        near = swap(mine, 1)
        pair = call(stack_kernel, (2, rows, feat), BF16, mine, near)
        acc = call(first_kernel, (rows, own * HD), F32, pair, w_query, flops=FIRST)
        got = [swap(pair, apart) for apart in ORDER]
        for apart, x in zip(ORDER[:2], got):
            step = functools.partial(next_kernel, apart)
            acc = call(step, (rows, own * HD), F32, x, w_query, acc, flops=10**10 if apart == ORDER[0] else 0)
        step = functools.partial(last_kernel, ORDER[2])
        q = call(step, (n, rows * own, HD), BF16, got[2], w_query, acc, scratch=scratch)
    else:
        x = call(spread_kernel, (n, rows, feat), BF16, hidden, flops=LONG)
        x = exchange(x, 1)
        q = call(query_kernel, (n, rows * own, HD), BF16, x, w_query, scratch=scratch)
    q = exchange(q, 1)
    if not usual:
        q = q.reshape(KVH, GROUP, rows, HD).transpose(0, 2, 1, 3).reshape(KVH, rows * GROUP, HD)
    part = call(
        attend_kernel,
        (o_shared * KVH, rows * GROUP + STATS, HD),
        BF16,
        cache_lengths,
        new_lengths,
        q,
        cache,
        fresh,
        flops=ATTEND,
        specs=[SMEM] * 2 + [VMEM] * 3,
    )
    if not usual:
        stats = jnp.broadcast_to(part[:1, rows * GROUP :], (n, STATS, HD))
        part = part[:, : rows * GROUP].reshape(KVH, rows, GROUP, HD).transpose(0, 2, 1, 3)
        part = jnp.concatenate([part.reshape(n, rows * own, HD), stats], axis=1)
    part = exchange(part, o_shared)
    terms = call(
        functools.partial(project_kernel, o_shared, own),
        (o_shared * n, rows, wide // o_shared),
        BF16,
        part,
        w_output,
        scratch=[pltpu.VMEM((rows * own, HD), F32)],
    )
    terms = exchange(terms, o_shared)
    return call(sum_kernel, (rows, wide), BF16, terms)


def solution(mesh):
    return jax.shard_map(
        body,
        mesh=mesh,
        in_specs=(
            P(("groups", "section"), "tensor"),
            P(None, "tensor"),
            P("tensor", None),
            P(("groups", "section"), "tensor", None),
            P(("groups", "section"), "tensor", None),
            P(("groups", "section")),
            P(("groups", "section")),
        ),
        out_specs=P(("groups", "section"), "tensor"),
        check_vma=False,
    )
```

```python
import functools

import jax
import jax.numpy as jnp
from jax import lax
from jax.experimental import pallas as pl
from jax.experimental.pallas import tpu as pltpu
from jax.sharding import PartitionSpec as P

KVH = 8
HD = 128
GROUP = 8
HEADS = KVH * GROUP
STATS = 8
F32 = jnp.float32
BF16 = jnp.bfloat16
VMEM = pl.BlockSpec(memory_space=pltpu.VMEM)
SMEM = pl.BlockSpec(memory_space=pltpu.SMEM)
BOTH = ("section", "tensor")
SPLIT_OUTPUT = False
ORDER = (4, 6, 2)
LONG = 10**12
FIRST = 0
ATTEND = 0


def exchange(x, shared):
    return lax.all_to_all(x, BOTH if shared > 1 else "tensor", 0, 0, tiled=True)


def dot(a, b):
    return jnp.dot(a, b, preferred_element_type=F32)


def swap(x, apart):
    n = lax.axis_size("tensor")
    return lax.ppermute(x, "tensor", [(i, i ^ apart) for i in range(n)])


def flip(x, apart):
    n = lax.axis_size("tensor")
    return lax.ppermute(x, BOTH, [(i, ((i // n) ^ 1) * n + (i % n ^ apart)) for i in range(2 * n)])


def call(kernel, shape, dtype, *args, specs=None, scratch=(), flops=0):
    return pl.pallas_call(
        kernel,
        in_specs=specs or [VMEM] * len(args),
        out_specs=VMEM,
        out_shape=jax.ShapeDtypeStruct(shape, dtype),
        scratch_shapes=scratch,
        cost_estimate=pl.CostEstimate(flops=flops, bytes_accessed=0, transcendentals=0),
        compiler_params=pltpu.CompilerParams(vmem_limit_bytes=8 << 20),
    )(*args)


def spread_kernel(x_ref, o_ref):
    o_ref[...] = jnp.broadcast_to(x_ref[...][None], o_ref.shape)


def copy_kernel(x_ref, o_ref):
    o_ref[...] = x_ref[...]


def stack_kernel(x_ref, y_ref, o_ref):
    o_ref[0] = x_ref[...]
    o_ref[1] = y_ref[...]


def write_queries(acc, o_ref, heads_ref):
    rows = acc.shape[0]
    own = acc.shape[1] // HD
    for h in range(own):
        heads_ref[pl.ds(h, rows, stride=own), :] = acc[:, h * HD : (h + 1) * HD]
    o_ref[...] = jnp.broadcast_to(heads_ref[...].astype(BF16)[None], o_ref.shape)


def query_kernel(all_ref, w_ref, o_ref, heads_ref):
    n, rows, feat = all_ref.shape
    acc = jnp.zeros((rows, w_ref.shape[1]), F32)
    for t in range(n):
        acc += dot(all_ref[t], w_ref[t * feat : (t + 1) * feat, :])
    write_queries(acc, o_ref, heads_ref)


def pair_product(apart, x_ref, w_ref):
    feat = x_ref.shape[2]
    me = lax.axis_index("tensor")
    acc = jnp.zeros((x_ref.shape[1], w_ref.shape[1]), F32)
    for i in range(2):
        at = pl.multiple_of((me ^ (apart + i)) * feat, feat)
        acc += dot(x_ref[i], w_ref[pl.ds(at, feat), :])
    return acc


def first_kernel(x_ref, w_ref, acc_ref):
    acc_ref[...] = pair_product(0, x_ref, w_ref)


def next_kernel(apart, x_ref, w_ref, old_ref, acc_ref):
    acc_ref[...] = old_ref[...] + pair_product(apart, x_ref, w_ref)


def last_kernel(apart, x_ref, w_ref, old_ref, o_ref, heads_ref):
    write_queries(old_ref[...] + pair_product(apart, x_ref, w_ref), o_ref, heads_ref)


def attend_kernel(clen_ref, nlen_ref, q_ref, cache_ref, fresh_ref, o_ref):
    rows, cc, width = cache_ref.shape
    width = width // 2
    fc = fresh_ref.shape[1]
    shares = q_ref.shape[0] // KVH
    part = GROUP // shares
    place = lax.axis_index("tensor")
    lane = lax.broadcasted_iota(jnp.int32, (HD, 2 * HEADS), 1)

    def logits(ref, r, wide, start, length_ref):
        s = [
            dot(ref[r + i, :, 0:width], wide[i])
            for i in range(2)
        ]
        s = s[0] + s[1]
        second = lax.broadcasted_iota(jnp.int32, s.shape, 1) >= HEADS
        length = jnp.where(second, length_ref[r + 1], length_ref[r])
        valid = start + lax.broadcasted_iota(jnp.int32, s.shape, 0) < length
        return jnp.where(valid, s * HD**-0.5, -1e30), valid

    scores = []
    for r in range(0, rows, 2):
        at = slice(r * part, (r + 2) * part)
        both = [
            q_ref[s * KVH + g, at, :].astype(F32) for g in range(KVH) for s in range(shares)
        ]
        q = [x[i * part : (i + 1) * part] for i in range(2) for x in both]
        q = jnp.concatenate(q, axis=0).T
        wide = []
        for i in range(2):
            blocks = []
            for g in range(KVH):
                first = i * HEADS + g * GROUP
                blocks.append(jnp.where((lane >= first) & (lane < first + GROUP), q, 0.0))
            wide.append(jnp.concatenate(blocks, axis=0).astype(BF16))
        scores.append(
            (
                logits(cache_ref, r, wide, place * cc, clen_ref),
                logits(fresh_ref, r, wide, place * fc, nlen_ref),
            )
        )
    stats, weights = [], []
    for (sc, okc), (sf, okf) in scores:
        top = jnp.maximum(
            jnp.max(sc, axis=0, keepdims=True), jnp.max(sf, axis=0, keepdims=True)
        )
        wc = jnp.where(okc, jnp.exp(sc - top), 0.0)
        wf = jnp.where(okf, jnp.exp(sf - top), 0.0)
        total = jnp.sum(wc, axis=0, keepdims=True) + jnp.sum(wf, axis=0, keepdims=True)
        some = total > 0.0
        total = jnp.where(some, total, 1.0)
        inverse = 1.0 / total
        weights.append(((wc * inverse).T.astype(BF16), (wf * inverse).T.astype(BF16)))
        rest = jnp.where(some, top + jnp.log(total), -1e30)
        for _ in range(3):
            piece = rest.astype(BF16).astype(F32)
            stats.append(piece)
            rest = rest - piece
        stats.append(jnp.zeros_like(rest))
    for two, (pc, pf) in enumerate(weights):
        for pair in range(KVH // 2):
            vals = slice(width + 2 * pair * HD, width + 2 * (pair + 1) * HD)
            nums = []
            for i in range(2):
                at = slice(i * HEADS + 2 * pair * GROUP, i * HEADS + 2 * (pair + 1) * GROUP)
                nums.append(
                    dot(pc[at], cache_ref[2 * two + i, :, vals])
                    + dot(pf[at], fresh_ref[2 * two + i, :, vals])
                )
            at = slice(two * 2 * GROUP, (two + 1) * 2 * GROUP)
            for j in range(2):
                num = [x[j * GROUP : (j + 1) * GROUP, j * HD : (j + 1) * HD] for x in nums]
                num = jnp.concatenate(num, axis=0).astype(BF16)
                for d in range(2 * pair + j, o_ref.shape[0], KVH):
                    o_ref[d, at, :] = num
    stats = jnp.concatenate(stats, axis=0).astype(BF16)
    for d in range(o_ref.shape[0]):
        o_ref[d, rows * GROUP :, :] = stats


def project_kernel(shared, own, got_ref, w_ref, o_ref, heads_ref):
    total, both, _ = got_ref.shape
    both -= STATS
    n = total // shared
    rows = both // own
    wide = o_ref.shape[2]
    me = lax.axis_index("tensor")
    line = lax.broadcasted_iota(jnp.int32, (both, HD), 0)
    column = lax.broadcasted_iota(jnp.int32, (both, HD), 1)
    mine = column == (line // own % 2) * HEADS + me * own + line % own
    mine = mine.astype(F32).astype(BF16)
    line = lax.broadcasted_iota(jnp.int32, (both, n * STATS), 0)
    column = lax.broadcasted_iota(jnp.int32, (both, n * STATS), 1)
    pair = (column % STATS) // (STATS // 2) == line // own // 2
    context = []
    for s in range(shared):
        stats = [got_ref[s * n + t, both:, :].astype(F32) for t in range(n)]
        stats = jnp.concatenate(stats, axis=0).astype(BF16)
        pieces = lax.dot_general(
            mine, stats, (((1,), (1,)), ((), ())), preferred_element_type=F32
        )
        pieces = jnp.where(pair, pieces, 0.0)
        logs = [
            jnp.sum(jnp.where(column // STATS == t, pieces, 0.0), axis=1, keepdims=True)
            for t in range(n)
        ]
        top = functools.reduce(jnp.maximum, logs)
        scales = [jnp.exp(x - top) for x in logs]
        inverse = 1.0 / functools.reduce(jnp.add, scales)
        heads_ref[...] = functools.reduce(
            jnp.add,
            [
                got_ref[s * n + t, 0:both, :].astype(F32) * (scales[t] * inverse)
                for t in range(n)
            ],
        )
        context.append(
            jnp.concatenate(
                [heads_ref[pl.ds(h, rows, stride=own), :] for h in range(own)], axis=1
            )
        )
    context = jnp.concatenate(context, axis=0).astype(BF16)
    offset = 0
    if shared > 1:
        offset = lax.axis_index("section") * wide
    for t in range(n):
        at = t * shared * wide + offset
        if shared > 1:
            at = pl.multiple_of(at, HD)
        terms = dot(context, w_ref[:, pl.ds(at, wide)])
        for s in range(shared):
            o_ref[s * n + t] = terms[s * rows : (s + 1) * rows].astype(BF16)


def sum_kernel(x_ref, o_ref):
    total, _, wide = x_ref.shape
    shared = o_ref.shape[1] // wide
    n = total // shared
    for s in range(shared):
        x = x_ref[s * n : (s + 1) * n].astype(F32)
        o_ref[:, s * wide : (s + 1) * wide] = jnp.sum(x, axis=0).astype(BF16)


def body(hidden, w_query, w_output, cache, fresh, cache_lengths, new_lengths):
    rows, feat = hidden.shape
    n = lax.axis_size("tensor")
    cores = lax.axis_size("section")
    own = w_query.shape[1] // HD
    wide = w_output.shape[1] // n
    usual = own == GROUP
    o_shared = cores if usual and SPLIT_OUTPUT else 1
    w_query = pltpu.with_memory_space_constraint(w_query, pltpu.VMEM)
    w_output = pltpu.with_memory_space_constraint(w_output, pltpu.VMEM)
    cache = pltpu.with_memory_space_constraint(cache, pltpu.VMEM)
    fresh = pltpu.with_memory_space_constraint(fresh, pltpu.VMEM)

    scratch = [pltpu.VMEM((rows * own, HD), F32)]
    if n == 8:
        mine = call(copy_kernel, (rows, feat), BF16, hidden, flops=LONG)
        near = flip(mine, 1)
        pair = call(stack_kernel, (2, rows, feat), BF16, flip(mine, 0), near)
        acc = call(first_kernel, (rows, own * HD), F32, flip(pair, 0), w_query, flops=FIRST)
        got = [flip(pair, apart) for apart in ORDER]
        for apart, x in zip(ORDER[:2], got):
            step = functools.partial(next_kernel, apart)
            acc = call(step, (rows, own * HD), F32, x, w_query, acc, flops=10**10 if apart == ORDER[0] else 0)
        step = functools.partial(last_kernel, ORDER[2])
        q = call(step, (n, rows * own, HD), BF16, got[2], w_query, acc, scratch=scratch)
    else:
        x = call(spread_kernel, (n, rows, feat), BF16, hidden, flops=LONG)
        x = exchange(x, 1)
        q = call(query_kernel, (n, rows * own, HD), BF16, x, w_query, scratch=scratch)
    q = exchange(q, 1)
    if not usual:
        q = q.reshape(KVH, GROUP, rows, HD).transpose(0, 2, 1, 3).reshape(KVH, rows * GROUP, HD)
    part = call(
        attend_kernel,
        (o_shared * KVH, rows * GROUP + STATS, HD),
        BF16,
        cache_lengths,
        new_lengths,
        q,
        cache,
        fresh,
        flops=ATTEND,
        specs=[SMEM] * 2 + [VMEM] * 3,
    )
    if not usual:
        stats = jnp.broadcast_to(part[:1, rows * GROUP :], (n, STATS, HD))
        part = part[:, : rows * GROUP].reshape(KVH, rows, GROUP, HD).transpose(0, 2, 1, 3)
        part = jnp.concatenate([part.reshape(n, rows * own, HD), stats], axis=1)
    part = exchange(part, o_shared)
    terms = call(
        functools.partial(project_kernel, o_shared, own),
        (o_shared * n, rows, wide // o_shared),
        BF16,
        part,
        w_output,
        scratch=[pltpu.VMEM((rows * own, HD), F32)],
    )
    terms = exchange(terms, o_shared)
    return call(sum_kernel, (rows, wide), BF16, terms)


def solution(mesh):
    return jax.shard_map(
        body,
        mesh=mesh,
        in_specs=(
            P(("groups", "section"), "tensor"),
            P(None, "tensor"),
            P("tensor", None),
            P(("groups", "section"), "tensor", None),
            P(("groups", "section"), "tensor", None),
            P(("groups", "section")),
            P(("groups", "section")),
        ),
        out_specs=P(("groups", "section"), "tensor"),
        check_vma=False,
    )
```

```python
import functools

import jax
import jax.numpy as jnp
from jax import lax
from jax.experimental import pallas as pl
from jax.experimental.pallas import tpu as pltpu
from jax.sharding import PartitionSpec as P

KVH = 8
HD = 128
GROUP = 8
HEADS = KVH * GROUP
STATS = 8
F32 = jnp.float32
BF16 = jnp.bfloat16
VMEM = pl.BlockSpec(memory_space=pltpu.VMEM)
SMEM = pl.BlockSpec(memory_space=pltpu.SMEM)
BOTH = ("section", "tensor")
SPLIT_OUTPUT = False
ORDER = (4, 6, 2)
BACK = (4, 6, 2)
ADD = 23000000
PIECE = 11500000
LONG = 10**12
FIRST = 0
ATTEND = 0


def exchange(x, shared):
    return lax.all_to_all(x, BOTH if shared > 1 else "tensor", 0, 0, tiled=True)


def dot(a, b):
    return jnp.dot(a, b, preferred_element_type=F32)


def swap(x, apart):
    n = lax.axis_size("tensor")
    return lax.ppermute(x, "tensor", [(i, i ^ apart) for i in range(n)])


def flip(x, apart):
    n = lax.axis_size("tensor")
    return lax.ppermute(x, BOTH, [(i, ((i // n) ^ 1) * n + (i % n ^ apart)) for i in range(2 * n)])


def call(kernel, shape, dtype, *args, specs=None, scratch=(), flops=0):
    if isinstance(shape, list):
        out = [jax.ShapeDtypeStruct(*x) for x in zip(shape, dtype)]
        outs = [VMEM] * len(out)
    else:
        out, outs = jax.ShapeDtypeStruct(shape, dtype), VMEM
    return pl.pallas_call(
        kernel,
        in_specs=specs or [VMEM] * len(args),
        out_specs=outs,
        out_shape=out,
        scratch_shapes=scratch,
        cost_estimate=pl.CostEstimate(flops=flops, bytes_accessed=0, transcendentals=0),
        compiler_params=pltpu.CompilerParams(vmem_limit_bytes=8 << 20),
    )(*args)


def spread_kernel(x_ref, o_ref):
    o_ref[...] = jnp.broadcast_to(x_ref[...][None], o_ref.shape)


def copy_kernel(x_ref, o_ref):
    o_ref[...] = x_ref[...]


def stack_kernel(x_ref, y_ref, o_ref):
    o_ref[0] = x_ref[...]
    o_ref[1] = y_ref[...]


def write_queries(acc, o_ref, heads_ref):
    rows = acc.shape[0]
    own = acc.shape[1] // HD
    for h in range(own):
        heads_ref[pl.ds(h, rows, stride=own), :] = acc[:, h * HD : (h + 1) * HD]
    o_ref[...] = jnp.broadcast_to(heads_ref[...].astype(BF16)[None], o_ref.shape)


def query_kernel(all_ref, w_ref, o_ref, heads_ref):
    n, rows, feat = all_ref.shape
    acc = jnp.zeros((rows, w_ref.shape[1]), F32)
    for t in range(n):
        acc += dot(all_ref[t], w_ref[t * feat : (t + 1) * feat, :])
    write_queries(acc, o_ref, heads_ref)


def pair_product(apart, x_ref, w_ref):
    feat = x_ref.shape[2]
    me = lax.axis_index("tensor")
    acc = jnp.zeros((x_ref.shape[1], w_ref.shape[1]), F32)
    for i in range(2):
        at = pl.multiple_of((me ^ (apart + i)) * feat, feat)
        acc += dot(x_ref[i], w_ref[pl.ds(at, feat), :])
    return acc


def first_kernel(x_ref, w_ref, acc_ref):
    acc_ref[...] = pair_product(0, x_ref, w_ref)


def next_kernel(apart, x_ref, w_ref, old_ref, acc_ref):
    acc_ref[...] = old_ref[...] + pair_product(apart, x_ref, w_ref)


def last_kernel(apart, x_ref, w_ref, old_ref, o_ref, heads_ref):
    write_queries(old_ref[...] + pair_product(apart, x_ref, w_ref), o_ref, heads_ref)


def attend_kernel(clen_ref, nlen_ref, q_ref, cache_ref, fresh_ref, o_ref):
    rows, cc, width = cache_ref.shape
    width = width // 2
    fc = fresh_ref.shape[1]
    shares = q_ref.shape[0] // KVH
    part = GROUP // shares
    place = lax.axis_index("tensor")
    lane = lax.broadcasted_iota(jnp.int32, (HD, 2 * HEADS), 1)

    def logits(ref, r, wide, start, length_ref):
        s = [
            dot(ref[r + i, :, 0:width], wide[i])
            for i in range(2)
        ]
        s = s[0] + s[1]
        second = lax.broadcasted_iota(jnp.int32, s.shape, 1) >= HEADS
        length = jnp.where(second, length_ref[r + 1], length_ref[r])
        valid = start + lax.broadcasted_iota(jnp.int32, s.shape, 0) < length
        return jnp.where(valid, s * HD**-0.5, -1e30), valid

    scores = []
    for r in range(0, rows, 2):
        at = slice(r * part, (r + 2) * part)
        both = [
            q_ref[s * KVH + g, at, :].astype(F32) for g in range(KVH) for s in range(shares)
        ]
        q = [x[i * part : (i + 1) * part] for i in range(2) for x in both]
        q = jnp.concatenate(q, axis=0).T
        wide = []
        for i in range(2):
            blocks = []
            for g in range(KVH):
                first = i * HEADS + g * GROUP
                blocks.append(jnp.where((lane >= first) & (lane < first + GROUP), q, 0.0))
            wide.append(jnp.concatenate(blocks, axis=0).astype(BF16))
        scores.append(
            (
                logits(cache_ref, r, wide, place * cc, clen_ref),
                logits(fresh_ref, r, wide, place * fc, nlen_ref),
            )
        )
    stats, weights = [], []
    for (sc, okc), (sf, okf) in scores:
        top = jnp.maximum(
            jnp.max(sc, axis=0, keepdims=True), jnp.max(sf, axis=0, keepdims=True)
        )
        wc = jnp.where(okc, jnp.exp(sc - top), 0.0)
        wf = jnp.where(okf, jnp.exp(sf - top), 0.0)
        total = jnp.sum(wc, axis=0, keepdims=True) + jnp.sum(wf, axis=0, keepdims=True)
        some = total > 0.0
        total = jnp.where(some, total, 1.0)
        inverse = 1.0 / total
        weights.append(((wc * inverse).T.astype(BF16), (wf * inverse).T.astype(BF16)))
        rest = jnp.where(some, top + jnp.log(total), -1e30)
        for _ in range(3):
            piece = rest.astype(BF16).astype(F32)
            stats.append(piece)
            rest = rest - piece
        stats.append(jnp.zeros_like(rest))
    for two, (pc, pf) in enumerate(weights):
        for pair in range(KVH // 2):
            vals = slice(width + 2 * pair * HD, width + 2 * (pair + 1) * HD)
            nums = []
            for i in range(2):
                at = slice(i * HEADS + 2 * pair * GROUP, i * HEADS + 2 * (pair + 1) * GROUP)
                nums.append(
                    dot(pc[at], cache_ref[2 * two + i, :, vals])
                    + dot(pf[at], fresh_ref[2 * two + i, :, vals])
                )
            at = slice(two * 2 * GROUP, (two + 1) * 2 * GROUP)
            for j in range(2):
                num = [x[j * GROUP : (j + 1) * GROUP, j * HD : (j + 1) * HD] for x in nums]
                num = jnp.concatenate(num, axis=0).astype(BF16)
                for d in range(2 * pair + j, o_ref.shape[0], KVH):
                    o_ref[d, at, :] = num
    stats = jnp.concatenate(stats, axis=0).astype(BF16)
    for d in range(o_ref.shape[0]):
        o_ref[d, rows * GROUP :, :] = stats


def combine(shared, own, got_ref, heads_ref):
    total, both, _ = got_ref.shape
    both -= STATS
    n = total // shared
    rows = both // own
    me = lax.axis_index("tensor")
    line = lax.broadcasted_iota(jnp.int32, (both, HD), 0)
    column = lax.broadcasted_iota(jnp.int32, (both, HD), 1)
    mine = column == (line // own % 2) * HEADS + me * own + line % own
    mine = mine.astype(F32).astype(BF16)
    line = lax.broadcasted_iota(jnp.int32, (both, n * STATS), 0)
    column = lax.broadcasted_iota(jnp.int32, (both, n * STATS), 1)
    pair = (column % STATS) // (STATS // 2) == line // own // 2
    context = []
    for s in range(shared):
        stats = [got_ref[s * n + t, both:, :].astype(F32) for t in range(n)]
        stats = jnp.concatenate(stats, axis=0).astype(BF16)
        pieces = lax.dot_general(
            mine, stats, (((1,), (1,)), ((), ())), preferred_element_type=F32
        )
        pieces = jnp.where(pair, pieces, 0.0)
        logs = [
            jnp.sum(jnp.where(column // STATS == t, pieces, 0.0), axis=1, keepdims=True)
            for t in range(n)
        ]
        top = functools.reduce(jnp.maximum, logs)
        scales = [jnp.exp(x - top) for x in logs]
        inverse = 1.0 / functools.reduce(jnp.add, scales)
        heads_ref[...] = functools.reduce(
            jnp.add,
            [
                got_ref[s * n + t, 0:both, :].astype(F32) * (scales[t] * inverse)
                for t in range(n)
            ],
        )
        context.append(
            jnp.concatenate(
                [heads_ref[pl.ds(h, rows, stride=own), :] for h in range(own)], axis=1
            )
        )
    return jnp.concatenate(context, axis=0).astype(BF16)


def project_kernel(shared, own, got_ref, w_ref, o_ref, heads_ref):
    context = combine(shared, own, got_ref, heads_ref)
    total, rows, wide = o_ref.shape
    n = total // shared
    offset = 0
    if shared > 1:
        offset = lax.axis_index("section") * wide
    for t in range(n):
        at = t * shared * wide + offset
        if shared > 1:
            at = pl.multiple_of(at, HD)
        terms = dot(context, w_ref[:, pl.ds(at, wide)])
        for s in range(shared):
            o_ref[s * n + t] = terms[s * rows : (s + 1) * rows].astype(BF16)


def pair_terms(apart, context, w_ref, o_ref):
    wide = o_ref.shape[2]
    me = lax.axis_index("tensor")
    for i in range(2):
        at = pl.multiple_of((me ^ (apart + i)) * wide, wide)
        o_ref[i] = dot(context, w_ref[:, pl.ds(at, wide)]).astype(o_ref.dtype)


def begin_kernel(apart, own, got_ref, w_ref, o_ref, context_ref, heads_ref):
    context = combine(1, own, got_ref, heads_ref)
    context_ref[...] = context
    pair_terms(apart, context, w_ref, o_ref)


def terms_kernel(apart, context_ref, w_ref, o_ref):
    pair_terms(apart, context_ref[...], w_ref, o_ref)


def widen_kernel(x_ref, o_ref):
    o_ref[...] = x_ref[...].astype(F32)


def merge_kernel(x_ref, y_ref, o_ref):
    o_ref[...] = x_ref[...].astype(F32) + y_ref[...].astype(F32)


def finish_kernel(x_ref, y_ref, mine_ref, far_ref):
    out = x_ref[...] + y_ref[...].astype(F32)
    mine_ref[...] = out[0]
    far_ref[...] = out[1].astype(BF16)


def add_kernel(x_ref, y_ref, o_ref):
    o_ref[...] = (x_ref[...] + y_ref[...].astype(F32)).astype(BF16)


def sum_kernel(x_ref, o_ref):
    total, _, wide = x_ref.shape
    shared = o_ref.shape[1] // wide
    n = total // shared
    for s in range(shared):
        x = x_ref[s * n : (s + 1) * n].astype(F32)
        o_ref[:, s * wide : (s + 1) * wide] = jnp.sum(x, axis=0).astype(BF16)


def body(hidden, w_query, w_output, cache, fresh, cache_lengths, new_lengths):
    rows, feat = hidden.shape
    n = lax.axis_size("tensor")
    cores = lax.axis_size("section")
    own = w_query.shape[1] // HD
    wide = w_output.shape[1] // n
    usual = own == GROUP
    o_shared = cores if usual and SPLIT_OUTPUT else 1
    w_query = pltpu.with_memory_space_constraint(w_query, pltpu.VMEM)
    w_output = pltpu.with_memory_space_constraint(w_output, pltpu.VMEM)
    cache = pltpu.with_memory_space_constraint(cache, pltpu.VMEM)
    fresh = pltpu.with_memory_space_constraint(fresh, pltpu.VMEM)

    scratch = [pltpu.VMEM((rows * own, HD), F32)]
    if n == 8:
        mine = call(copy_kernel, (rows, feat), BF16, hidden, flops=LONG)
        near = flip(mine, 1)
        pair = call(stack_kernel, (2, rows, feat), BF16, flip(mine, 0), near)
        acc = call(first_kernel, (rows, own * HD), F32, flip(pair, 0), w_query, flops=FIRST)
        got = [flip(pair, apart) for apart in ORDER]
        for apart, x in zip(ORDER[:2], got):
            step = functools.partial(next_kernel, apart)
            acc = call(step, (rows, own * HD), F32, x, w_query, acc, flops=10**10 if apart == ORDER[0] else 0)
        step = functools.partial(last_kernel, ORDER[2])
        q = call(step, (n, rows * own, HD), BF16, got[2], w_query, acc, scratch=scratch)
    else:
        x = call(spread_kernel, (n, rows, feat), BF16, hidden, flops=LONG)
        x = exchange(x, 1)
        q = call(query_kernel, (n, rows * own, HD), BF16, x, w_query, scratch=scratch)
    q = exchange(q, 1)
    if not usual:
        q = q.reshape(KVH, GROUP, rows, HD).transpose(0, 2, 1, 3).reshape(KVH, rows * GROUP, HD)
    part = call(
        attend_kernel,
        (o_shared * KVH, rows * GROUP + STATS, HD),
        BF16,
        cache_lengths,
        new_lengths,
        q,
        cache,
        fresh,
        flops=ATTEND,
        specs=[SMEM] * 2 + [VMEM] * 3,
    )
    if not usual:
        stats = jnp.broadcast_to(part[:1, rows * GROUP :], (n, STATS, HD))
        part = part[:, : rows * GROUP].reshape(KVH, rows, GROUP, HD).transpose(0, 2, 1, 3)
        part = jnp.concatenate([part.reshape(n, rows * own, HD), stats], axis=1)
    part = exchange(part, o_shared)
    scratch = [pltpu.VMEM((rows * own, HD), F32)]
    if n == 8:
        two = (2, rows, wide)
        step = functools.partial(begin_kernel, BACK[0], own)
        shapes = [two, (rows, own * HD)]
        out, context = call(
            step, shapes, [BF16, BF16], part, w_output, scratch=scratch, flops=PIECE
        )
        got = [flip(out, BACK[0])]
        for apart in BACK[1:]:
            step = functools.partial(terms_kernel, apart)
            out = call(step, two, BF16, context, w_output, flops=PIECE)
            got.append(flip(out, apart))
        own_terms = call(
            functools.partial(terms_kernel, 0), two, BF16, context, w_output, flops=PIECE
        )
        out = call(widen_kernel, two, F32, got[0], flops=ADD)
        out = call(merge_kernel, two, F32, out, got[1], flops=ADD)
        out = call(merge_kernel, two, F32, out, got[2], flops=ADD)
        mine, far = call(
            finish_kernel, [(rows, wide)] * 2, [F32, BF16], out, flip(own_terms, 0), flops=ADD
        )
        return call(add_kernel, (rows, wide), BF16, flip(mine, 0), flip(far, 1))
    terms = call(
        functools.partial(project_kernel, o_shared, own),
        (o_shared * n, rows, wide // o_shared),
        BF16,
        part,
        w_output,
        scratch=scratch,
    )
    terms = exchange(terms, o_shared)
    return call(sum_kernel, (rows, wide), BF16, terms)


def solution(mesh):
    return jax.shard_map(
        body,
        mesh=mesh,
        in_specs=(
            P(("groups", "section"), "tensor"),
            P(None, "tensor"),
            P("tensor", None),
            P(("groups", "section"), "tensor", None),
            P(("groups", "section"), "tensor", None),
            P(("groups", "section")),
            P(("groups", "section")),
        ),
        out_specs=P(("groups", "section"), "tensor"),
        check_vma=False,
    )
```

```python
import functools

import jax
import jax.numpy as jnp
from jax import lax
from jax.experimental import pallas as pl
from jax.experimental.pallas import tpu as pltpu
from jax.sharding import PartitionSpec as P

KVH = 8
HD = 128
GROUP = 8
HEADS = KVH * GROUP
STATS = 8
F32 = jnp.float32
BF16 = jnp.bfloat16
VMEM = pl.BlockSpec(memory_space=pltpu.VMEM)
SMEM = pl.BlockSpec(memory_space=pltpu.SMEM)
BOTH = ("section", "tensor")
SPLIT_OUTPUT = False
ORDER = (4, 6, 2)
MIDDLE = (4, 6, 2)
BACK = (4, 6, 2)
ADD = 23000000
PIECE = 11500000
LONG = 10**12
FIRST = 0
ATTEND = 0


def exchange(x, shared):
    return lax.all_to_all(x, BOTH if shared > 1 else "tensor", 0, 0, tiled=True)


def dot(a, b):
    return jnp.dot(a, b, preferred_element_type=F32)


def swap(x, apart):
    n = lax.axis_size("tensor")
    return lax.ppermute(x, "tensor", [(i, i ^ apart) for i in range(n)])


def flip(x, apart):
    n = lax.axis_size("tensor")
    return lax.ppermute(x, BOTH, [(i, ((i // n) ^ 1) * n + (i % n ^ apart)) for i in range(2 * n)])


def call(kernel, shape, dtype, *args, specs=None, scratch=(), flops=0):
    if isinstance(shape, list):
        out = [jax.ShapeDtypeStruct(*x) for x in zip(shape, dtype)]
        outs = [VMEM] * len(out)
    else:
        out, outs = jax.ShapeDtypeStruct(shape, dtype), VMEM
    return pl.pallas_call(
        kernel,
        in_specs=specs or [VMEM] * len(args),
        out_specs=outs,
        out_shape=out,
        scratch_shapes=scratch,
        cost_estimate=pl.CostEstimate(flops=flops, bytes_accessed=0, transcendentals=0),
        compiler_params=pltpu.CompilerParams(vmem_limit_bytes=8 << 20),
    )(*args)


def spread_kernel(x_ref, o_ref):
    o_ref[...] = jnp.broadcast_to(x_ref[...][None], o_ref.shape)


def copy_kernel(x_ref, o_ref):
    o_ref[...] = x_ref[...]


def stack_kernel(x_ref, y_ref, o_ref):
    o_ref[0] = x_ref[...]
    o_ref[1] = y_ref[...]


def write_queries(acc, o_ref, heads_ref):
    rows = acc.shape[0]
    own = acc.shape[1] // HD
    for h in range(own):
        heads_ref[pl.ds(h, rows, stride=own), :] = acc[:, h * HD : (h + 1) * HD]
    q = heads_ref[...].astype(BF16)
    o_ref[...] = q if len(o_ref.shape) == 2 else jnp.broadcast_to(q[None], o_ref.shape)


def query_kernel(all_ref, w_ref, o_ref, heads_ref):
    n, rows, feat = all_ref.shape
    acc = jnp.zeros((rows, w_ref.shape[1]), F32)
    for t in range(n):
        acc += dot(all_ref[t], w_ref[t * feat : (t + 1) * feat, :])
    write_queries(acc, o_ref, heads_ref)


def pair_product(apart, x_ref, w_ref):
    feat = x_ref.shape[2]
    me = lax.axis_index("tensor")
    acc = jnp.zeros((x_ref.shape[1], w_ref.shape[1]), F32)
    for i in range(2):
        at = pl.multiple_of((me ^ (apart + i)) * feat, feat)
        acc += dot(x_ref[i], w_ref[pl.ds(at, feat), :])
    return acc


def first_kernel(x_ref, w_ref, acc_ref):
    acc_ref[...] = pair_product(0, x_ref, w_ref)


def next_kernel(apart, x_ref, w_ref, old_ref, acc_ref):
    acc_ref[...] = old_ref[...] + pair_product(apart, x_ref, w_ref)


def last_kernel(apart, x_ref, w_ref, old_ref, o_ref, heads_ref):
    write_queries(old_ref[...] + pair_product(apart, x_ref, w_ref), o_ref, heads_ref)


def attend_kernel(clen_ref, nlen_ref, q_ref, cache_ref, fresh_ref, o_ref):
    rows, cc, width = cache_ref.shape
    width = width // 2
    fc = fresh_ref.shape[1]
    shares = q_ref.shape[0] // KVH
    part = GROUP // shares
    place = lax.axis_index("tensor")
    lane = lax.broadcasted_iota(jnp.int32, (HD, 2 * HEADS), 1)

    def logits(ref, r, wide, start, length_ref):
        s = [
            dot(ref[r + i, :, 0:width], wide[i])
            for i in range(2)
        ]
        s = s[0] + s[1]
        second = lax.broadcasted_iota(jnp.int32, s.shape, 1) >= HEADS
        length = jnp.where(second, length_ref[r + 1], length_ref[r])
        valid = start + lax.broadcasted_iota(jnp.int32, s.shape, 0) < length
        return jnp.where(valid, s * HD**-0.5, -1e30), valid

    scores = []
    for r in range(0, rows, 2):
        at = slice(r * part, (r + 2) * part)
        both = [
            q_ref[s * KVH + g, at, :].astype(F32) for g in range(KVH) for s in range(shares)
        ]
        q = [x[i * part : (i + 1) * part] for i in range(2) for x in both]
        q = jnp.concatenate(q, axis=0).T
        wide = []
        for i in range(2):
            blocks = []
            for g in range(KVH):
                first = i * HEADS + g * GROUP
                blocks.append(jnp.where((lane >= first) & (lane < first + GROUP), q, 0.0))
            wide.append(jnp.concatenate(blocks, axis=0).astype(BF16))
        scores.append(
            (
                logits(cache_ref, r, wide, place * cc, clen_ref),
                logits(fresh_ref, r, wide, place * fc, nlen_ref),
            )
        )
    stats, weights = [], []
    for (sc, okc), (sf, okf) in scores:
        top = jnp.maximum(
            jnp.max(sc, axis=0, keepdims=True), jnp.max(sf, axis=0, keepdims=True)
        )
        wc = jnp.where(okc, jnp.exp(sc - top), 0.0)
        wf = jnp.where(okf, jnp.exp(sf - top), 0.0)
        total = jnp.sum(wc, axis=0, keepdims=True) + jnp.sum(wf, axis=0, keepdims=True)
        some = total > 0.0
        total = jnp.where(some, total, 1.0)
        inverse = 1.0 / total
        weights.append(((wc * inverse).T.astype(BF16), (wf * inverse).T.astype(BF16)))
        rest = jnp.where(some, top + jnp.log(total), -1e30)
        for _ in range(3):
            piece = rest.astype(BF16).astype(F32)
            stats.append(piece)
            rest = rest - piece
        stats.append(jnp.zeros_like(rest))
    for two, (pc, pf) in enumerate(weights):
        for pair in range(KVH // 2):
            vals = slice(width + 2 * pair * HD, width + 2 * (pair + 1) * HD)
            nums = []
            for i in range(2):
                at = slice(i * HEADS + 2 * pair * GROUP, i * HEADS + 2 * (pair + 1) * GROUP)
                nums.append(
                    dot(pc[at], cache_ref[2 * two + i, :, vals])
                    + dot(pf[at], fresh_ref[2 * two + i, :, vals])
                )
            at = slice(two * 2 * GROUP, (two + 1) * 2 * GROUP)
            for j in range(2):
                num = [x[j * GROUP : (j + 1) * GROUP, j * HD : (j + 1) * HD] for x in nums]
                num = jnp.concatenate(num, axis=0).astype(BF16)
                for d in range(2 * pair + j, o_ref.shape[0], KVH):
                    o_ref[d, at, :] = num
    stats = jnp.concatenate(stats, axis=0).astype(BF16)
    for d in range(o_ref.shape[0]):
        o_ref[d, rows * GROUP :, :] = stats


def order_kernel(x_ref, y_ref, o_ref):
    odd = lax.axis_index("tensor") % 2
    o_ref[odd] = x_ref[...]
    o_ref[1 - odd] = y_ref[...]


def pair_attend_kernel(apart, clen_ref, nlen_ref, q_ref, cache_ref, fresh_ref, o_ref):
    rows, cc, width = cache_ref.shape
    width = width // 2
    fc = fresh_ref.shape[1]
    both = 2 * GROUP
    place = lax.axis_index("tensor")
    at = (place ^ apart) // 2 * (2 * HD)
    keys = pl.ds(pl.multiple_of(at, 2 * HD), 2 * HD)
    vals = pl.ds(pl.multiple_of(width + at, 2 * HD), 2 * HD)
    lane = lax.broadcasted_iota(jnp.int32, (HD, rows * both), 1)
    heads = [q_ref[i].astype(F32) for i in range(2)]
    q = [heads[i][r * GROUP : (r + 1) * GROUP] for r in range(rows) for i in range(2)]
    q = jnp.concatenate(q, axis=0).T
    wide = []
    for r in range(rows):
        blocks = []
        for i in range(2):
            first = r * both + i * GROUP
            blocks.append(jnp.where((lane >= first) & (lane < first + GROUP), q, 0.0))
        wide.append(jnp.concatenate(blocks, axis=0).astype(BF16))

    def logits(ref, start, length_ref):
        s = functools.reduce(jnp.add, [dot(ref[r, :, keys], wide[r]) for r in range(rows)])
        request = lax.broadcasted_iota(jnp.int32, s.shape, 1) // both
        length = jnp.full(s.shape, length_ref[0], jnp.int32)
        for r in range(1, rows):
            length = jnp.where(request == r, length_ref[r], length)
        valid = start + lax.broadcasted_iota(jnp.int32, s.shape, 0) < length
        return jnp.where(valid, s * HD**-0.5, -1e30), valid

    sc, okc = logits(cache_ref, place * cc, clen_ref)
    sf, okf = logits(fresh_ref, place * fc, nlen_ref)
    top = jnp.maximum(jnp.max(sc, axis=0, keepdims=True), jnp.max(sf, axis=0, keepdims=True))
    wc = jnp.where(okc, jnp.exp(sc - top), 0.0)
    wf = jnp.where(okf, jnp.exp(sf - top), 0.0)
    total = jnp.sum(wc, axis=0, keepdims=True) + jnp.sum(wf, axis=0, keepdims=True)
    some = total > 0.0
    total = jnp.where(some, total, 1.0)
    inverse = 1.0 / total
    pc = (wc * inverse).T.astype(BF16)
    pf = (wf * inverse).T.astype(BF16)
    nums = []
    for r in range(rows):
        mine = slice(r * both, (r + 1) * both)
        nums.append(dot(pc[mine], cache_ref[r, :, vals]) + dot(pf[mine], fresh_ref[r, :, vals]))
    for i in range(2):
        for r in range(0, rows, 2):
            num = [x[i * GROUP : (i + 1) * GROUP, i * HD : (i + 1) * HD] for x in nums[r : r + 2]]
            o_ref[i, r * GROUP : (r + 2) * GROUP, :] = jnp.concatenate(num, axis=0).astype(BF16)
    rest = jnp.where(some, top + jnp.log(total), -1e30)
    stats = []
    for _ in range(3):
        piece = rest.astype(BF16).astype(F32)
        stats.append(piece)
        rest = rest - piece
    stats.append(jnp.zeros((STATS - 3, rows * both), F32))
    stats = jnp.concatenate(stats, axis=0)
    stats = jnp.concatenate([stats, jnp.zeros((STATS, HD - rows * both), F32)], axis=1)
    for i in range(2):
        o_ref[i, rows * GROUP :, :] = stats.astype(BF16)


def part_kernel(a_ref, b_ref, c_ref, d_ref, mine_ref, far_ref):
    odd = lax.axis_index("tensor") % 2
    for i, ref in enumerate((a_ref, b_ref, c_ref, d_ref)):
        mine_ref[i] = ref[odd]
        far_ref[i] = ref[1 - odd]


def combine_pair(a_ref, b_ref, heads_ref):
    n = 2 * a_ref.shape[0]
    both = a_ref.shape[1] - STATS
    rows = both // GROUP
    odd = lax.axis_index("tensor") % 2
    line = lax.broadcasted_iota(jnp.int32, (both, HD), 0)
    column = lax.broadcasted_iota(jnp.int32, (both, HD), 1)
    mine = column == (line // GROUP) * 2 * GROUP + odd * GROUP + line % GROUP
    mine = mine.astype(F32).astype(BF16)
    column = lax.broadcasted_iota(jnp.int32, (both, n * STATS), 1)
    parts = [ref.at[i] for ref in (a_ref, b_ref) for i in range(n // 2)]
    stats = [x[both:, :].astype(F32) for x in parts]
    stats = jnp.concatenate(stats, axis=0).astype(BF16)
    pieces = lax.dot_general(mine, stats, (((1,), (1,)), ((), ())), preferred_element_type=F32)
    logs = [
        jnp.sum(jnp.where(column // STATS == t, pieces, 0.0), axis=1, keepdims=True)
        for t in range(n)
    ]
    top = functools.reduce(jnp.maximum, logs)
    scales = [jnp.exp(x - top) for x in logs]
    inverse = 1.0 / functools.reduce(jnp.add, scales)
    heads_ref[...] = functools.reduce(
        jnp.add,
        [x[0:both, :].astype(F32) * (scale * inverse) for x, scale in zip(parts, scales)],
    )
    context = [heads_ref[pl.ds(h, rows, stride=GROUP), :] for h in range(GROUP)]
    return jnp.concatenate(context, axis=1).astype(BF16)


def combine(shared, own, got_ref, heads_ref):
    total, both, _ = got_ref.shape
    both -= STATS
    n = total // shared
    rows = both // own
    me = lax.axis_index("tensor")
    line = lax.broadcasted_iota(jnp.int32, (both, HD), 0)
    column = lax.broadcasted_iota(jnp.int32, (both, HD), 1)
    mine = column == (line // own % 2) * HEADS + me * own + line % own
    mine = mine.astype(F32).astype(BF16)
    line = lax.broadcasted_iota(jnp.int32, (both, n * STATS), 0)
    column = lax.broadcasted_iota(jnp.int32, (both, n * STATS), 1)
    pair = (column % STATS) // (STATS // 2) == line // own // 2
    context = []
    for s in range(shared):
        stats = [got_ref[s * n + t, both:, :].astype(F32) for t in range(n)]
        stats = jnp.concatenate(stats, axis=0).astype(BF16)
        pieces = lax.dot_general(
            mine, stats, (((1,), (1,)), ((), ())), preferred_element_type=F32
        )
        pieces = jnp.where(pair, pieces, 0.0)
        logs = [
            jnp.sum(jnp.where(column // STATS == t, pieces, 0.0), axis=1, keepdims=True)
            for t in range(n)
        ]
        top = functools.reduce(jnp.maximum, logs)
        scales = [jnp.exp(x - top) for x in logs]
        inverse = 1.0 / functools.reduce(jnp.add, scales)
        heads_ref[...] = functools.reduce(
            jnp.add,
            [
                got_ref[s * n + t, 0:both, :].astype(F32) * (scales[t] * inverse)
                for t in range(n)
            ],
        )
        context.append(
            jnp.concatenate(
                [heads_ref[pl.ds(h, rows, stride=own), :] for h in range(own)], axis=1
            )
        )
    return jnp.concatenate(context, axis=0).astype(BF16)


def project_kernel(shared, own, got_ref, w_ref, o_ref, heads_ref):
    context = combine(shared, own, got_ref, heads_ref)
    total, rows, wide = o_ref.shape
    n = total // shared
    offset = 0
    if shared > 1:
        offset = lax.axis_index("section") * wide
    for t in range(n):
        at = t * shared * wide + offset
        if shared > 1:
            at = pl.multiple_of(at, HD)
        terms = dot(context, w_ref[:, pl.ds(at, wide)])
        for s in range(shared):
            o_ref[s * n + t] = terms[s * rows : (s + 1) * rows].astype(BF16)


def pair_terms(apart, context, w_ref, o_ref):
    wide = o_ref.shape[2]
    me = lax.axis_index("tensor")
    for i in range(2):
        at = pl.multiple_of((me ^ (apart + i)) * wide, wide)
        o_ref[i] = dot(context, w_ref[:, pl.ds(at, wide)]).astype(o_ref.dtype)


def begin_kernel(apart, a_ref, b_ref, w_ref, o_ref, context_ref, heads_ref):
    context = combine_pair(a_ref, b_ref, heads_ref)
    context_ref[...] = context
    pair_terms(apart, context, w_ref, o_ref)


def terms_kernel(apart, context_ref, w_ref, o_ref):
    pair_terms(apart, context_ref[...], w_ref, o_ref)


def widen_kernel(x_ref, o_ref):
    o_ref[...] = x_ref[...].astype(F32)


def merge_kernel(x_ref, y_ref, o_ref):
    o_ref[...] = x_ref[...].astype(F32) + y_ref[...].astype(F32)


def finish_kernel(x_ref, y_ref, mine_ref, far_ref):
    out = x_ref[...] + y_ref[...].astype(F32)
    mine_ref[...] = out[0]
    far_ref[...] = out[1].astype(BF16)


def add_kernel(x_ref, y_ref, o_ref):
    o_ref[...] = (x_ref[...] + y_ref[...].astype(F32)).astype(BF16)


def sum_kernel(x_ref, o_ref):
    total, _, wide = x_ref.shape
    shared = o_ref.shape[1] // wide
    n = total // shared
    for s in range(shared):
        x = x_ref[s * n : (s + 1) * n].astype(F32)
        o_ref[:, s * wide : (s + 1) * wide] = jnp.sum(x, axis=0).astype(BF16)


def body(hidden, w_query, w_output, cache, fresh, cache_lengths, new_lengths):
    rows, feat = hidden.shape
    n = lax.axis_size("tensor")
    cores = lax.axis_size("section")
    own = w_query.shape[1] // HD
    wide = w_output.shape[1] // n
    usual = own == GROUP
    o_shared = cores if usual and SPLIT_OUTPUT else 1
    w_query = pltpu.with_memory_space_constraint(w_query, pltpu.VMEM)
    w_output = pltpu.with_memory_space_constraint(w_output, pltpu.VMEM)
    cache = pltpu.with_memory_space_constraint(cache, pltpu.VMEM)
    fresh = pltpu.with_memory_space_constraint(fresh, pltpu.VMEM)

    scratch = [pltpu.VMEM((rows * own, HD), F32)]
    if n == 8:
        mine = call(copy_kernel, (rows, feat), BF16, hidden, flops=LONG)
        near = flip(mine, 1)
        pair = call(stack_kernel, (2, rows, feat), BF16, flip(mine, 0), near)
        acc = call(first_kernel, (rows, own * HD), F32, flip(pair, 0), w_query, flops=FIRST)
        got = [flip(pair, apart) for apart in ORDER]
        for apart, x in zip(ORDER[:2], got):
            step = functools.partial(next_kernel, apart)
            acc = call(step, (rows, own * HD), F32, x, w_query, acc, flops=10**10 if apart == ORDER[0] else 0)
        step = functools.partial(last_kernel, ORDER[2])
        q = call(step, (rows * own, HD), BF16, got[2], w_query, acc, scratch=scratch)
    else:
        x = call(spread_kernel, (n, rows, feat), BF16, hidden, flops=LONG)
        x = exchange(x, 1)
        q = call(query_kernel, (n, rows * own, HD), BF16, x, w_query, scratch=scratch)
    if n == 8:
        near = flip(q, 1)
        pair = call(order_kernel, (2, rows * own, HD), BF16, flip(q, 0), near)

        def attend(apart):
            return call(
                functools.partial(pair_attend_kernel, apart),
                (2, rows * GROUP + STATS, HD),
                BF16,
                cache_lengths,
                new_lengths,
                flip(pair, apart),
                cache,
                fresh,
                specs=[SMEM] * 2 + [VMEM] * 3,
                flops=PIECE,
            )

        parts = [flip(attend(apart), apart) for apart in (0,) + MIDDLE]
        shape = (4, rows * GROUP + STATS, HD)
        mine, far = call(part_kernel, [shape] * 2, [BF16, BF16], *parts, flops=ADD)
        parts = flip(mine, 0), flip(far, 1)
    else:
        q = exchange(q, 1)
        if not usual:
            q = q.reshape(KVH, GROUP, rows, HD).transpose(0, 2, 1, 3).reshape(KVH, rows * GROUP, HD)
        part = call(
            attend_kernel,
            (o_shared * KVH, rows * GROUP + STATS, HD),
            BF16,
            cache_lengths,
            new_lengths,
            q,
            cache,
            fresh,
            flops=ATTEND,
            specs=[SMEM] * 2 + [VMEM] * 3,
        )
        if not usual:
            stats = jnp.broadcast_to(part[:1, rows * GROUP :], (n, STATS, HD))
            part = part[:, : rows * GROUP].reshape(KVH, rows, GROUP, HD).transpose(0, 2, 1, 3)
            part = jnp.concatenate([part.reshape(n, rows * own, HD), stats], axis=1)
        part = exchange(part, o_shared)
    scratch = [pltpu.VMEM((rows * own, HD), F32)]
    if n == 8:
        two = (2, rows, wide)
        step = functools.partial(begin_kernel, BACK[0])
        shapes = [two, (rows, own * HD)]
        out, context = call(
            step, shapes, [BF16, BF16], *parts, w_output, scratch=scratch, flops=PIECE
        )
        got = [flip(out, BACK[0])]
        for apart in BACK[1:]:
            step = functools.partial(terms_kernel, apart)
            out = call(step, two, BF16, context, w_output, flops=PIECE)
            got.append(flip(out, apart))
        own_terms = call(
            functools.partial(terms_kernel, 0), two, BF16, context, w_output, flops=PIECE
        )
        out = call(widen_kernel, two, F32, got[0], flops=ADD)
        out = call(merge_kernel, two, F32, out, got[1], flops=ADD)
        out = call(merge_kernel, two, F32, out, got[2], flops=ADD)
        mine, far = call(
            finish_kernel, [(rows, wide)] * 2, [F32, BF16], out, flip(own_terms, 0), flops=ADD
        )
        return call(add_kernel, (rows, wide), BF16, flip(mine, 0), flip(far, 1))
    terms = call(
        functools.partial(project_kernel, o_shared, own),
        (o_shared * n, rows, wide // o_shared),
        BF16,
        part,
        w_output,
        scratch=scratch,
    )
    terms = exchange(terms, o_shared)
    return call(sum_kernel, (rows, wide), BF16, terms)


def solution(mesh):
    return jax.shard_map(
        body,
        mesh=mesh,
        in_specs=(
            P(("groups", "section"), "tensor"),
            P(None, "tensor"),
            P("tensor", None),
            P(("groups", "section"), "tensor", None),
            P(("groups", "section"), "tensor", None),
            P(("groups", "section")),
            P(("groups", "section")),
        ),
        out_specs=P(("groups", "section"), "tensor"),
        check_vma=False,
    )
```

```python
import functools

import jax
import jax.numpy as jnp
from jax import lax
from jax.experimental import pallas as pl
from jax.experimental.pallas import tpu as pltpu
from jax.sharding import PartitionSpec as P

KVH = 8
HD = 128
GROUP = 8
HEADS = KVH * GROUP
STATS = 8
F32 = jnp.float32
BF16 = jnp.bfloat16
VMEM = pl.BlockSpec(memory_space=pltpu.VMEM)
SMEM = pl.BlockSpec(memory_space=pltpu.SMEM)
BOTH = ("section", "tensor")
SPLIT_OUTPUT = False
ORDER = (4, 6, 2)
MIDDLE = (4, 6, 2)
BACK = (4, 6, 2)
ADD = 23000000
PIECE = 11500000
LONG = 10**12
FIRST = 0
ATTEND = 0


def exchange(x, shared):
    return lax.all_to_all(x, BOTH if shared > 1 else "tensor", 0, 0, tiled=True)


def dot(a, b):
    return jnp.dot(a, b, preferred_element_type=F32)


def swap(x, apart):
    n = lax.axis_size("tensor")
    return lax.ppermute(x, "tensor", [(i, i ^ apart) for i in range(n)])


def flip(x, apart):
    n = lax.axis_size("tensor")
    return lax.ppermute(x, BOTH, [(i, ((i // n) ^ 1) * n + (i % n ^ apart)) for i in range(2 * n)])


def call(kernel, shape, dtype, *args, specs=None, scratch=(), flops=0):
    if isinstance(shape, list):
        out = [jax.ShapeDtypeStruct(*x) for x in zip(shape, dtype)]
        outs = [VMEM] * len(out)
    else:
        out, outs = jax.ShapeDtypeStruct(shape, dtype), VMEM
    return pl.pallas_call(
        kernel,
        in_specs=specs or [VMEM] * len(args),
        out_specs=outs,
        out_shape=out,
        scratch_shapes=scratch,
        cost_estimate=pl.CostEstimate(flops=flops, bytes_accessed=0, transcendentals=0),
        compiler_params=pltpu.CompilerParams(vmem_limit_bytes=8 << 20),
    )(*args)


def spread_kernel(x_ref, o_ref):
    o_ref[...] = jnp.broadcast_to(x_ref[...][None], o_ref.shape)


def copy_kernel(x_ref, o_ref):
    o_ref[...] = x_ref[...]


def stack_kernel(x_ref, y_ref, o_ref):
    o_ref[0] = x_ref[...]
    o_ref[1] = y_ref[...]


def write_queries(acc, o_ref, heads_ref):
    rows = acc.shape[0]
    own = acc.shape[1] // HD
    for h in range(own):
        heads_ref[pl.ds(h, rows, stride=own), :] = acc[:, h * HD : (h + 1) * HD]
    q = heads_ref[...].astype(BF16)
    o_ref[...] = q if len(o_ref.shape) == 2 else jnp.broadcast_to(q[None], o_ref.shape)


def query_kernel(all_ref, w_ref, o_ref, heads_ref):
    n, rows, feat = all_ref.shape
    acc = jnp.zeros((rows, w_ref.shape[1]), F32)
    for t in range(n):
        acc += dot(all_ref[t], w_ref[t * feat : (t + 1) * feat, :])
    write_queries(acc, o_ref, heads_ref)


def pair_product(apart, x_ref, w_ref):
    feat = x_ref.shape[2]
    me = lax.axis_index("tensor")
    acc = jnp.zeros((x_ref.shape[1], w_ref.shape[1]), F32)
    for i in range(2):
        at = pl.multiple_of((me ^ (apart + i)) * feat, feat)
        acc += dot(x_ref[i], w_ref[pl.ds(at, feat), :])
    return acc


def first_kernel(cc, fc, clen_ref, nlen_ref, x_ref, w_ref, acc_ref, limit_ref):
    limit_kernel(cc, fc, clen_ref, nlen_ref, limit_ref)
    acc_ref[...] = pair_product(0, x_ref, w_ref)


def next_kernel(apart, x_ref, w_ref, old_ref, acc_ref):
    acc_ref[...] = old_ref[...] + pair_product(apart, x_ref, w_ref)


def last_kernel(apart, x_ref, w_ref, old_ref, o_ref, heads_ref):
    write_queries(old_ref[...] + pair_product(apart, x_ref, w_ref), o_ref, heads_ref)


def attend_kernel(clen_ref, nlen_ref, q_ref, cache_ref, fresh_ref, o_ref):
    rows, cc, width = cache_ref.shape
    width = width // 2
    fc = fresh_ref.shape[1]
    shares = q_ref.shape[0] // KVH
    part = GROUP // shares
    place = lax.axis_index("tensor")
    lane = lax.broadcasted_iota(jnp.int32, (HD, 2 * HEADS), 1)

    def logits(ref, r, wide, start, length_ref):
        s = [
            dot(ref[r + i, :, 0:width], wide[i])
            for i in range(2)
        ]
        s = s[0] + s[1]
        second = lax.broadcasted_iota(jnp.int32, s.shape, 1) >= HEADS
        length = jnp.where(second, length_ref[r + 1], length_ref[r])
        valid = start + lax.broadcasted_iota(jnp.int32, s.shape, 0) < length
        return jnp.where(valid, s * HD**-0.5, -1e30), valid

    scores = []
    for r in range(0, rows, 2):
        at = slice(r * part, (r + 2) * part)
        both = [
            q_ref[s * KVH + g, at, :].astype(F32) for g in range(KVH) for s in range(shares)
        ]
        q = [x[i * part : (i + 1) * part] for i in range(2) for x in both]
        q = jnp.concatenate(q, axis=0).T
        wide = []
        for i in range(2):
            blocks = []
            for g in range(KVH):
                first = i * HEADS + g * GROUP
                blocks.append(jnp.where((lane >= first) & (lane < first + GROUP), q, 0.0))
            wide.append(jnp.concatenate(blocks, axis=0).astype(BF16))
        scores.append(
            (
                logits(cache_ref, r, wide, place * cc, clen_ref),
                logits(fresh_ref, r, wide, place * fc, nlen_ref),
            )
        )
    stats, weights = [], []
    for (sc, okc), (sf, okf) in scores:
        top = jnp.maximum(
            jnp.max(sc, axis=0, keepdims=True), jnp.max(sf, axis=0, keepdims=True)
        )
        wc = jnp.where(okc, jnp.exp(sc - top), 0.0)
        wf = jnp.where(okf, jnp.exp(sf - top), 0.0)
        total = jnp.sum(wc, axis=0, keepdims=True) + jnp.sum(wf, axis=0, keepdims=True)
        some = total > 0.0
        total = jnp.where(some, total, 1.0)
        inverse = 1.0 / total
        weights.append(((wc * inverse).T.astype(BF16), (wf * inverse).T.astype(BF16)))
        rest = jnp.where(some, top + jnp.log(total), -1e30)
        for _ in range(3):
            piece = rest.astype(BF16).astype(F32)
            stats.append(piece)
            rest = rest - piece
        stats.append(jnp.zeros_like(rest))
    for two, (pc, pf) in enumerate(weights):
        for pair in range(KVH // 2):
            vals = slice(width + 2 * pair * HD, width + 2 * (pair + 1) * HD)
            nums = []
            for i in range(2):
                at = slice(i * HEADS + 2 * pair * GROUP, i * HEADS + 2 * (pair + 1) * GROUP)
                nums.append(
                    dot(pc[at], cache_ref[2 * two + i, :, vals])
                    + dot(pf[at], fresh_ref[2 * two + i, :, vals])
                )
            at = slice(two * 2 * GROUP, (two + 1) * 2 * GROUP)
            for j in range(2):
                num = [x[j * GROUP : (j + 1) * GROUP, j * HD : (j + 1) * HD] for x in nums]
                num = jnp.concatenate(num, axis=0).astype(BF16)
                for d in range(2 * pair + j, o_ref.shape[0], KVH):
                    o_ref[d, at, :] = num
    stats = jnp.concatenate(stats, axis=0).astype(BF16)
    for d in range(o_ref.shape[0]):
        o_ref[d, rows * GROUP :, :] = stats


def order_kernel(x_ref, y_ref, o_ref):
    odd = lax.axis_index("tensor") % 2
    o_ref[odd] = x_ref[...]
    o_ref[1 - odd] = y_ref[...]


def limit_kernel(cc, fc, clen_ref, nlen_ref, o_ref):
    place = lax.axis_index("tensor")
    request = lax.broadcasted_iota(jnp.int32, (1, o_ref.shape[1]), 1) // (2 * GROUP)
    for i, (ref, count) in enumerate(((clen_ref, cc), (nlen_ref, fc))):
        limit = jnp.full(request.shape, ref[0] - place * count, jnp.int32)
        for r in range(1, ref.shape[0]):
            limit = jnp.where(request == r, ref[r] - place * count, limit)
        o_ref[i : i + 1, :] = limit


def pair_attend_kernel(apart, limit_ref, q_ref, cache_ref, fresh_ref, o_ref):
    rows, _, width = cache_ref.shape
    width = width // 2
    both = 2 * GROUP
    place = lax.axis_index("tensor")
    at = (place ^ apart) // 2 * (2 * HD)
    keys = pl.ds(pl.multiple_of(at, 2 * HD), 2 * HD)
    vals = pl.ds(pl.multiple_of(width + at, 2 * HD), 2 * HD)
    lane = lax.broadcasted_iota(jnp.int32, (HD, rows * both), 1)
    heads = [q_ref[i].astype(F32) for i in range(2)]
    q = [heads[i][r * GROUP : (r + 1) * GROUP] for r in range(rows) for i in range(2)]
    q = jnp.concatenate(q, axis=0).T
    wide = []
    for r in range(rows):
        blocks = []
        for i in range(2):
            first = r * both + i * GROUP
            blocks.append(jnp.where((lane >= first) & (lane < first + GROUP), q, 0.0))
        wide.append(jnp.concatenate(blocks, axis=0).astype(BF16))

    def logits(ref, limit):
        s = functools.reduce(jnp.add, [dot(ref[r, :, keys], wide[r]) for r in range(rows)])
        valid = lax.broadcasted_iota(jnp.int32, s.shape, 0) < limit
        return jnp.where(valid, s * HD**-0.5, -1e30), valid

    sc, okc = logits(cache_ref, limit_ref[0:1, :])
    sf, okf = logits(fresh_ref, limit_ref[1:2, :])
    top = jnp.maximum(jnp.max(sc, axis=0, keepdims=True), jnp.max(sf, axis=0, keepdims=True))
    wc = jnp.where(okc, jnp.exp(sc - top), 0.0)
    wf = jnp.where(okf, jnp.exp(sf - top), 0.0)
    total = jnp.sum(wc, axis=0, keepdims=True) + jnp.sum(wf, axis=0, keepdims=True)
    some = total > 0.0
    total = jnp.where(some, total, 1.0)
    inverse = 1.0 / total
    pc = (wc * inverse).T.astype(BF16)
    pf = (wf * inverse).T.astype(BF16)
    nums = []
    for r in range(rows):
        mine = slice(r * both, (r + 1) * both)
        nums.append(dot(pc[mine], cache_ref[r, :, vals]) + dot(pf[mine], fresh_ref[r, :, vals]))
    for i in range(2):
        for r in range(0, rows, 2):
            num = [x[i * GROUP : (i + 1) * GROUP, i * HD : (i + 1) * HD] for x in nums[r : r + 2]]
            o_ref[i, r * GROUP : (r + 2) * GROUP, :] = jnp.concatenate(num, axis=0).astype(BF16)
    rest = jnp.where(some, top + jnp.log(total), -1e30)
    stats = []
    for _ in range(3):
        piece = rest.astype(BF16).astype(F32)
        stats.append(piece)
        rest = rest - piece
    stats.append(jnp.zeros((STATS - 3, rows * both), F32))
    stats = jnp.concatenate(stats, axis=0)
    stats = jnp.concatenate([stats, jnp.zeros((STATS, HD - rows * both), F32)], axis=1)
    for i in range(2):
        o_ref[i, rows * GROUP :, :] = stats.astype(BF16)


def part_kernel(a_ref, b_ref, c_ref, d_ref, mine_ref, far_ref):
    odd = lax.axis_index("tensor") % 2
    for i, ref in enumerate((a_ref, b_ref, c_ref, d_ref)):
        mine_ref[i] = ref[odd]
        far_ref[i] = ref[1 - odd]


def combine_pair(a_ref, b_ref, heads_ref):
    n = 2 * a_ref.shape[0]
    both = a_ref.shape[1] - STATS
    rows = both // GROUP
    odd = lax.axis_index("tensor") % 2
    line = lax.broadcasted_iota(jnp.int32, (both, HD), 0)
    column = lax.broadcasted_iota(jnp.int32, (both, HD), 1)
    mine = column == (line // GROUP) * 2 * GROUP + odd * GROUP + line % GROUP
    mine = mine.astype(F32).astype(BF16)
    column = lax.broadcasted_iota(jnp.int32, (both, n * STATS), 1)
    parts = [ref.at[i] for ref in (a_ref, b_ref) for i in range(n // 2)]
    stats = [x[both:, :].astype(F32) for x in parts]
    stats = jnp.concatenate(stats, axis=0).astype(BF16)
    pieces = lax.dot_general(mine, stats, (((1,), (1,)), ((), ())), preferred_element_type=F32)
    logs = [
        jnp.sum(jnp.where(column // STATS == t, pieces, 0.0), axis=1, keepdims=True)
        for t in range(n)
    ]
    top = functools.reduce(jnp.maximum, logs)
    scales = [jnp.exp(x - top) for x in logs]
    inverse = 1.0 / functools.reduce(jnp.add, scales)
    heads_ref[...] = functools.reduce(
        jnp.add,
        [x[0:both, :].astype(F32) * (scale * inverse) for x, scale in zip(parts, scales)],
    )
    context = [heads_ref[pl.ds(h, rows, stride=GROUP), :] for h in range(GROUP)]
    return jnp.concatenate(context, axis=1).astype(BF16)


def combine(shared, own, got_ref, heads_ref):
    total, both, _ = got_ref.shape
    both -= STATS
    n = total // shared
    rows = both // own
    me = lax.axis_index("tensor")
    line = lax.broadcasted_iota(jnp.int32, (both, HD), 0)
    column = lax.broadcasted_iota(jnp.int32, (both, HD), 1)
    mine = column == (line // own % 2) * HEADS + me * own + line % own
    mine = mine.astype(F32).astype(BF16)
    line = lax.broadcasted_iota(jnp.int32, (both, n * STATS), 0)
    column = lax.broadcasted_iota(jnp.int32, (both, n * STATS), 1)
    pair = (column % STATS) // (STATS // 2) == line // own // 2
    context = []
    for s in range(shared):
        stats = [got_ref[s * n + t, both:, :].astype(F32) for t in range(n)]
        stats = jnp.concatenate(stats, axis=0).astype(BF16)
        pieces = lax.dot_general(
            mine, stats, (((1,), (1,)), ((), ())), preferred_element_type=F32
        )
        pieces = jnp.where(pair, pieces, 0.0)
        logs = [
            jnp.sum(jnp.where(column // STATS == t, pieces, 0.0), axis=1, keepdims=True)
            for t in range(n)
        ]
        top = functools.reduce(jnp.maximum, logs)
        scales = [jnp.exp(x - top) for x in logs]
        inverse = 1.0 / functools.reduce(jnp.add, scales)
        heads_ref[...] = functools.reduce(
            jnp.add,
            [
                got_ref[s * n + t, 0:both, :].astype(F32) * (scales[t] * inverse)
                for t in range(n)
            ],
        )
        context.append(
            jnp.concatenate(
                [heads_ref[pl.ds(h, rows, stride=own), :] for h in range(own)], axis=1
            )
        )
    return jnp.concatenate(context, axis=0).astype(BF16)


def project_kernel(shared, own, got_ref, w_ref, o_ref, heads_ref):
    context = combine(shared, own, got_ref, heads_ref)
    total, rows, wide = o_ref.shape
    n = total // shared
    offset = 0
    if shared > 1:
        offset = lax.axis_index("section") * wide
    for t in range(n):
        at = t * shared * wide + offset
        if shared > 1:
            at = pl.multiple_of(at, HD)
        terms = dot(context, w_ref[:, pl.ds(at, wide)])
        for s in range(shared):
            o_ref[s * n + t] = terms[s * rows : (s + 1) * rows].astype(BF16)


def pair_terms(apart, context, w_ref, o_ref):
    wide = o_ref.shape[2]
    me = lax.axis_index("tensor")
    for i in range(2):
        at = pl.multiple_of((me ^ (apart + i)) * wide, wide)
        o_ref[i] = dot(context, w_ref[:, pl.ds(at, wide)]).astype(o_ref.dtype)


def begin_kernel(apart, a_ref, b_ref, w_ref, o_ref, context_ref, heads_ref):
    context = combine_pair(a_ref, b_ref, heads_ref)
    context_ref[...] = context
    pair_terms(apart, context, w_ref, o_ref)


def terms_kernel(apart, context_ref, w_ref, o_ref):
    pair_terms(apart, context_ref[...], w_ref, o_ref)


def widen_kernel(x_ref, o_ref):
    o_ref[...] = x_ref[...].astype(F32)


def merge_kernel(x_ref, y_ref, o_ref):
    o_ref[...] = x_ref[...].astype(F32) + y_ref[...].astype(F32)


def finish_kernel(x_ref, y_ref, mine_ref, far_ref):
    out = x_ref[...] + y_ref[...].astype(F32)
    mine_ref[...] = out[0]
    far_ref[...] = out[1].astype(BF16)


def add_kernel(x_ref, y_ref, o_ref):
    o_ref[...] = (x_ref[...] + y_ref[...].astype(F32)).astype(BF16)


def sum_kernel(x_ref, o_ref):
    total, _, wide = x_ref.shape
    shared = o_ref.shape[1] // wide
    n = total // shared
    for s in range(shared):
        x = x_ref[s * n : (s + 1) * n].astype(F32)
        o_ref[:, s * wide : (s + 1) * wide] = jnp.sum(x, axis=0).astype(BF16)


def body(hidden, w_query, w_output, cache, fresh, cache_lengths, new_lengths):
    rows, feat = hidden.shape
    n = lax.axis_size("tensor")
    cores = lax.axis_size("section")
    own = w_query.shape[1] // HD
    wide = w_output.shape[1] // n
    usual = own == GROUP
    o_shared = cores if usual and SPLIT_OUTPUT else 1
    w_query = pltpu.with_memory_space_constraint(w_query, pltpu.VMEM)
    w_output = pltpu.with_memory_space_constraint(w_output, pltpu.VMEM)
    cache = pltpu.with_memory_space_constraint(cache, pltpu.VMEM)
    fresh = pltpu.with_memory_space_constraint(fresh, pltpu.VMEM)

    scratch = [pltpu.VMEM((rows * own, HD), F32)]
    if n == 8:
        mine = call(copy_kernel, (rows, feat), BF16, hidden, flops=LONG)
        near = flip(mine, 1)
        pair = call(stack_kernel, (2, rows, feat), BF16, flip(mine, 0), near)
        acc, limits = call(
            functools.partial(first_kernel, cache.shape[1], fresh.shape[1]),
            [(rows, own * HD), (2, rows * 2 * GROUP)],
            [F32, jnp.int32],
            cache_lengths,
            new_lengths,
            flip(pair, 0),
            w_query,
            specs=[SMEM] * 2 + [VMEM] * 2,
            flops=FIRST,
        )
        got = [flip(pair, apart) for apart in ORDER]
        for apart, x in zip(ORDER[:2], got):
            step = functools.partial(next_kernel, apart)
            acc = call(step, (rows, own * HD), F32, x, w_query, acc, flops=10**10 if apart == ORDER[0] else 0)
        step = functools.partial(last_kernel, ORDER[2])
        q = call(step, (rows * own, HD), BF16, got[2], w_query, acc, scratch=scratch)
    else:
        x = call(spread_kernel, (n, rows, feat), BF16, hidden, flops=LONG)
        x = exchange(x, 1)
        q = call(query_kernel, (n, rows * own, HD), BF16, x, w_query, scratch=scratch)
    if n == 8:
        near = flip(q, 1)
        pair = call(order_kernel, (2, rows * own, HD), BF16, flip(q, 0), near)

        def attend(apart):
            return call(
                functools.partial(pair_attend_kernel, apart),
                (2, rows * GROUP + STATS, HD),
                BF16,
                limits,
                flip(pair, apart),
                cache,
                fresh,
                flops=PIECE,
            )

        parts = [flip(attend(apart), apart) for apart in (0,) + MIDDLE]
        shape = (4, rows * GROUP + STATS, HD)
        mine, far = call(part_kernel, [shape] * 2, [BF16, BF16], *parts, flops=ADD)
        parts = flip(mine, 0), flip(far, 1)
    else:
        q = exchange(q, 1)
        if not usual:
            q = q.reshape(KVH, GROUP, rows, HD).transpose(0, 2, 1, 3).reshape(KVH, rows * GROUP, HD)
        part = call(
            attend_kernel,
            (o_shared * KVH, rows * GROUP + STATS, HD),
            BF16,
            cache_lengths,
            new_lengths,
            q,
            cache,
            fresh,
            flops=ATTEND,
            specs=[SMEM] * 2 + [VMEM] * 3,
        )
        if not usual:
            stats = jnp.broadcast_to(part[:1, rows * GROUP :], (n, STATS, HD))
            part = part[:, : rows * GROUP].reshape(KVH, rows, GROUP, HD).transpose(0, 2, 1, 3)
            part = jnp.concatenate([part.reshape(n, rows * own, HD), stats], axis=1)
        part = exchange(part, o_shared)
    scratch = [pltpu.VMEM((rows * own, HD), F32)]
    if n == 8:
        two = (2, rows, wide)
        step = functools.partial(begin_kernel, BACK[0])
        shapes = [two, (rows, own * HD)]
        out, context = call(
            step, shapes, [BF16, BF16], *parts, w_output, scratch=scratch, flops=PIECE
        )
        got = [flip(out, BACK[0])]
        for apart in BACK[1:]:
            step = functools.partial(terms_kernel, apart)
            out = call(step, two, BF16, context, w_output, flops=PIECE)
            got.append(flip(out, apart))
        own_terms = call(
            functools.partial(terms_kernel, 0), two, BF16, context, w_output, flops=PIECE
        )
        out = call(widen_kernel, two, F32, got[0], flops=ADD)
        out = call(merge_kernel, two, F32, out, got[1], flops=ADD)
        out = call(merge_kernel, two, F32, out, got[2], flops=ADD)
        mine, far = call(
            finish_kernel, [(rows, wide)] * 2, [F32, BF16], out, flip(own_terms, 0), flops=ADD
        )
        return call(add_kernel, (rows, wide), BF16, flip(mine, 0), flip(far, 1))
    terms = call(
        functools.partial(project_kernel, o_shared, own),
        (o_shared * n, rows, wide // o_shared),
        BF16,
        part,
        w_output,
        scratch=scratch,
    )
    terms = exchange(terms, o_shared)
    return call(sum_kernel, (rows, wide), BF16, terms)


def solution(mesh):
    return jax.shard_map(
        body,
        mesh=mesh,
        in_specs=(
            P(("groups", "section"), "tensor"),
            P(None, "tensor"),
            P("tensor", None),
            P(("groups", "section"), "tensor", None),
            P(("groups", "section"), "tensor", None),
            P(("groups", "section")),
            P(("groups", "section")),
        ),
        out_specs=P(("groups", "section"), "tensor"),
        check_vma=False,
    )
```

```python
import functools

import jax
import jax.numpy as jnp
from jax import lax
from jax.experimental import pallas as pl
from jax.experimental.pallas import tpu as pltpu
from jax.sharding import PartitionSpec as P

KVH = 8
HD = 128
GROUP = 8
HEADS = KVH * GROUP
STATS = 8
F32 = jnp.float32
BF16 = jnp.bfloat16
VMEM = pl.BlockSpec(memory_space=pltpu.VMEM)
SMEM = pl.BlockSpec(memory_space=pltpu.SMEM)
BOTH = ("section", "tensor")
SPLIT_OUTPUT = False
ORDER = (4, 6, 2)
MIDDLE = (4, 6, 2)
LIMIT = 10**7
BACK = (4, 6, 2)
ADD = 23000000
PIECE = 11500000
LONG = 10**12
FIRST = 0
ATTEND = 0


def exchange(x, shared):
    return lax.all_to_all(x, BOTH if shared > 1 else "tensor", 0, 0, tiled=True)


def dot(a, b):
    return jnp.dot(a, b, preferred_element_type=F32)


def swap(x, apart):
    n = lax.axis_size("tensor")
    return lax.ppermute(x, "tensor", [(i, i ^ apart) for i in range(n)])


def flip(x, apart):
    n = lax.axis_size("tensor")
    return lax.ppermute(x, BOTH, [(i, ((i // n) ^ 1) * n + (i % n ^ apart)) for i in range(2 * n)])


def call(kernel, shape, dtype, *args, specs=None, scratch=(), flops=0):
    if isinstance(shape, list):
        out = [jax.ShapeDtypeStruct(*x) for x in zip(shape, dtype)]
        outs = [VMEM] * len(out)
    else:
        out, outs = jax.ShapeDtypeStruct(shape, dtype), VMEM
    return pl.pallas_call(
        kernel,
        in_specs=specs or [VMEM] * len(args),
        out_specs=outs,
        out_shape=out,
        scratch_shapes=scratch,
        cost_estimate=pl.CostEstimate(flops=flops, bytes_accessed=0, transcendentals=0),
        compiler_params=pltpu.CompilerParams(vmem_limit_bytes=8 << 20),
    )(*args)


def spread_kernel(x_ref, o_ref):
    o_ref[...] = jnp.broadcast_to(x_ref[...][None], o_ref.shape)


def copy_kernel(x_ref, o_ref):
    o_ref[...] = x_ref[...]


def stack_kernel(x_ref, y_ref, _, o_ref):
    o_ref[0] = x_ref[...]
    o_ref[1] = y_ref[...]


def write_queries(acc, o_ref, heads_ref):
    rows = acc.shape[0]
    own = acc.shape[1] // HD
    for h in range(own):
        heads_ref[pl.ds(h, rows, stride=own), :] = acc[:, h * HD : (h + 1) * HD]
    q = heads_ref[...].astype(BF16)
    o_ref[...] = q if len(o_ref.shape) == 2 else jnp.broadcast_to(q[None], o_ref.shape)


def query_kernel(all_ref, w_ref, o_ref, heads_ref):
    n, rows, feat = all_ref.shape
    acc = jnp.zeros((rows, w_ref.shape[1]), F32)
    for t in range(n):
        acc += dot(all_ref[t], w_ref[t * feat : (t + 1) * feat, :])
    write_queries(acc, o_ref, heads_ref)


def pair_product(apart, x_ref, w_ref):
    feat = x_ref.shape[2]
    me = lax.axis_index("tensor")
    acc = jnp.zeros((x_ref.shape[1], w_ref.shape[1]), F32)
    for i in range(2):
        at = pl.multiple_of((me ^ (apart + i)) * feat, feat)
        acc += dot(x_ref[i], w_ref[pl.ds(at, feat), :])
    return acc


def first_kernel(x_ref, w_ref, acc_ref):
    acc_ref[...] = pair_product(0, x_ref, w_ref)


def next_kernel(apart, x_ref, w_ref, old_ref, acc_ref):
    acc_ref[...] = old_ref[...] + pair_product(apart, x_ref, w_ref)


def last_kernel(apart, x_ref, w_ref, old_ref, o_ref, heads_ref):
    write_queries(old_ref[...] + pair_product(apart, x_ref, w_ref), o_ref, heads_ref)


def attend_kernel(clen_ref, nlen_ref, q_ref, cache_ref, fresh_ref, o_ref):
    rows, cc, width = cache_ref.shape
    width = width // 2
    fc = fresh_ref.shape[1]
    shares = q_ref.shape[0] // KVH
    part = GROUP // shares
    place = lax.axis_index("tensor")
    lane = lax.broadcasted_iota(jnp.int32, (HD, 2 * HEADS), 1)

    def logits(ref, r, wide, start, length_ref):
        s = [
            dot(ref[r + i, :, 0:width], wide[i])
            for i in range(2)
        ]
        s = s[0] + s[1]
        second = lax.broadcasted_iota(jnp.int32, s.shape, 1) >= HEADS
        length = jnp.where(second, length_ref[r + 1], length_ref[r])
        valid = start + lax.broadcasted_iota(jnp.int32, s.shape, 0) < length
        return jnp.where(valid, s * HD**-0.5, -1e30), valid

    scores = []
    for r in range(0, rows, 2):
        at = slice(r * part, (r + 2) * part)
        both = [
            q_ref[s * KVH + g, at, :].astype(F32) for g in range(KVH) for s in range(shares)
        ]
        q = [x[i * part : (i + 1) * part] for i in range(2) for x in both]
        q = jnp.concatenate(q, axis=0).T
        wide = []
        for i in range(2):
            blocks = []
            for g in range(KVH):
                first = i * HEADS + g * GROUP
                blocks.append(jnp.where((lane >= first) & (lane < first + GROUP), q, 0.0))
            wide.append(jnp.concatenate(blocks, axis=0).astype(BF16))
        scores.append(
            (
                logits(cache_ref, r, wide, place * cc, clen_ref),
                logits(fresh_ref, r, wide, place * fc, nlen_ref),
            )
        )
    stats, weights = [], []
    for (sc, okc), (sf, okf) in scores:
        top = jnp.maximum(
            jnp.max(sc, axis=0, keepdims=True), jnp.max(sf, axis=0, keepdims=True)
        )
        wc = jnp.where(okc, jnp.exp(sc - top), 0.0)
        wf = jnp.where(okf, jnp.exp(sf - top), 0.0)
        total = jnp.sum(wc, axis=0, keepdims=True) + jnp.sum(wf, axis=0, keepdims=True)
        some = total > 0.0
        total = jnp.where(some, total, 1.0)
        inverse = 1.0 / total
        weights.append(((wc * inverse).T.astype(BF16), (wf * inverse).T.astype(BF16)))
        rest = jnp.where(some, top + jnp.log(total), -1e30)
        for _ in range(3):
            piece = rest.astype(BF16).astype(F32)
            stats.append(piece)
            rest = rest - piece
        stats.append(jnp.zeros_like(rest))
    for two, (pc, pf) in enumerate(weights):
        for pair in range(KVH // 2):
            vals = slice(width + 2 * pair * HD, width + 2 * (pair + 1) * HD)
            nums = []
            for i in range(2):
                at = slice(i * HEADS + 2 * pair * GROUP, i * HEADS + 2 * (pair + 1) * GROUP)
                nums.append(
                    dot(pc[at], cache_ref[2 * two + i, :, vals])
                    + dot(pf[at], fresh_ref[2 * two + i, :, vals])
                )
            at = slice(two * 2 * GROUP, (two + 1) * 2 * GROUP)
            for j in range(2):
                num = [x[j * GROUP : (j + 1) * GROUP, j * HD : (j + 1) * HD] for x in nums]
                num = jnp.concatenate(num, axis=0).astype(BF16)
                for d in range(2 * pair + j, o_ref.shape[0], KVH):
                    o_ref[d, at, :] = num
    stats = jnp.concatenate(stats, axis=0).astype(BF16)
    for d in range(o_ref.shape[0]):
        o_ref[d, rows * GROUP :, :] = stats


def order_kernel(x_ref, y_ref, o_ref):
    odd = lax.axis_index("tensor") % 2
    o_ref[odd] = x_ref[...]
    o_ref[1 - odd] = y_ref[...]


def limit_kernel(cc, fc, clen_ref, nlen_ref, o_ref):
    place = lax.axis_index("tensor")
    request = lax.broadcasted_iota(jnp.int32, (1, o_ref.shape[1]), 1) // (2 * GROUP)
    for i, (ref, count) in enumerate(((clen_ref, cc), (nlen_ref, fc))):
        limit = jnp.full(request.shape, ref[0] - place * count, jnp.int32)
        for r in range(1, ref.shape[0]):
            limit = jnp.where(request == r, ref[r] - place * count, limit)
        o_ref[i : i + 1, :] = limit


def pair_attend_kernel(apart, limit_ref, q_ref, cache_ref, fresh_ref, o_ref):
    rows, _, width = cache_ref.shape
    width = width // 2
    both = 2 * GROUP
    place = lax.axis_index("tensor")
    at = (place ^ apart) // 2 * (2 * HD)
    keys = pl.ds(pl.multiple_of(at, 2 * HD), 2 * HD)
    vals = pl.ds(pl.multiple_of(width + at, 2 * HD), 2 * HD)
    lane = lax.broadcasted_iota(jnp.int32, (HD, rows * both), 1)
    heads = [q_ref[i].astype(F32) for i in range(2)]
    q = [heads[i][r * GROUP : (r + 1) * GROUP] for r in range(rows) for i in range(2)]
    q = jnp.concatenate(q, axis=0).T
    wide = []
    for r in range(rows):
        blocks = []
        for i in range(2):
            first = r * both + i * GROUP
            blocks.append(jnp.where((lane >= first) & (lane < first + GROUP), q, 0.0))
        wide.append(jnp.concatenate(blocks, axis=0).astype(BF16))

    def logits(ref, limit):
        s = functools.reduce(jnp.add, [dot(ref[r, :, keys], wide[r]) for r in range(rows)])
        valid = lax.broadcasted_iota(jnp.int32, s.shape, 0) < limit
        return jnp.where(valid, s * HD**-0.5, -1e30), valid

    sc, okc = logits(cache_ref, limit_ref[0:1, :])
    sf, okf = logits(fresh_ref, limit_ref[1:2, :])
    top = jnp.maximum(jnp.max(sc, axis=0, keepdims=True), jnp.max(sf, axis=0, keepdims=True))
    wc = jnp.where(okc, jnp.exp(sc - top), 0.0)
    wf = jnp.where(okf, jnp.exp(sf - top), 0.0)
    total = jnp.sum(wc, axis=0, keepdims=True) + jnp.sum(wf, axis=0, keepdims=True)
    some = total > 0.0
    total = jnp.where(some, total, 1.0)
    inverse = 1.0 / total
    pc = (wc * inverse).T.astype(BF16)
    pf = (wf * inverse).T.astype(BF16)
    nums = []
    for r in range(rows):
        mine = slice(r * both, (r + 1) * both)
        nums.append(dot(pc[mine], cache_ref[r, :, vals]) + dot(pf[mine], fresh_ref[r, :, vals]))
    for i in range(2):
        for r in range(0, rows, 2):
            num = [x[i * GROUP : (i + 1) * GROUP, i * HD : (i + 1) * HD] for x in nums[r : r + 2]]
            o_ref[i, r * GROUP : (r + 2) * GROUP, :] = jnp.concatenate(num, axis=0).astype(BF16)
    rest = jnp.where(some, top + jnp.log(total), -1e30)
    stats = []
    for _ in range(3):
        piece = rest.astype(BF16).astype(F32)
        stats.append(piece)
        rest = rest - piece
    stats.append(jnp.zeros((STATS - 3, rows * both), F32))
    stats = jnp.concatenate(stats, axis=0)
    stats = jnp.concatenate([stats, jnp.zeros((STATS, HD - rows * both), F32)], axis=1)
    for i in range(2):
        o_ref[i, rows * GROUP :, :] = stats.astype(BF16)


def part_kernel(a_ref, b_ref, c_ref, d_ref, mine_ref, far_ref):
    odd = lax.axis_index("tensor") % 2
    for i, ref in enumerate((a_ref, b_ref, c_ref, d_ref)):
        mine_ref[i] = ref[odd]
        far_ref[i] = ref[1 - odd]


def combine_pair(a_ref, b_ref, heads_ref):
    n = 2 * a_ref.shape[0]
    both = a_ref.shape[1] - STATS
    rows = both // GROUP
    odd = lax.axis_index("tensor") % 2
    line = lax.broadcasted_iota(jnp.int32, (both, HD), 0)
    column = lax.broadcasted_iota(jnp.int32, (both, HD), 1)
    mine = column == (line // GROUP) * 2 * GROUP + odd * GROUP + line % GROUP
    mine = mine.astype(F32).astype(BF16)
    column = lax.broadcasted_iota(jnp.int32, (both, n * STATS), 1)
    parts = [ref.at[i] for ref in (a_ref, b_ref) for i in range(n // 2)]
    stats = [x[both:, :].astype(F32) for x in parts]
    stats = jnp.concatenate(stats, axis=0).astype(BF16)
    pieces = lax.dot_general(mine, stats, (((1,), (1,)), ((), ())), preferred_element_type=F32)
    logs = [
        jnp.sum(jnp.where(column // STATS == t, pieces, 0.0), axis=1, keepdims=True)
        for t in range(n)
    ]
    top = functools.reduce(jnp.maximum, logs)
    scales = [jnp.exp(x - top) for x in logs]
    inverse = 1.0 / functools.reduce(jnp.add, scales)
    heads_ref[...] = functools.reduce(
        jnp.add,
        [x[0:both, :].astype(F32) * (scale * inverse) for x, scale in zip(parts, scales)],
    )
    context = [heads_ref[pl.ds(h, rows, stride=GROUP), :] for h in range(GROUP)]
    return jnp.concatenate(context, axis=1).astype(BF16)


def combine(shared, own, got_ref, heads_ref):
    total, both, _ = got_ref.shape
    both -= STATS
    n = total // shared
    rows = both // own
    me = lax.axis_index("tensor")
    line = lax.broadcasted_iota(jnp.int32, (both, HD), 0)
    column = lax.broadcasted_iota(jnp.int32, (both, HD), 1)
    mine = column == (line // own % 2) * HEADS + me * own + line % own
    mine = mine.astype(F32).astype(BF16)
    line = lax.broadcasted_iota(jnp.int32, (both, n * STATS), 0)
    column = lax.broadcasted_iota(jnp.int32, (both, n * STATS), 1)
    pair = (column % STATS) // (STATS // 2) == line // own // 2
    context = []
    for s in range(shared):
        stats = [got_ref[s * n + t, both:, :].astype(F32) for t in range(n)]
        stats = jnp.concatenate(stats, axis=0).astype(BF16)
        pieces = lax.dot_general(
            mine, stats, (((1,), (1,)), ((), ())), preferred_element_type=F32
        )
        pieces = jnp.where(pair, pieces, 0.0)
        logs = [
            jnp.sum(jnp.where(column // STATS == t, pieces, 0.0), axis=1, keepdims=True)
            for t in range(n)
        ]
        top = functools.reduce(jnp.maximum, logs)
        scales = [jnp.exp(x - top) for x in logs]
        inverse = 1.0 / functools.reduce(jnp.add, scales)
        heads_ref[...] = functools.reduce(
            jnp.add,
            [
                got_ref[s * n + t, 0:both, :].astype(F32) * (scales[t] * inverse)
                for t in range(n)
            ],
        )
        context.append(
            jnp.concatenate(
                [heads_ref[pl.ds(h, rows, stride=own), :] for h in range(own)], axis=1
            )
        )
    return jnp.concatenate(context, axis=0).astype(BF16)


def project_kernel(shared, own, got_ref, w_ref, o_ref, heads_ref):
    context = combine(shared, own, got_ref, heads_ref)
    total, rows, wide = o_ref.shape
    n = total // shared
    offset = 0
    if shared > 1:
        offset = lax.axis_index("section") * wide
    for t in range(n):
        at = t * shared * wide + offset
        if shared > 1:
            at = pl.multiple_of(at, HD)
        terms = dot(context, w_ref[:, pl.ds(at, wide)])
        for s in range(shared):
            o_ref[s * n + t] = terms[s * rows : (s + 1) * rows].astype(BF16)


def pair_terms(apart, context, w_ref, o_ref):
    wide = o_ref.shape[2]
    me = lax.axis_index("tensor")
    for i in range(2):
        at = pl.multiple_of((me ^ (apart + i)) * wide, wide)
        o_ref[i] = dot(context, w_ref[:, pl.ds(at, wide)]).astype(o_ref.dtype)


def begin_kernel(apart, a_ref, b_ref, w_ref, o_ref, context_ref, heads_ref):
    context = combine_pair(a_ref, b_ref, heads_ref)
    context_ref[...] = context
    pair_terms(apart, context, w_ref, o_ref)


def terms_kernel(apart, context_ref, w_ref, o_ref):
    pair_terms(apart, context_ref[...], w_ref, o_ref)


def widen_kernel(x_ref, o_ref):
    o_ref[...] = x_ref[...].astype(F32)


def merge_kernel(x_ref, y_ref, o_ref):
    o_ref[...] = x_ref[...].astype(F32) + y_ref[...].astype(F32)


def finish_kernel(x_ref, y_ref, mine_ref, far_ref):
    out = x_ref[...] + y_ref[...].astype(F32)
    mine_ref[...] = out[0]
    far_ref[...] = out[1].astype(BF16)


def add_kernel(x_ref, y_ref, o_ref):
    o_ref[...] = (x_ref[...] + y_ref[...].astype(F32)).astype(BF16)


def sum_kernel(x_ref, o_ref):
    total, _, wide = x_ref.shape
    shared = o_ref.shape[1] // wide
    n = total // shared
    for s in range(shared):
        x = x_ref[s * n : (s + 1) * n].astype(F32)
        o_ref[:, s * wide : (s + 1) * wide] = jnp.sum(x, axis=0).astype(BF16)


def body(hidden, w_query, w_output, cache, fresh, cache_lengths, new_lengths):
    rows, feat = hidden.shape
    n = lax.axis_size("tensor")
    cores = lax.axis_size("section")
    own = w_query.shape[1] // HD
    wide = w_output.shape[1] // n
    usual = own == GROUP
    o_shared = cores if usual and SPLIT_OUTPUT else 1
    w_query = pltpu.with_memory_space_constraint(w_query, pltpu.VMEM)
    w_output = pltpu.with_memory_space_constraint(w_output, pltpu.VMEM)
    cache = pltpu.with_memory_space_constraint(cache, pltpu.VMEM)
    fresh = pltpu.with_memory_space_constraint(fresh, pltpu.VMEM)

    scratch = [pltpu.VMEM((rows * own, HD), F32)]
    if n == 8:
        mine = call(copy_kernel, (rows, feat), BF16, hidden, flops=LONG)
        near = flip(mine, 1)
        limits = call(
            functools.partial(limit_kernel, cache.shape[1], fresh.shape[1]),
            (2, rows * 2 * GROUP),
            jnp.int32,
            cache_lengths,
            new_lengths,
            specs=[SMEM] * 2,
            flops=LIMIT,
        )
        pair = call(stack_kernel, (2, rows, feat), BF16, flip(mine, 0), near, limits)
        acc = call(first_kernel, (rows, own * HD), F32, flip(pair, 0), w_query, flops=FIRST)
        got = [flip(pair, apart) for apart in ORDER]
        for apart, x in zip(ORDER[:2], got):
            step = functools.partial(next_kernel, apart)
            acc = call(step, (rows, own * HD), F32, x, w_query, acc, flops=10**10 if apart == ORDER[0] else 0)
        step = functools.partial(last_kernel, ORDER[2])
        q = call(step, (rows * own, HD), BF16, got[2], w_query, acc, scratch=scratch)
    else:
        x = call(spread_kernel, (n, rows, feat), BF16, hidden, flops=LONG)
        x = exchange(x, 1)
        q = call(query_kernel, (n, rows * own, HD), BF16, x, w_query, scratch=scratch)
    if n == 8:
        near = flip(q, 1)
        pair = call(order_kernel, (2, rows * own, HD), BF16, flip(q, 0), near)

        def attend(apart):
            return call(
                functools.partial(pair_attend_kernel, apart),
                (2, rows * GROUP + STATS, HD),
                BF16,
                limits,
                flip(pair, apart),
                cache,
                fresh,
                flops=PIECE,
            )

        parts = [flip(attend(apart), apart) for apart in MIDDLE + (0,)]
        shape = (4, rows * GROUP + STATS, HD)
        mine, far = call(part_kernel, [shape] * 2, [BF16, BF16], *parts, flops=ADD)
        parts = flip(mine, 0), flip(far, 1)
    else:
        q = exchange(q, 1)
        if not usual:
            q = q.reshape(KVH, GROUP, rows, HD).transpose(0, 2, 1, 3).reshape(KVH, rows * GROUP, HD)
        part = call(
            attend_kernel,
            (o_shared * KVH, rows * GROUP + STATS, HD),
            BF16,
            cache_lengths,
            new_lengths,
            q,
            cache,
            fresh,
            flops=ATTEND,
            specs=[SMEM] * 2 + [VMEM] * 3,
        )
        if not usual:
            stats = jnp.broadcast_to(part[:1, rows * GROUP :], (n, STATS, HD))
            part = part[:, : rows * GROUP].reshape(KVH, rows, GROUP, HD).transpose(0, 2, 1, 3)
            part = jnp.concatenate([part.reshape(n, rows * own, HD), stats], axis=1)
        part = exchange(part, o_shared)
    scratch = [pltpu.VMEM((rows * own, HD), F32)]
    if n == 8:
        two = (2, rows, wide)
        step = functools.partial(begin_kernel, BACK[0])
        shapes = [two, (rows, own * HD)]
        out, context = call(
            step, shapes, [BF16, BF16], *parts, w_output, scratch=scratch, flops=PIECE
        )
        got = [flip(out, BACK[0])]
        for apart in BACK[1:]:
            step = functools.partial(terms_kernel, apart)
            out = call(step, two, BF16, context, w_output, flops=PIECE)
            got.append(flip(out, apart))
        own_terms = call(
            functools.partial(terms_kernel, 0), two, BF16, context, w_output, flops=PIECE
        )
        out = call(widen_kernel, two, F32, got[0], flops=ADD)
        out = call(merge_kernel, two, F32, out, got[1], flops=ADD)
        out = call(merge_kernel, two, F32, out, got[2], flops=ADD)
        mine, far = call(
            finish_kernel, [(rows, wide)] * 2, [F32, BF16], out, flip(own_terms, 0), flops=ADD
        )
        return call(add_kernel, (rows, wide), BF16, flip(mine, 0), flip(far, 1))
    terms = call(
        functools.partial(project_kernel, o_shared, own),
        (o_shared * n, rows, wide // o_shared),
        BF16,
        part,
        w_output,
        scratch=scratch,
    )
    terms = exchange(terms, o_shared)
    return call(sum_kernel, (rows, wide), BF16, terms)


def solution(mesh):
    return jax.shard_map(
        body,
        mesh=mesh,
        in_specs=(
            P(("groups", "section"), "tensor"),
            P(None, "tensor"),
            P("tensor", None),
            P(("groups", "section"), "tensor", None),
            P(("groups", "section"), "tensor", None),
            P(("groups", "section")),
            P(("groups", "section")),
        ),
        out_specs=P(("groups", "section"), "tensor"),
        check_vma=False,
    )
```

```python
import functools

import jax
import jax.numpy as jnp
from jax import lax
from jax.experimental import pallas as pl
from jax.experimental.pallas import tpu as pltpu
from jax.sharding import PartitionSpec as P

KVH = 8
HD = 128
GROUP = 8
HEADS = KVH * GROUP
STATS = 8
F32 = jnp.float32
BF16 = jnp.bfloat16
VMEM = pl.BlockSpec(memory_space=pltpu.VMEM)
SMEM = pl.BlockSpec(memory_space=pltpu.SMEM)
BOTH = ("section", "tensor")
SPLIT_OUTPUT = False
ORDER = (4, 6, 2)
MIDDLE = (2, 6, 4)
LIMIT = 10**7
BACK = (4, 6, 2)
ADD = 23000000
PIECE = 11500000
LONG = 10**12
FIRST = 0
ATTEND = 0


def exchange(x, shared):
    return lax.all_to_all(x, BOTH if shared > 1 else "tensor", 0, 0, tiled=True)


def dot(a, b):
    return jnp.dot(a, b, preferred_element_type=F32)


def swap(x, apart):
    n = lax.axis_size("tensor")
    return lax.ppermute(x, "tensor", [(i, i ^ apart) for i in range(n)])


def flip(x, apart):
    n = lax.axis_size("tensor")
    return lax.ppermute(x, BOTH, [(i, ((i // n) ^ 1) * n + (i % n ^ apart)) for i in range(2 * n)])


def call(kernel, shape, dtype, *args, specs=None, scratch=(), flops=0):
    if isinstance(shape, list):
        out = [jax.ShapeDtypeStruct(*x) for x in zip(shape, dtype)]
        outs = [VMEM] * len(out)
    else:
        out, outs = jax.ShapeDtypeStruct(shape, dtype), VMEM
    return pl.pallas_call(
        kernel,
        in_specs=specs or [VMEM] * len(args),
        out_specs=outs,
        out_shape=out,
        scratch_shapes=scratch,
        cost_estimate=pl.CostEstimate(flops=flops, bytes_accessed=0, transcendentals=0),
        compiler_params=pltpu.CompilerParams(vmem_limit_bytes=8 << 20),
    )(*args)


def spread_kernel(x_ref, o_ref):
    o_ref[...] = jnp.broadcast_to(x_ref[...][None], o_ref.shape)


def copy_kernel(x_ref, o_ref):
    o_ref[...] = x_ref[...]


def stack_kernel(x_ref, y_ref, _, o_ref):
    o_ref[0] = x_ref[...]
    o_ref[1] = y_ref[...]


def write_queries(acc, o_ref, heads_ref):
    rows = acc.shape[0]
    own = acc.shape[1] // HD
    for h in range(own):
        heads_ref[pl.ds(h, rows, stride=own), :] = acc[:, h * HD : (h + 1) * HD]
    q = heads_ref[...].astype(BF16)
    o_ref[...] = q if len(o_ref.shape) == 2 else jnp.broadcast_to(q[None], o_ref.shape)


def query_kernel(all_ref, w_ref, o_ref, heads_ref):
    n, rows, feat = all_ref.shape
    acc = jnp.zeros((rows, w_ref.shape[1]), F32)
    for t in range(n):
        acc += dot(all_ref[t], w_ref[t * feat : (t + 1) * feat, :])
    write_queries(acc, o_ref, heads_ref)


def pair_product(apart, x_ref, w_ref):
    feat = x_ref.shape[2]
    me = lax.axis_index("tensor")
    acc = jnp.zeros((x_ref.shape[1], w_ref.shape[1]), F32)
    for i in range(2):
        at = pl.multiple_of((me ^ (apart + i)) * feat, feat)
        acc += dot(x_ref[i], w_ref[pl.ds(at, feat), :])
    return acc


def first_kernel(x_ref, w_ref, acc_ref):
    acc_ref[...] = pair_product(0, x_ref, w_ref)


def next_kernel(apart, x_ref, w_ref, old_ref, acc_ref):
    acc_ref[...] = old_ref[...] + pair_product(apart, x_ref, w_ref)


def last_kernel(apart, x_ref, w_ref, old_ref, o_ref, heads_ref):
    write_queries(old_ref[...] + pair_product(apart, x_ref, w_ref), o_ref, heads_ref)


def attend_kernel(clen_ref, nlen_ref, q_ref, cache_ref, fresh_ref, o_ref):
    rows, cc, width = cache_ref.shape
    width = width // 2
    fc = fresh_ref.shape[1]
    shares = q_ref.shape[0] // KVH
    part = GROUP // shares
    place = lax.axis_index("tensor")
    lane = lax.broadcasted_iota(jnp.int32, (HD, 2 * HEADS), 1)

    def logits(ref, r, wide, start, length_ref):
        s = [
            dot(ref[r + i, :, 0:width], wide[i])
            for i in range(2)
        ]
        s = s[0] + s[1]
        second = lax.broadcasted_iota(jnp.int32, s.shape, 1) >= HEADS
        length = jnp.where(second, length_ref[r + 1], length_ref[r])
        valid = start + lax.broadcasted_iota(jnp.int32, s.shape, 0) < length
        return jnp.where(valid, s * HD**-0.5, -1e30), valid

    scores = []
    for r in range(0, rows, 2):
        at = slice(r * part, (r + 2) * part)
        both = [
            q_ref[s * KVH + g, at, :].astype(F32) for g in range(KVH) for s in range(shares)
        ]
        q = [x[i * part : (i + 1) * part] for i in range(2) for x in both]
        q = jnp.concatenate(q, axis=0).T
        wide = []
        for i in range(2):
            blocks = []
            for g in range(KVH):
                first = i * HEADS + g * GROUP
                blocks.append(jnp.where((lane >= first) & (lane < first + GROUP), q, 0.0))
            wide.append(jnp.concatenate(blocks, axis=0).astype(BF16))
        scores.append(
            (
                logits(cache_ref, r, wide, place * cc, clen_ref),
                logits(fresh_ref, r, wide, place * fc, nlen_ref),
            )
        )
    stats, weights = [], []
    for (sc, okc), (sf, okf) in scores:
        top = jnp.maximum(
            jnp.max(sc, axis=0, keepdims=True), jnp.max(sf, axis=0, keepdims=True)
        )
        wc = jnp.where(okc, jnp.exp(sc - top), 0.0)
        wf = jnp.where(okf, jnp.exp(sf - top), 0.0)
        total = jnp.sum(wc, axis=0, keepdims=True) + jnp.sum(wf, axis=0, keepdims=True)
        some = total > 0.0
        total = jnp.where(some, total, 1.0)
        inverse = 1.0 / total
        weights.append(((wc * inverse).T.astype(BF16), (wf * inverse).T.astype(BF16)))
        rest = jnp.where(some, top + jnp.log(total), -1e30)
        for _ in range(3):
            piece = rest.astype(BF16).astype(F32)
            stats.append(piece)
            rest = rest - piece
        stats.append(jnp.zeros_like(rest))
    for two, (pc, pf) in enumerate(weights):
        for pair in range(KVH // 2):
            vals = slice(width + 2 * pair * HD, width + 2 * (pair + 1) * HD)
            nums = []
            for i in range(2):
                at = slice(i * HEADS + 2 * pair * GROUP, i * HEADS + 2 * (pair + 1) * GROUP)
                nums.append(
                    dot(pc[at], cache_ref[2 * two + i, :, vals])
                    + dot(pf[at], fresh_ref[2 * two + i, :, vals])
                )
            at = slice(two * 2 * GROUP, (two + 1) * 2 * GROUP)
            for j in range(2):
                num = [x[j * GROUP : (j + 1) * GROUP, j * HD : (j + 1) * HD] for x in nums]
                num = jnp.concatenate(num, axis=0).astype(BF16)
                for d in range(2 * pair + j, o_ref.shape[0], KVH):
                    o_ref[d, at, :] = num
    stats = jnp.concatenate(stats, axis=0).astype(BF16)
    for d in range(o_ref.shape[0]):
        o_ref[d, rows * GROUP :, :] = stats


def order_kernel(x_ref, y_ref, o_ref):
    odd = lax.axis_index("tensor") % 2
    o_ref[odd] = x_ref[...]
    o_ref[1 - odd] = y_ref[...]


def limit_kernel(cc, fc, clen_ref, nlen_ref, o_ref):
    place = lax.axis_index("tensor")
    request = lax.broadcasted_iota(jnp.int32, (1, o_ref.shape[1]), 1) // (2 * GROUP)
    for i, (ref, count) in enumerate(((clen_ref, cc), (nlen_ref, fc))):
        limit = jnp.full(request.shape, ref[0] - place * count, jnp.int32)
        for r in range(1, ref.shape[0]):
            limit = jnp.where(request == r, ref[r] - place * count, limit)
        o_ref[i : i + 1, :] = limit


def pair_attend_kernel(apart, limit_ref, q_ref, cache_ref, fresh_ref, o_ref):
    rows, _, width = cache_ref.shape
    width = width // 2
    both = 2 * GROUP
    place = lax.axis_index("tensor")
    at = (place ^ apart) // 2 * (2 * HD)
    keys = pl.ds(pl.multiple_of(at, 2 * HD), 2 * HD)
    vals = pl.ds(pl.multiple_of(width + at, 2 * HD), 2 * HD)
    lane = lax.broadcasted_iota(jnp.int32, (HD, rows * both), 1)
    heads = [q_ref[i].astype(F32) for i in range(2)]
    q = [heads[i][r * GROUP : (r + 1) * GROUP] for r in range(rows) for i in range(2)]
    q = jnp.concatenate(q, axis=0).T
    wide = []
    for r in range(rows):
        blocks = []
        for i in range(2):
            first = r * both + i * GROUP
            blocks.append(jnp.where((lane >= first) & (lane < first + GROUP), q, 0.0))
        wide.append(jnp.concatenate(blocks, axis=0).astype(BF16))

    def logits(ref, limit):
        s = functools.reduce(jnp.add, [dot(ref[r, :, keys], wide[r]) for r in range(rows)])
        valid = lax.broadcasted_iota(jnp.int32, s.shape, 0) < limit
        return jnp.where(valid, s * HD**-0.5, -1e30), valid

    sc, okc = logits(cache_ref, limit_ref[0:1, :])
    sf, okf = logits(fresh_ref, limit_ref[1:2, :])
    top = jnp.maximum(jnp.max(sc, axis=0, keepdims=True), jnp.max(sf, axis=0, keepdims=True))
    wc = jnp.where(okc, jnp.exp(sc - top), 0.0)
    wf = jnp.where(okf, jnp.exp(sf - top), 0.0)
    total = jnp.sum(wc, axis=0, keepdims=True) + jnp.sum(wf, axis=0, keepdims=True)
    some = total > 0.0
    total = jnp.where(some, total, 1.0)
    inverse = 1.0 / total
    pc = (wc * inverse).T.astype(BF16)
    pf = (wf * inverse).T.astype(BF16)
    nums = []
    for r in range(rows):
        mine = slice(r * both, (r + 1) * both)
        nums.append(dot(pc[mine], cache_ref[r, :, vals]) + dot(pf[mine], fresh_ref[r, :, vals]))
    for i in range(2):
        for r in range(0, rows, 2):
            num = [x[i * GROUP : (i + 1) * GROUP, i * HD : (i + 1) * HD] for x in nums[r : r + 2]]
            o_ref[i, r * GROUP : (r + 2) * GROUP, :] = jnp.concatenate(num, axis=0).astype(BF16)
    rest = jnp.where(some, top + jnp.log(total), -1e30)
    stats = []
    for _ in range(3):
        piece = rest.astype(BF16).astype(F32)
        stats.append(piece)
        rest = rest - piece
    stats.append(jnp.zeros((STATS - 3, rows * both), F32))
    stats = jnp.concatenate(stats, axis=0)
    stats = jnp.concatenate([stats, jnp.zeros((STATS, HD - rows * both), F32)], axis=1)
    for i in range(2):
        o_ref[i, rows * GROUP :, :] = stats.astype(BF16)


def part_kernel(a_ref, b_ref, c_ref, d_ref, mine_ref, far_ref):
    odd = lax.axis_index("tensor") % 2
    for i, ref in enumerate((a_ref, b_ref, c_ref, d_ref)):
        mine_ref[i] = ref[odd]
        far_ref[i] = ref[1 - odd]


def combine_pair(a_ref, b_ref, heads_ref):
    n = 2 * a_ref.shape[0]
    both = a_ref.shape[1] - STATS
    rows = both // GROUP
    odd = lax.axis_index("tensor") % 2
    line = lax.broadcasted_iota(jnp.int32, (both, HD), 0)
    column = lax.broadcasted_iota(jnp.int32, (both, HD), 1)
    mine = column == (line // GROUP) * 2 * GROUP + odd * GROUP + line % GROUP
    mine = mine.astype(F32).astype(BF16)
    column = lax.broadcasted_iota(jnp.int32, (both, n * STATS), 1)
    parts = [ref.at[i] for ref in (a_ref, b_ref) for i in range(n // 2)]
    stats = [x[both:, :].astype(F32) for x in parts]
    stats = jnp.concatenate(stats, axis=0).astype(BF16)
    pieces = lax.dot_general(mine, stats, (((1,), (1,)), ((), ())), preferred_element_type=F32)
    logs = [
        jnp.sum(jnp.where(column // STATS == t, pieces, 0.0), axis=1, keepdims=True)
        for t in range(n)
    ]
    top = functools.reduce(jnp.maximum, logs)
    scales = [jnp.exp(x - top) for x in logs]
    inverse = 1.0 / functools.reduce(jnp.add, scales)
    heads_ref[...] = functools.reduce(
        jnp.add,
        [x[0:both, :].astype(F32) * (scale * inverse) for x, scale in zip(parts, scales)],
    )
    context = [heads_ref[pl.ds(h, rows, stride=GROUP), :] for h in range(GROUP)]
    return jnp.concatenate(context, axis=1).astype(BF16)


def combine(shared, own, got_ref, heads_ref):
    total, both, _ = got_ref.shape
    both -= STATS
    n = total // shared
    rows = both // own
    me = lax.axis_index("tensor")
    line = lax.broadcasted_iota(jnp.int32, (both, HD), 0)
    column = lax.broadcasted_iota(jnp.int32, (both, HD), 1)
    mine = column == (line // own % 2) * HEADS + me * own + line % own
    mine = mine.astype(F32).astype(BF16)
    line = lax.broadcasted_iota(jnp.int32, (both, n * STATS), 0)
    column = lax.broadcasted_iota(jnp.int32, (both, n * STATS), 1)
    pair = (column % STATS) // (STATS // 2) == line // own // 2
    context = []
    for s in range(shared):
        stats = [got_ref[s * n + t, both:, :].astype(F32) for t in range(n)]
        stats = jnp.concatenate(stats, axis=0).astype(BF16)
        pieces = lax.dot_general(
            mine, stats, (((1,), (1,)), ((), ())), preferred_element_type=F32
        )
        pieces = jnp.where(pair, pieces, 0.0)
        logs = [
            jnp.sum(jnp.where(column // STATS == t, pieces, 0.0), axis=1, keepdims=True)
            for t in range(n)
        ]
        top = functools.reduce(jnp.maximum, logs)
        scales = [jnp.exp(x - top) for x in logs]
        inverse = 1.0 / functools.reduce(jnp.add, scales)
        heads_ref[...] = functools.reduce(
            jnp.add,
            [
                got_ref[s * n + t, 0:both, :].astype(F32) * (scales[t] * inverse)
                for t in range(n)
            ],
        )
        context.append(
            jnp.concatenate(
                [heads_ref[pl.ds(h, rows, stride=own), :] for h in range(own)], axis=1
            )
        )
    return jnp.concatenate(context, axis=0).astype(BF16)


def project_kernel(shared, own, got_ref, w_ref, o_ref, heads_ref):
    context = combine(shared, own, got_ref, heads_ref)
    total, rows, wide = o_ref.shape
    n = total // shared
    offset = 0
    if shared > 1:
        offset = lax.axis_index("section") * wide
    for t in range(n):
        at = t * shared * wide + offset
        if shared > 1:
            at = pl.multiple_of(at, HD)
        terms = dot(context, w_ref[:, pl.ds(at, wide)])
        for s in range(shared):
            o_ref[s * n + t] = terms[s * rows : (s + 1) * rows].astype(BF16)


def pair_terms(apart, context, w_ref, o_ref):
    wide = o_ref.shape[2]
    me = lax.axis_index("tensor")
    for i in range(2):
        at = pl.multiple_of((me ^ (apart + i)) * wide, wide)
        o_ref[i] = dot(context, w_ref[:, pl.ds(at, wide)]).astype(o_ref.dtype)


def begin_kernel(apart, a_ref, b_ref, w_ref, o_ref, context_ref, heads_ref):
    context = combine_pair(a_ref, b_ref, heads_ref)
    context_ref[...] = context
    pair_terms(apart, context, w_ref, o_ref)


def terms_kernel(apart, context_ref, w_ref, o_ref):
    pair_terms(apart, context_ref[...], w_ref, o_ref)


def widen_kernel(x_ref, o_ref):
    o_ref[...] = x_ref[...].astype(F32)


def merge_kernel(x_ref, y_ref, o_ref):
    o_ref[...] = x_ref[...].astype(F32) + y_ref[...].astype(F32)


def finish_kernel(x_ref, y_ref, mine_ref, far_ref):
    out = x_ref[...] + y_ref[...].astype(F32)
    mine_ref[...] = out[0]
    far_ref[...] = out[1].astype(BF16)


def add_kernel(x_ref, y_ref, o_ref):
    o_ref[...] = (x_ref[...] + y_ref[...].astype(F32)).astype(BF16)


def sum_kernel(x_ref, o_ref):
    total, _, wide = x_ref.shape
    shared = o_ref.shape[1] // wide
    n = total // shared
    for s in range(shared):
        x = x_ref[s * n : (s + 1) * n].astype(F32)
        o_ref[:, s * wide : (s + 1) * wide] = jnp.sum(x, axis=0).astype(BF16)


def body(hidden, w_query, w_output, cache, fresh, cache_lengths, new_lengths):
    rows, feat = hidden.shape
    n = lax.axis_size("tensor")
    cores = lax.axis_size("section")
    own = w_query.shape[1] // HD
    wide = w_output.shape[1] // n
    usual = own == GROUP
    o_shared = cores if usual and SPLIT_OUTPUT else 1
    w_query = pltpu.with_memory_space_constraint(w_query, pltpu.VMEM)
    w_output = pltpu.with_memory_space_constraint(w_output, pltpu.VMEM)
    cache = pltpu.with_memory_space_constraint(cache, pltpu.VMEM)
    fresh = pltpu.with_memory_space_constraint(fresh, pltpu.VMEM)

    scratch = [pltpu.VMEM((rows * own, HD), F32)]
    if n == 8:
        mine = call(copy_kernel, (rows, feat), BF16, hidden, flops=LONG)
        near = flip(mine, 1)
        limits = call(
            functools.partial(limit_kernel, cache.shape[1], fresh.shape[1]),
            (2, rows * 2 * GROUP),
            jnp.int32,
            cache_lengths,
            new_lengths,
            specs=[SMEM] * 2,
            flops=LIMIT,
        )
        pair = call(stack_kernel, (2, rows, feat), BF16, flip(mine, 0), near, limits)
        acc = call(first_kernel, (rows, own * HD), F32, flip(pair, 0), w_query, flops=FIRST)
        got = [flip(pair, apart) for apart in ORDER]
        for apart, x in zip(ORDER[:2], got):
            step = functools.partial(next_kernel, apart)
            acc = call(step, (rows, own * HD), F32, x, w_query, acc, flops=10**10 if apart == ORDER[0] else 0)
        step = functools.partial(last_kernel, ORDER[2])
        q = call(step, (rows * own, HD), BF16, got[2], w_query, acc, scratch=scratch)
    else:
        x = call(spread_kernel, (n, rows, feat), BF16, hidden, flops=LONG)
        x = exchange(x, 1)
        q = call(query_kernel, (n, rows * own, HD), BF16, x, w_query, scratch=scratch)
    if n == 8:
        near = flip(q, 1)
        pair = call(order_kernel, (2, rows * own, HD), BF16, flip(q, 0), near)

        def attend(apart):
            return call(
                functools.partial(pair_attend_kernel, apart),
                (2, rows * GROUP + STATS, HD),
                BF16,
                limits,
                flip(pair, apart),
                cache,
                fresh,
                flops=PIECE,
            )

        parts = [flip(attend(apart), apart) for apart in MIDDLE + (0,)]
        shape = (4, rows * GROUP + STATS, HD)
        mine, far = call(part_kernel, [shape] * 2, [BF16, BF16], *parts, flops=ADD)
        parts = flip(mine, 0), flip(far, 1)
    else:
        q = exchange(q, 1)
        if not usual:
            q = q.reshape(KVH, GROUP, rows, HD).transpose(0, 2, 1, 3).reshape(KVH, rows * GROUP, HD)
        part = call(
            attend_kernel,
            (o_shared * KVH, rows * GROUP + STATS, HD),
            BF16,
            cache_lengths,
            new_lengths,
            q,
            cache,
            fresh,
            flops=ATTEND,
            specs=[SMEM] * 2 + [VMEM] * 3,
        )
        if not usual:
            stats = jnp.broadcast_to(part[:1, rows * GROUP :], (n, STATS, HD))
            part = part[:, : rows * GROUP].reshape(KVH, rows, GROUP, HD).transpose(0, 2, 1, 3)
            part = jnp.concatenate([part.reshape(n, rows * own, HD), stats], axis=1)
        part = exchange(part, o_shared)
    scratch = [pltpu.VMEM((rows * own, HD), F32)]
    if n == 8:
        two = (2, rows, wide)
        step = functools.partial(begin_kernel, BACK[0])
        shapes = [two, (rows, own * HD)]
        out, context = call(
            step, shapes, [BF16, BF16], *parts, w_output, scratch=scratch, flops=PIECE
        )
        got = [flip(out, BACK[0])]
        for apart in BACK[1:]:
            step = functools.partial(terms_kernel, apart)
            out = call(step, two, BF16, context, w_output, flops=PIECE)
            got.append(flip(out, apart))
        own_terms = call(
            functools.partial(terms_kernel, 0), two, BF16, context, w_output, flops=PIECE
        )
        out = call(widen_kernel, two, F32, got[0], flops=ADD)
        out = call(merge_kernel, two, F32, out, got[1], flops=ADD)
        out = call(merge_kernel, two, F32, out, got[2], flops=ADD)
        mine, far = call(
            finish_kernel, [(rows, wide)] * 2, [F32, BF16], out, flip(own_terms, 0), flops=ADD
        )
        return call(add_kernel, (rows, wide), BF16, flip(mine, 0), flip(far, 1))
    terms = call(
        functools.partial(project_kernel, o_shared, own),
        (o_shared * n, rows, wide // o_shared),
        BF16,
        part,
        w_output,
        scratch=scratch,
    )
    terms = exchange(terms, o_shared)
    return call(sum_kernel, (rows, wide), BF16, terms)


def solution(mesh):
    return jax.shard_map(
        body,
        mesh=mesh,
        in_specs=(
            P(("groups", "section"), "tensor"),
            P(None, "tensor"),
            P("tensor", None),
            P(("groups", "section"), "tensor", None),
            P(("groups", "section"), "tensor", None),
            P(("groups", "section")),
            P(("groups", "section")),
        ),
        out_specs=P(("groups", "section"), "tensor"),
        check_vma=False,
    )
```

```python
import functools

import jax
import jax.numpy as jnp
from jax import lax
from jax.experimental import pallas as pl
from jax.experimental.pallas import tpu as pltpu
from jax.sharding import PartitionSpec as P

KVH = 8
HD = 128
GROUP = 8
HEADS = KVH * GROUP
STATS = 8
F32 = jnp.float32
BF16 = jnp.bfloat16
VMEM = pl.BlockSpec(memory_space=pltpu.VMEM)
SMEM = pl.BlockSpec(memory_space=pltpu.SMEM)
BOTH = ("section", "tensor")
SPLIT_OUTPUT = False
ORDER = (2, 6, 4)
MIDDLE = (2, 6, 4)
LIMIT = 10**7
BACK = (4, 6, 2)
ADD = 23000000
PIECE = 11500000
LONG = 10**12
FIRST = 0
ATTEND = 0


def exchange(x, shared):
    return lax.all_to_all(x, BOTH if shared > 1 else "tensor", 0, 0, tiled=True)


def dot(a, b):
    return jnp.dot(a, b, preferred_element_type=F32)


def swap(x, apart):
    n = lax.axis_size("tensor")
    return lax.ppermute(x, "tensor", [(i, i ^ apart) for i in range(n)])


def flip(x, apart):
    n = lax.axis_size("tensor")
    return lax.ppermute(x, BOTH, [(i, ((i // n) ^ 1) * n + (i % n ^ apart)) for i in range(2 * n)])


def call(kernel, shape, dtype, *args, specs=None, scratch=(), flops=0):
    if isinstance(shape, list):
        out = [jax.ShapeDtypeStruct(*x) for x in zip(shape, dtype)]
        outs = [VMEM] * len(out)
    else:
        out, outs = jax.ShapeDtypeStruct(shape, dtype), VMEM
    return pl.pallas_call(
        kernel,
        in_specs=specs or [VMEM] * len(args),
        out_specs=outs,
        out_shape=out,
        scratch_shapes=scratch,
        cost_estimate=pl.CostEstimate(flops=flops, bytes_accessed=0, transcendentals=0),
        compiler_params=pltpu.CompilerParams(vmem_limit_bytes=8 << 20),
    )(*args)


def spread_kernel(x_ref, o_ref):
    o_ref[...] = jnp.broadcast_to(x_ref[...][None], o_ref.shape)


def copy_kernel(x_ref, o_ref):
    o_ref[...] = x_ref[...]


def stack_kernel(x_ref, y_ref, _, o_ref):
    o_ref[0] = x_ref[...]
    o_ref[1] = y_ref[...]


def write_queries(acc, o_ref, heads_ref):
    rows = acc.shape[0]
    own = acc.shape[1] // HD
    for h in range(own):
        heads_ref[pl.ds(h, rows, stride=own), :] = acc[:, h * HD : (h + 1) * HD]
    q = heads_ref[...].astype(BF16)
    o_ref[...] = q if len(o_ref.shape) == 2 else jnp.broadcast_to(q[None], o_ref.shape)


def query_kernel(all_ref, w_ref, o_ref, heads_ref):
    n, rows, feat = all_ref.shape
    acc = jnp.zeros((rows, w_ref.shape[1]), F32)
    for t in range(n):
        acc += dot(all_ref[t], w_ref[t * feat : (t + 1) * feat, :])
    write_queries(acc, o_ref, heads_ref)


def pair_product(apart, x_ref, w_ref):
    feat = x_ref.shape[2]
    me = lax.axis_index("tensor")
    acc = jnp.zeros((x_ref.shape[1], w_ref.shape[1]), F32)
    for i in range(2):
        at = pl.multiple_of((me ^ (apart + i)) * feat, feat)
        acc += dot(x_ref[i], w_ref[pl.ds(at, feat), :])
    return acc


def first_kernel(x_ref, w_ref, acc_ref):
    acc_ref[...] = pair_product(0, x_ref, w_ref)


def next_kernel(apart, x_ref, w_ref, old_ref, acc_ref):
    acc_ref[...] = old_ref[...] + pair_product(apart, x_ref, w_ref)


def last_kernel(apart, x_ref, w_ref, old_ref, o_ref, heads_ref):
    write_queries(old_ref[...] + pair_product(apart, x_ref, w_ref), o_ref, heads_ref)


def attend_kernel(clen_ref, nlen_ref, q_ref, cache_ref, fresh_ref, o_ref):
    rows, cc, width = cache_ref.shape
    width = width // 2
    fc = fresh_ref.shape[1]
    shares = q_ref.shape[0] // KVH
    part = GROUP // shares
    place = lax.axis_index("tensor")
    lane = lax.broadcasted_iota(jnp.int32, (HD, 2 * HEADS), 1)

    def logits(ref, r, wide, start, length_ref):
        s = [
            dot(ref[r + i, :, 0:width], wide[i])
            for i in range(2)
        ]
        s = s[0] + s[1]
        second = lax.broadcasted_iota(jnp.int32, s.shape, 1) >= HEADS
        length = jnp.where(second, length_ref[r + 1], length_ref[r])
        valid = start + lax.broadcasted_iota(jnp.int32, s.shape, 0) < length
        return jnp.where(valid, s * HD**-0.5, -1e30), valid

    scores = []
    for r in range(0, rows, 2):
        at = slice(r * part, (r + 2) * part)
        both = [
            q_ref[s * KVH + g, at, :].astype(F32) for g in range(KVH) for s in range(shares)
        ]
        q = [x[i * part : (i + 1) * part] for i in range(2) for x in both]
        q = jnp.concatenate(q, axis=0).T
        wide = []
        for i in range(2):
            blocks = []
            for g in range(KVH):
                first = i * HEADS + g * GROUP
                blocks.append(jnp.where((lane >= first) & (lane < first + GROUP), q, 0.0))
            wide.append(jnp.concatenate(blocks, axis=0).astype(BF16))
        scores.append(
            (
                logits(cache_ref, r, wide, place * cc, clen_ref),
                logits(fresh_ref, r, wide, place * fc, nlen_ref),
            )
        )
    stats, weights = [], []
    for (sc, okc), (sf, okf) in scores:
        top = jnp.maximum(
            jnp.max(sc, axis=0, keepdims=True), jnp.max(sf, axis=0, keepdims=True)
        )
        wc = jnp.where(okc, jnp.exp(sc - top), 0.0)
        wf = jnp.where(okf, jnp.exp(sf - top), 0.0)
        total = jnp.sum(wc, axis=0, keepdims=True) + jnp.sum(wf, axis=0, keepdims=True)
        some = total > 0.0
        total = jnp.where(some, total, 1.0)
        inverse = 1.0 / total
        weights.append(((wc * inverse).T.astype(BF16), (wf * inverse).T.astype(BF16)))
        rest = jnp.where(some, top + jnp.log(total), -1e30)
        for _ in range(3):
            piece = rest.astype(BF16).astype(F32)
            stats.append(piece)
            rest = rest - piece
        stats.append(jnp.zeros_like(rest))
    for two, (pc, pf) in enumerate(weights):
        for pair in range(KVH // 2):
            vals = slice(width + 2 * pair * HD, width + 2 * (pair + 1) * HD)
            nums = []
            for i in range(2):
                at = slice(i * HEADS + 2 * pair * GROUP, i * HEADS + 2 * (pair + 1) * GROUP)
                nums.append(
                    dot(pc[at], cache_ref[2 * two + i, :, vals])
                    + dot(pf[at], fresh_ref[2 * two + i, :, vals])
                )
            at = slice(two * 2 * GROUP, (two + 1) * 2 * GROUP)
            for j in range(2):
                num = [x[j * GROUP : (j + 1) * GROUP, j * HD : (j + 1) * HD] for x in nums]
                num = jnp.concatenate(num, axis=0).astype(BF16)
                for d in range(2 * pair + j, o_ref.shape[0], KVH):
                    o_ref[d, at, :] = num
    stats = jnp.concatenate(stats, axis=0).astype(BF16)
    for d in range(o_ref.shape[0]):
        o_ref[d, rows * GROUP :, :] = stats


def order_kernel(x_ref, y_ref, o_ref):
    odd = lax.axis_index("tensor") % 2
    o_ref[odd] = x_ref[...]
    o_ref[1 - odd] = y_ref[...]


def limit_kernel(cc, fc, clen_ref, nlen_ref, o_ref):
    place = lax.axis_index("tensor")
    request = lax.broadcasted_iota(jnp.int32, (1, o_ref.shape[1]), 1) // (2 * GROUP)
    for i, (ref, count) in enumerate(((clen_ref, cc), (nlen_ref, fc))):
        limit = jnp.full(request.shape, ref[0] - place * count, jnp.int32)
        for r in range(1, ref.shape[0]):
            limit = jnp.where(request == r, ref[r] - place * count, limit)
        o_ref[i : i + 1, :] = limit


def pair_attend_kernel(apart, limit_ref, q_ref, cache_ref, fresh_ref, o_ref):
    rows, _, width = cache_ref.shape
    width = width // 2
    both = 2 * GROUP
    place = lax.axis_index("tensor")
    at = (place ^ apart) // 2 * (2 * HD)
    keys = pl.ds(pl.multiple_of(at, 2 * HD), 2 * HD)
    vals = pl.ds(pl.multiple_of(width + at, 2 * HD), 2 * HD)
    lane = lax.broadcasted_iota(jnp.int32, (HD, rows * both), 1)
    heads = [q_ref[i].astype(F32) for i in range(2)]
    q = [heads[i][r * GROUP : (r + 1) * GROUP] for r in range(rows) for i in range(2)]
    q = jnp.concatenate(q, axis=0).T
    wide = []
    for r in range(rows):
        blocks = []
        for i in range(2):
            first = r * both + i * GROUP
            blocks.append(jnp.where((lane >= first) & (lane < first + GROUP), q, 0.0))
        wide.append(jnp.concatenate(blocks, axis=0).astype(BF16))

    def logits(ref, limit):
        s = functools.reduce(jnp.add, [dot(ref[r, :, keys], wide[r]) for r in range(rows)])
        valid = lax.broadcasted_iota(jnp.int32, s.shape, 0) < limit
        return jnp.where(valid, s * HD**-0.5, -1e30), valid

    sc, okc = logits(cache_ref, limit_ref[0:1, :])
    sf, okf = logits(fresh_ref, limit_ref[1:2, :])
    top = jnp.maximum(jnp.max(sc, axis=0, keepdims=True), jnp.max(sf, axis=0, keepdims=True))
    wc = jnp.where(okc, jnp.exp(sc - top), 0.0)
    wf = jnp.where(okf, jnp.exp(sf - top), 0.0)
    total = jnp.sum(wc, axis=0, keepdims=True) + jnp.sum(wf, axis=0, keepdims=True)
    some = total > 0.0
    total = jnp.where(some, total, 1.0)
    inverse = 1.0 / total
    pc = (wc * inverse).T.astype(BF16)
    pf = (wf * inverse).T.astype(BF16)
    nums = []
    for r in range(rows):
        mine = slice(r * both, (r + 1) * both)
        nums.append(dot(pc[mine], cache_ref[r, :, vals]) + dot(pf[mine], fresh_ref[r, :, vals]))
    for i in range(2):
        for r in range(0, rows, 2):
            num = [x[i * GROUP : (i + 1) * GROUP, i * HD : (i + 1) * HD] for x in nums[r : r + 2]]
            o_ref[i, r * GROUP : (r + 2) * GROUP, :] = jnp.concatenate(num, axis=0).astype(BF16)
    rest = jnp.where(some, top + jnp.log(total), -1e30)
    stats = []
    for _ in range(3):
        piece = rest.astype(BF16).astype(F32)
        stats.append(piece)
        rest = rest - piece
    stats.append(jnp.zeros((STATS - 3, rows * both), F32))
    stats = jnp.concatenate(stats, axis=0)
    stats = jnp.concatenate([stats, jnp.zeros((STATS, HD - rows * both), F32)], axis=1)
    for i in range(2):
        o_ref[i, rows * GROUP :, :] = stats.astype(BF16)


def part_kernel(a_ref, b_ref, c_ref, d_ref, mine_ref, far_ref):
    odd = lax.axis_index("tensor") % 2
    for i, ref in enumerate((a_ref, b_ref, c_ref, d_ref)):
        mine_ref[i] = ref[odd]
        far_ref[i] = ref[1 - odd]


def combine_pair(a_ref, b_ref, heads_ref):
    n = 2 * a_ref.shape[0]
    both = a_ref.shape[1] - STATS
    rows = both // GROUP
    odd = lax.axis_index("tensor") % 2
    line = lax.broadcasted_iota(jnp.int32, (both, HD), 0)
    column = lax.broadcasted_iota(jnp.int32, (both, HD), 1)
    mine = column == (line // GROUP) * 2 * GROUP + odd * GROUP + line % GROUP
    mine = mine.astype(F32).astype(BF16)
    column = lax.broadcasted_iota(jnp.int32, (both, n * STATS), 1)
    parts = [ref.at[i] for ref in (a_ref, b_ref) for i in range(n // 2)]
    stats = [x[both:, :].astype(F32) for x in parts]
    stats = jnp.concatenate(stats, axis=0).astype(BF16)
    pieces = lax.dot_general(mine, stats, (((1,), (1,)), ((), ())), preferred_element_type=F32)
    logs = [
        jnp.sum(jnp.where(column // STATS == t, pieces, 0.0), axis=1, keepdims=True)
        for t in range(n)
    ]
    top = functools.reduce(jnp.maximum, logs)
    scales = [jnp.exp(x - top) for x in logs]
    inverse = 1.0 / functools.reduce(jnp.add, scales)
    heads_ref[...] = functools.reduce(
        jnp.add,
        [x[0:both, :].astype(F32) * (scale * inverse) for x, scale in zip(parts, scales)],
    )
    context = [heads_ref[pl.ds(h, rows, stride=GROUP), :] for h in range(GROUP)]
    return jnp.concatenate(context, axis=1).astype(BF16)


def combine(shared, own, got_ref, heads_ref):
    total, both, _ = got_ref.shape
    both -= STATS
    n = total // shared
    rows = both // own
    me = lax.axis_index("tensor")
    line = lax.broadcasted_iota(jnp.int32, (both, HD), 0)
    column = lax.broadcasted_iota(jnp.int32, (both, HD), 1)
    mine = column == (line // own % 2) * HEADS + me * own + line % own
    mine = mine.astype(F32).astype(BF16)
    line = lax.broadcasted_iota(jnp.int32, (both, n * STATS), 0)
    column = lax.broadcasted_iota(jnp.int32, (both, n * STATS), 1)
    pair = (column % STATS) // (STATS // 2) == line // own // 2
    context = []
    for s in range(shared):
        stats = [got_ref[s * n + t, both:, :].astype(F32) for t in range(n)]
        stats = jnp.concatenate(stats, axis=0).astype(BF16)
        pieces = lax.dot_general(
            mine, stats, (((1,), (1,)), ((), ())), preferred_element_type=F32
        )
        pieces = jnp.where(pair, pieces, 0.0)
        logs = [
            jnp.sum(jnp.where(column // STATS == t, pieces, 0.0), axis=1, keepdims=True)
            for t in range(n)
        ]
        top = functools.reduce(jnp.maximum, logs)
        scales = [jnp.exp(x - top) for x in logs]
        inverse = 1.0 / functools.reduce(jnp.add, scales)
        heads_ref[...] = functools.reduce(
            jnp.add,
            [
                got_ref[s * n + t, 0:both, :].astype(F32) * (scales[t] * inverse)
                for t in range(n)
            ],
        )
        context.append(
            jnp.concatenate(
                [heads_ref[pl.ds(h, rows, stride=own), :] for h in range(own)], axis=1
            )
        )
    return jnp.concatenate(context, axis=0).astype(BF16)


def project_kernel(shared, own, got_ref, w_ref, o_ref, heads_ref):
    context = combine(shared, own, got_ref, heads_ref)
    total, rows, wide = o_ref.shape
    n = total // shared
    offset = 0
    if shared > 1:
        offset = lax.axis_index("section") * wide
    for t in range(n):
        at = t * shared * wide + offset
        if shared > 1:
            at = pl.multiple_of(at, HD)
        terms = dot(context, w_ref[:, pl.ds(at, wide)])
        for s in range(shared):
            o_ref[s * n + t] = terms[s * rows : (s + 1) * rows].astype(BF16)


def pair_terms(apart, context, w_ref, o_ref):
    wide = o_ref.shape[2]
    me = lax.axis_index("tensor")
    for i in range(2):
        at = pl.multiple_of((me ^ (apart + i)) * wide, wide)
        o_ref[i] = dot(context, w_ref[:, pl.ds(at, wide)]).astype(o_ref.dtype)


def begin_kernel(apart, a_ref, b_ref, w_ref, o_ref, context_ref, heads_ref):
    context = combine_pair(a_ref, b_ref, heads_ref)
    context_ref[...] = context
    pair_terms(apart, context, w_ref, o_ref)


def terms_kernel(apart, context_ref, w_ref, o_ref):
    pair_terms(apart, context_ref[...], w_ref, o_ref)


def widen_kernel(x_ref, o_ref):
    o_ref[...] = x_ref[...].astype(F32)


def merge_kernel(x_ref, y_ref, o_ref):
    o_ref[...] = x_ref[...].astype(F32) + y_ref[...].astype(F32)


def finish_kernel(x_ref, y_ref, mine_ref, far_ref):
    out = x_ref[...] + y_ref[...].astype(F32)
    mine_ref[...] = out[0]
    far_ref[...] = out[1].astype(BF16)


def add_kernel(x_ref, y_ref, o_ref):
    o_ref[...] = (x_ref[...] + y_ref[...].astype(F32)).astype(BF16)


def sum_kernel(x_ref, o_ref):
    total, _, wide = x_ref.shape
    shared = o_ref.shape[1] // wide
    n = total // shared
    for s in range(shared):
        x = x_ref[s * n : (s + 1) * n].astype(F32)
        o_ref[:, s * wide : (s + 1) * wide] = jnp.sum(x, axis=0).astype(BF16)


def body(hidden, w_query, w_output, cache, fresh, cache_lengths, new_lengths):
    rows, feat = hidden.shape
    n = lax.axis_size("tensor")
    cores = lax.axis_size("section")
    own = w_query.shape[1] // HD
    wide = w_output.shape[1] // n
    usual = own == GROUP
    o_shared = cores if usual and SPLIT_OUTPUT else 1
    w_query = pltpu.with_memory_space_constraint(w_query, pltpu.VMEM)
    w_output = pltpu.with_memory_space_constraint(w_output, pltpu.VMEM)
    cache = pltpu.with_memory_space_constraint(cache, pltpu.VMEM)
    fresh = pltpu.with_memory_space_constraint(fresh, pltpu.VMEM)

    scratch = [pltpu.VMEM((rows * own, HD), F32)]
    if n == 8:
        mine = call(copy_kernel, (rows, feat), BF16, hidden, flops=LONG)
        near = flip(mine, 1)
        limits = call(
            functools.partial(limit_kernel, cache.shape[1], fresh.shape[1]),
            (2, rows * 2 * GROUP),
            jnp.int32,
            cache_lengths,
            new_lengths,
            specs=[SMEM] * 2,
            flops=LIMIT,
        )
        pair = call(stack_kernel, (2, rows, feat), BF16, flip(mine, 0), near, limits)
        acc = call(first_kernel, (rows, own * HD), F32, flip(pair, 0), w_query, flops=FIRST)
        got = [flip(pair, apart) for apart in ORDER]
        for apart, x in zip(ORDER[:2], got):
            step = functools.partial(next_kernel, apart)
            acc = call(step, (rows, own * HD), F32, x, w_query, acc, flops=10**10 if apart == ORDER[0] else 0)
        step = functools.partial(last_kernel, ORDER[2])
        q = call(step, (rows * own, HD), BF16, got[2], w_query, acc, scratch=scratch)
    else:
        x = call(spread_kernel, (n, rows, feat), BF16, hidden, flops=LONG)
        x = exchange(x, 1)
        q = call(query_kernel, (n, rows * own, HD), BF16, x, w_query, scratch=scratch)
    if n == 8:
        near = flip(q, 1)
        pair = call(order_kernel, (2, rows * own, HD), BF16, flip(q, 0), near)

        def attend(apart):
            return call(
                functools.partial(pair_attend_kernel, apart),
                (2, rows * GROUP + STATS, HD),
                BF16,
                limits,
                flip(pair, apart),
                cache,
                fresh,
                flops=PIECE,
            )

        parts = [flip(attend(apart), apart) for apart in MIDDLE + (0,)]
        shape = (4, rows * GROUP + STATS, HD)
        mine, far = call(part_kernel, [shape] * 2, [BF16, BF16], *parts, flops=ADD)
        parts = flip(mine, 0), flip(far, 1)
    else:
        q = exchange(q, 1)
        if not usual:
            q = q.reshape(KVH, GROUP, rows, HD).transpose(0, 2, 1, 3).reshape(KVH, rows * GROUP, HD)
        part = call(
            attend_kernel,
            (o_shared * KVH, rows * GROUP + STATS, HD),
            BF16,
            cache_lengths,
            new_lengths,
            q,
            cache,
            fresh,
            flops=ATTEND,
            specs=[SMEM] * 2 + [VMEM] * 3,
        )
        if not usual:
            stats = jnp.broadcast_to(part[:1, rows * GROUP :], (n, STATS, HD))
            part = part[:, : rows * GROUP].reshape(KVH, rows, GROUP, HD).transpose(0, 2, 1, 3)
            part = jnp.concatenate([part.reshape(n, rows * own, HD), stats], axis=1)
        part = exchange(part, o_shared)
    scratch = [pltpu.VMEM((rows * own, HD), F32)]
    if n == 8:
        two = (2, rows, wide)
        step = functools.partial(begin_kernel, BACK[0])
        shapes = [two, (rows, own * HD)]
        out, context = call(
            step, shapes, [BF16, BF16], *parts, w_output, scratch=scratch, flops=PIECE
        )
        got = [flip(out, BACK[0])]
        for apart in BACK[1:]:
            step = functools.partial(terms_kernel, apart)
            out = call(step, two, BF16, context, w_output, flops=PIECE)
            got.append(flip(out, apart))
        own_terms = call(
            functools.partial(terms_kernel, 0), two, BF16, context, w_output, flops=PIECE
        )
        out = call(widen_kernel, two, F32, got[0], flops=ADD)
        out = call(merge_kernel, two, F32, out, got[1], flops=ADD)
        out = call(merge_kernel, two, F32, out, got[2], flops=ADD)
        mine, far = call(
            finish_kernel, [(rows, wide)] * 2, [F32, BF16], out, flip(own_terms, 0), flops=ADD
        )
        return call(add_kernel, (rows, wide), BF16, flip(mine, 0), flip(far, 1))
    terms = call(
        functools.partial(project_kernel, o_shared, own),
        (o_shared * n, rows, wide // o_shared),
        BF16,
        part,
        w_output,
        scratch=scratch,
    )
    terms = exchange(terms, o_shared)
    return call(sum_kernel, (rows, wide), BF16, terms)


def solution(mesh):
    return jax.shard_map(
        body,
        mesh=mesh,
        in_specs=(
            P(("groups", "section"), "tensor"),
            P(None, "tensor"),
            P("tensor", None),
            P(("groups", "section"), "tensor", None),
            P(("groups", "section"), "tensor", None),
            P(("groups", "section")),
            P(("groups", "section")),
        ),
        out_specs=P(("groups", "section"), "tensor"),
        check_vma=False,
    )
```
